32 devices in a mesh: dp: 4 (over z), ctx: 8 (over y, x, core).
Axes of the slice: x: 2, y: 2, z: 4, core: 2. Of those that a mesh axis runs over, the one named last changes fastest.
Arguments:
- tokens: bfloat16 [8, 1536, 1152], P('dp', 'ctx'), may hold values from -6 to 6
- cotangent: bfloat16 [8, 1536, 1152], P('dp', 'ctx'), may hold values from -12 to 12
- segment_ids: int32 [8, 1536], P('dp', 'ctx'), may hold values from 0 to 4, as said below
- query_weight: bfloat16 [1152, 1024], P('ctx'), may hold values from -0.1875 to 0.1875
- key_weight: bfloat16 [1152, 256], P('ctx'), may hold values from -0.1875 to 0.1875
- value_weight: bfloat16 [1152, 256], P('ctx'), may hold values from -0.1875 to 0.1875
- out_weight: bfloat16 [1024, 1152], P('ctx'), may hold values from -0.1875 to 0.1875
- gate_weight: bfloat16 [1152, 6912], P('ctx'), may hold values from -0.1875 to 0.1875
- up_weight: bfloat16 [1152, 6912], P('ctx'), may hold values from -0.1875 to 0.1875
- down_weight: bfloat16 [6912, 1152], P('ctx'), may hold values from -0.078125 to 0.078125
- gain_input: bfloat16 [1152], replicated, may hold values from 0.25 to 1.75
- gain_query: bfloat16 [256], replicated, may hold values from 0.25 to 1.75
- gain_key: bfloat16 [256], replicated, may hold values from 0.25 to 1.75
- gain_attended: bfloat16 [1152], replicated, may hold values from 0.25 to 1.75
- gain_feed: bfloat16 [1152], replicated, may hold values from 0.25 to 1.75
- gain_result: bfloat16 [1152], replicated, may hold values from 0.25 to 1.75
Outputs:
- result: bfloat16 [8, 1536, 1152], P('dp', 'ctx')
- tokens_grad: bfloat16 [8, 1536, 1152], P('dp', 'ctx')
- query_weight_grad: float32 [1152, 1024], P('ctx')
- key_weight_grad: float32 [1152, 256], P('ctx')
- value_weight_grad: float32 [1152, 256], P('ctx')
- out_weight_grad: float32 [1024, 1152], P('ctx')
- gate_weight_grad: float32 [1152, 6912], P('ctx')
- up_weight_grad: float32 [1152, 6912], P('ctx')
- down_weight_grad: float32 [6912, 1152], P('ctx')
- gain_input_grad: float32 [1152], replicated
- gain_query_grad: float32 [256], replicated
- gain_key_grad: float32 [256], replicated
- gain_attended_grad: float32 [1152], replicated
- gain_feed_grad: float32 [1152], replicated
- gain_result_grad: float32 [1152], replicated
The draws below stay inside these ranges and needn't reach their ends.
Inputs may be any that keep to these rules, and one draw needn't show every extreme that they name: `segment_ids`: taken in position order, ids never fall along a row; every row holds documents 0 to 4, each of one token or more; document 2 begins within the first 96 positions and ends within the last 96 positions.
All inputs are finite; a program needn't handle non-finite values.
Results may differ from the reference program's by a relative error of at most 0.024.
Values may be sent and summed in bfloat16 or wider, within the bound.
No kernel may reach another device: no remote copies, remote signals or barrier semaphores. Data moves between devices by JAX's collectives and lax.ppermute only.
A program may use at most 320 MiB of HBM per device.

```python
import jax
import jax.numpy as jnp
from jax import lax

D = 1152
HEADS = 4
HEAD_DIM = 256
FF = 6912
TOK_DEV = 192
QW = 1024
SEQ = 1536
ROWS = 8


def draw_cotangent(key, part):
    key = jax.random.fold_in(key, 5)
    ramp = 1.0 + 2.0 * jnp.arange(SEQ, dtype=jnp.float32) / (SEQ - 1)
    values = jnp.clip(jax.random.normal(key, (ROWS, SEQ, D), jnp.float32), -4.0, 4.0)
    return (values * ramp[None, :, None]).astype(jnp.bfloat16)


def draw_segment_ids(key, part):
    key = jax.random.fold_in(key, 11)
    span = TOK_DEV // 2
    pair_count = SEQ // TOK_DEV
    split_keys = jax.random.split(key, 4)
    first_start = jax.random.randint(split_keys[0], (ROWS, 1), 2, span)
    last_start = SEQ - jax.random.randint(split_keys[1], (ROWS, 1), 2, span)
    early_start = 1 + jax.random.randint(split_keys[2], (ROWS, 1), 0, 1048576) % (first_start - 1)
    late_start = last_start + 1 + jax.random.randint(split_keys[3], (ROWS, 1), 0, 1048576) % (SEQ - last_start - 1)
    slots = jnp.arange(SEQ, dtype=jnp.int32)
    block = slots // span
    device = block // 2
    span_index = jnp.where(block % 2 == 1, 2 * pair_count - 1 - device, device)
    places = (span_index * span + slots % span)[None, :]
    return (places >= early_start).astype(jnp.int32) + (places >= first_start).astype(jnp.int32) + (places >= last_start).astype(jnp.int32) + (places >= late_start).astype(jnp.int32)


def shard_levels(rng, extent, cuts, least, largest):
    level = 1.0
    for dim, shards_of in cuts:
        heights = jax.random.uniform(jax.random.fold_in(jax.random.fold_in(rng, 6), dim), (shards_of,), jnp.float32, least / len(cuts), largest / len(cuts))
        level = level * jnp.repeat(jnp.exp(heights), extent[dim] // shards_of).reshape((-1,) + (1,) * (len(extent) - 1 - dim))
    return level


def gaussian(key, dims, scale, bound, cuts=(), kind=jnp.bfloat16):
    gain = shard_levels(key, dims, cuts, -0.22, 0.18) if cuts else 1.0
    drawn = jax.random.normal(key, dims, jnp.float32) * scale * gain
    return jnp.minimum(jnp.maximum(drawn, -bound), bound).astype(kind)


def setup_inputs(seed: int = 0) -> dict:
    keys = jax.random.split(jax.random.key(seed), 17)
    return {
        "tokens": gaussian(keys[0], (ROWS, SEQ, D), 1.0, 6.0, ((0, 4), (1, 8))),
        "cotangent": draw_cotangent(jax.random.fold_in(keys[16], 71), 0),
        "segment_ids": draw_segment_ids(jax.random.fold_in(keys[16], 71), 0),
        "query_weight": gaussian(keys[3], (D, QW), D ** -0.5, 0.1875, ((0, 8),)),
        "key_weight": gaussian(keys[4], (D, HEAD_DIM), D ** -0.5, 0.1875, ((0, 8),)),
        "value_weight": gaussian(keys[5], (D, HEAD_DIM), D ** -0.5, 0.1875, ((0, 8),)),
        "out_weight": gaussian(keys[6], (QW, D), QW ** -0.5, 0.1875, ((0, 8),)),
        "gate_weight": gaussian(keys[7], (D, FF), D ** -0.5, 0.1875, ((0, 8),)),
        "up_weight": gaussian(keys[8], (D, FF), D ** -0.5, 0.1875, ((0, 8),)),
        "down_weight": gaussian(keys[9], (FF, D), FF ** -0.5, 0.078125, ((0, 8),)),
        "gain_input": jnp.clip(1.0 + 0.15 * jax.random.normal(keys[10], (D,), jnp.float32), 0.25, 1.75).astype(jnp.bfloat16),
        "gain_query": jnp.clip(1.0 + 0.15 * jax.random.normal(keys[11], (HEAD_DIM,), jnp.float32), 0.25, 1.75).astype(jnp.bfloat16),
        "gain_key": jnp.clip(1.0 + 0.15 * jax.random.normal(keys[12], (HEAD_DIM,), jnp.float32), 0.25, 1.75).astype(jnp.bfloat16),
        "gain_attended": jnp.clip(1.0 + 0.15 * jax.random.normal(keys[13], (D,), jnp.float32), 0.25, 1.75).astype(jnp.bfloat16),
        "gain_feed": jnp.clip(1.0 + 0.15 * jax.random.normal(keys[14], (D,), jnp.float32), 0.25, 1.75).astype(jnp.bfloat16),
        "gain_result": jnp.clip(1.0 + 0.15 * jax.random.normal(keys[15], (D,), jnp.float32), 0.25, 1.75).astype(jnp.bfloat16),
    }


EPSILON = 1e-06
ROPE_BASE = 1000000.0
SCORE_SCALE = 0.0625
NEGATIVE = -1e+30
GELU_COEFF = 0.044715
ROOT_TWO_PI = 0.7978845608028654

@jax.custom_vjp
def low(v):
    return lax.optimization_barrier(v.astype(jnp.bfloat16)).astype(jnp.float32)

@jax.custom_vjp
def low_back(v):
    return v

def low_keep(v):
    return (low(v), None)

def low_pass(kept, grad):
    return (grad,)

def back_keep(v):
    return (v, None)

def back_low(kept, grad):
    return (low(grad),)
low.defvjp(low_keep, low_pass)
low_back.defvjp(back_keep, back_low)

def matmul(left, right):
    return jnp.dot(left, right, precision=lax.Precision.HIGHEST)

def rms_norm(values, gain_values):
    return values * lax.rsqrt(lax.optimization_barrier(jnp.mean(values * values, axis=-1, keepdims=True)) + EPSILON) * gain_values

def angles_for(positions, width):
    half_width = width // 2
    frequencies = jnp.power(ROPE_BASE, -jnp.arange(half_width, dtype=jnp.float32) / half_width)
    return positions[:, None] * frequencies[None, :]

def rotary(values, angles):
    half_width = values.shape[-1] // 2
    cosine = jnp.cos(angles)
    sine_part = jnp.sin(angles)
    first_half = values[..., :half_width]
    second_half = values[..., half_width:]
    return jnp.concatenate([first_half * cosine - second_half * sine_part, second_half * cosine + first_half * sine_part], axis=-1)

def geglu(gate_proj, up_proj):
    cubic = gate_proj + GELU_COEFF * gate_proj * gate_proj * gate_proj
    return 0.5 * gate_proj * (1.0 + jnp.tanh(ROOT_TWO_PI * cubic)) * up_proj

def stored_to_place(length, span):
    pair_count = length // (2 * span)
    slots = jnp.arange(length, dtype=jnp.int32)
    block = slots // span
    device = block // 2
    span_index = jnp.where(block % 2 == 1, 2 * pair_count - 1 - device, device)
    return (span_index * span + slots % span).astype(jnp.int32)

def place_to_stored(length, span):
    pair_count = length // (2 * span)
    places = jnp.arange(length, dtype=jnp.int32)
    span_index = places // span
    upper = span_index >= pair_count
    device = jnp.where(upper, 2 * pair_count - 1 - span_index, span_index)
    return ((2 * device + upper.astype(jnp.int32)) * span + places % span).astype(jnp.int32)

def layer_row(weights, row_tokens, row_segments):
    query_weight, key_weight, value_weight, out_weight, gate_weight, up_weight, down_weight, gain_input, gain_query, gain_key, gain_attended, gain_feed, gain_result = weights
    length = row_tokens.shape[0]
    places = jnp.arange(length, dtype=jnp.int32)
    starts = lax.optimization_barrier(jnp.sum((row_segments[None, :] < row_segments[:, None]).astype(jnp.int32), axis=1))
    angles = angles_for((places - starts).astype(jnp.float32), HEAD_DIM)
    normed = low(rms_norm(row_tokens, gain_input))
    query_raw = low_back(matmul(normed, query_weight)).reshape(length, HEADS, HEAD_DIM)
    key_raw = low_back(matmul(normed, key_weight))
    values_all = low(low_back(matmul(normed, value_weight)))
    queries = low(rotary(rms_norm(query_raw, gain_query), angles[:, None, :]))
    keys_all = low(rotary(rms_norm(key_raw, gain_key), angles))
    block_rows = min(512, length)
    block_count = length // block_rows

    def attend(pieces):
        query_block, segment_block, place_block = pieces
        scores = low_back(jnp.einsum('qhd,kd->hqk', query_block, keys_all, precision=lax.Precision.HIGHEST) * SCORE_SCALE)
        allowed = (segment_block[:, None] == row_segments[None, :]) & (place_block[:, None] >= places[None, :])
        scores = jnp.where(allowed[None, :, :], scores, NEGATIVE)
        maxima = lax.optimization_barrier(jnp.max(scores, axis=-1, keepdims=True))
        exponents = jnp.exp(scores - maxima)
        probabilities = low(exponents / lax.optimization_barrier(jnp.sum(exponents, axis=-1, keepdims=True)))
        return jnp.einsum('hqk,kd->qhd', probabilities, values_all, precision=lax.Precision.HIGHEST)
    attended = lax.map(jax.checkpoint(attend), (queries.reshape(block_count, block_rows, HEADS, HEAD_DIM), row_segments.reshape(block_count, block_rows), places.reshape(block_count, block_rows)))
    attended = low(low_back(attended.reshape(length, HEADS * HEAD_DIM)))
    projected = low_back(matmul(attended, out_weight))
    hidden = row_tokens + rms_norm(projected, gain_attended)
    inner_rows = low(rms_norm(hidden, gain_feed))
    gate_proj = low_back(matmul(inner_rows, gate_weight))
    upward = low_back(matmul(inner_rows, up_weight))
    active = low(geglu(gate_proj, upward))
    lowered = low_back(matmul(active, down_weight))
    return hidden + rms_norm(lowered, gain_result)

def reference(tokens, cotangent, segment_ids, query_weight, key_weight, value_weight, out_weight, gate_weight, up_weight, down_weight, gain_input, gain_query, gain_key, gain_attended, gain_feed, gain_result):
    span = TOK_DEV // 2
    order = place_to_stored(SEQ, span)
    back = stored_to_place(SEQ, span)
    weights = tuple((weight.astype(jnp.float32) for weight in (query_weight, key_weight, value_weight, out_weight, gate_weight, up_weight, down_weight, gain_input, gain_query, gain_key, gain_attended, gain_feed, gain_result)))
    tokens_wide = jnp.take(tokens.astype(jnp.float32), order, axis=1)
    segments_placed = jnp.take(segment_ids, order, axis=1)
    upstream = jnp.take(cotangent.astype(jnp.float32), order, axis=1)

    def forward(weights, tokens_wide):
        row_step = jax.checkpoint(layer_row)
        return lax.map(lambda pieces: row_step(weights, pieces[0], pieces[1]), (tokens_wide, segments_placed))
    outputs, pullback = jax.vjp(forward, weights, tokens_wide)
    weight_grads, tokens_grad = pullback(upstream)
    outputs = jnp.take(outputs, back, axis=1)
    tokens_grad = jnp.take(tokens_grad, back, axis=1)
    return (outputs.astype(jnp.bfloat16), tokens_grad.astype(jnp.bfloat16), weight_grads[0], weight_grads[1], weight_grads[2], weight_grads[3], weight_grads[4], weight_grads[5], weight_grads[6], weight_grads[7], weight_grads[8], weight_grads[9], weight_grads[10], weight_grads[11], weight_grads[12])
```

```python
import jax
import jax.numpy as jnp
from jax import lax
from jax.experimental import pallas as pl
from jax.experimental.pallas import tpu as pltpu
from jax.sharding import PartitionSpec as P

EPSILON = 1e-06
ROPE_BASE = 1000000.0
SCORE_SCALE = 0.0625
NEGATIVE = -1e30
GELU_COEFF = 0.044715
ROOT_TWO_PI = 0.7978845608028654
BF16 = jnp.bfloat16
WIDE = jnp.float32


def rms_norm(values, gain_values):
    return (
        values
        * lax.rsqrt(jnp.mean(values * values, axis=-1, keepdims=True) + EPSILON)
        * gain_values
    )


def angles_for(positions, width):
    half_width = width // 2
    frequencies = jnp.power(ROPE_BASE, -jnp.arange(half_width, dtype=jnp.float32) / half_width)
    return positions[:, None] * frequencies[None, :]


def gelu_parts(gate):
    square = gate * gate
    bent = jnp.tanh(ROOT_TWO_PI * (gate + GELU_COEFF * gate * square))
    rise = 0.5 * (1.0 + bent)
    slope = rise + 0.5 * gate * (1.0 - bent * bent) * ROOT_TWO_PI * (
        1.0 + 3.0 * GELU_COEFF * square
    )
    return gate * rise, slope


def dot(left, right):
    return jnp.dot(left, right, preferred_element_type=WIDE)


def dot_t(left, right):
    return lax.dot_general(left, right, (((1,), (1,)), ((), ())), preferred_element_type=WIDE)


def t_dot(left, right):
    return lax.dot_general(left, right, (((0,), (0,)), ((), ())), preferred_element_type=WIDE)


def after(x, *earlier):
    return lax.optimization_barrier((x,) + earlier)[0] if earlier else x


def xor_permute(x, axis_size, code):
    return lax.ppermute(x, "ctx", [(i, i ^ code) for i in range(axis_size)])


def xor_layout(n):
    far_y, far_x = n // 2, n // 4
    near = [1 << b for b in range((n // 4).bit_length() - 1)]
    codes = [0, far_x, far_y, far_x ^ far_y]
    for bit in near:
        codes = codes + [c ^ bit for c in codes]
    return far_x, far_y, near, codes


class Gather:
    def __init__(self, x, n):
        self.n = n
        self.far_x, self.far_y, self.near_bits, _ = xor_layout(n)
        self.x = x
        self.a = xor_permute(x, n, self.far_x)
        self.b = xor_permute(x, n, self.far_y)

    def mid(self, *earlier):
        half = self.x.shape[0] // 2
        a = after(self.a, *earlier)
        self.d1 = xor_permute(a[:half], self.n, self.far_y)
        self.d2 = xor_permute(self.b[half:], self.n, self.far_x)
        return self

    def near(self, *earlier):
        d1 = after(self.d1, *earlier)
        self.blocks = [stack_blocks(self.x, self.a, self.b, d1, self.d2)]
        for bit in self.near_bits:
            self.blocks = self.blocks + [xor_permute(b, self.n, bit) for b in self.blocks]
        return self

    def flat(self):
        return [b.reshape((4 * self.x.shape[0],) + self.x.shape[1:]) for b in self.blocks]


class Scatter:
    def __init__(self, blocks, n):
        self.n = n
        self.far_x, self.far_y, self.near_bits, _ = xor_layout(n)
        self.blocks = list(blocks)
        self.bits = list(reversed(self.near_bits))
        self.send_near()

    def send_near(self):
        if self.bits:
            count = len(self.blocks) // 2
            self.arrived = [xor_permute(b, self.n, self.bits[0]) for b in self.blocks[count:]]

    def mid(self, *earlier):
        while self.bits:
            count = len(self.blocks) // 2
            self.arrived[0] = after(self.arrived[0], *earlier)
            self.blocks = [
                (mine.astype(WIDE) + theirs.astype(WIDE)).astype(BF16)
                for mine, theirs in zip(self.blocks[:count], self.arrived)
            ]
            self.bits = self.bits[1:]
            self.send_near()
        self.sums = self.blocks[0]
        half = self.sums.shape[1] // 2
        self.d_x = xor_permute(self.sums[3, :half], self.n, self.far_x)
        self.d_y = xor_permute(self.sums[3, half:], self.n, self.far_y)
        return self

    def far(self, *earlier):
        half = self.sums.shape[1] // 2
        d_x = after(self.d_x, *earlier).astype(WIDE)
        d_y = self.d_y.astype(WIDE)
        x, y = self.sums[1].astype(WIDE), self.sums[2].astype(WIDE)
        to_x = jnp.concatenate([x[:half], x[half:] + d_y], axis=0).astype(BF16)
        to_y = jnp.concatenate([y[:half] + d_x, y[half:]], axis=0).astype(BF16)
        self.from_x = xor_permute(to_x, self.n, self.far_x)
        self.from_y = xor_permute(to_y, self.n, self.far_y)
        self.sent = (to_x, to_y)
        return self

    def finish(self, *earlier):
        return self.sums, after(self.from_x, *earlier), self.from_y


class Line:
    def __init__(self, part, n):
        self.n = n
        self.total = part
        mid = n // 2
        self.steps = []
        for s in range(mid - 1):
            self.steps.append(("in", [(s, s + 1), (n - 1 - s, n - 2 - s)], None))
        self.steps.append(("in", [(mid - 1, mid), (mid, mid - 1)], None))
        for s in range(mid - 2, -1, -1):
            self.steps.append(("out", [(s + 1, s), (n - 2 - s, n - 1 - s)], (s, n - 1 - s)))
        self.at = 0
        self.send()

    def send(self):
        if self.at < len(self.steps):
            self.moved = lax.ppermute(self.total, "dp", self.steps[self.at][1])

    def step(self, *earlier):
        kind, _, ends = self.steps[self.at]
        moved = after(self.moved, *earlier)
        if kind == "in":
            total = self.total.astype(WIDE) + moved.astype(WIDE)
            self.total = total.astype(self.total.dtype)
        else:
            me = lax.axis_index("dp")
            self.total = jnp.where((me == ends[0]) | (me == ends[1]), moved, self.total)
        self.at += 1
        self.send()
        return self.total

    def finish(self):
        while self.at < len(self.steps):
            self.step()
        return self.total


NT = (((1,), (1,)), ((), ()))
TN = (((0,), (0,)), ((), ()))
VMEM_LIMIT = 48 * 1024 * 1024


def vmem_call(kernel, out_shape, **kwargs):
    return pl.pallas_call(
        kernel,
        out_shape=out_shape,
        compiler_params=pltpu.CompilerParams(vmem_limit_bytes=VMEM_LIMIT),
        cost_estimate=pl.CostEstimate(flops=0, bytes_accessed=0, transcendentals=0),
        **kwargs,
    )


def whole_spec():
    return pl.BlockSpec(memory_space=pltpu.VMEM)


def smem_spec():
    return pl.BlockSpec(memory_space=pltpu.SMEM)


def full_spec(shape):
    return pl.BlockSpec(shape, lambda i: (0,) * len(shape))


def row_spec(shape, row):
    return pl.BlockSpec((1,) + shape, lambda i: (row,) + (0,) * len(shape))


def unit(values, gain_values):
    r = lax.rsqrt(jnp.mean(values * values, axis=-1, keepdims=True) + EPSILON)
    return values * r * gain_values, r


def unit_back(values, r, gain_values, e):
    ge = gain_values * e
    d_values = r * ge - values * (r * r * r * jnp.mean(ge * values, axis=-1, keepdims=True))
    return d_values, jnp.sum(e * values * r, axis=0, keepdims=True)


def stack_blocks(x, a, b, d1, d2):
    half = d1.shape[0]

    def kernel(x_ref, a_ref, b_ref, d1_ref, d2_ref, out_ref):
        out_ref[0] = x_ref[...]
        out_ref[1] = a_ref[...]
        out_ref[2] = b_ref[...]
        out_ref[3, :half] = d1_ref[...]
        out_ref[3, half:] = d2_ref[...]

    return vmem_call(
        kernel,
        jax.ShapeDtypeStruct((4,) + x.shape, x.dtype),
        in_specs=[whole_spec()] * 5,
        out_specs=whole_spec(),
    )(x, a, b, d1, d2)


def spread_pieces(flag, first, second, n):
    rows, columns = first.shape
    share = columns // n

    def kernel(flag_ref, first_ref, second_ref, out_ref):
        def fill(source):
            for k in range(n):
                out_ref[k] = source[:, k * share : (k + 1) * share]

        @pl.when(flag_ref[0] == 1)
        def _():
            fill(first_ref)

        @pl.when(flag_ref[0] != 1)
        def _():
            fill(second_ref)

    return vmem_call(
        kernel,
        jax.ShapeDtypeStruct((n, rows, share), first.dtype),
        in_specs=[smem_spec(), whole_spec(), whole_spec()],
        out_specs=whole_spec(),
    )(flag, first, second)


def in_order(flag, first, second):
    def kernel(flag_ref, first_ref, second_ref, a_ref, b_ref):
        @pl.when(flag_ref[0] == 1)
        def _():
            a_ref[...] = first_ref[...]
            b_ref[...] = second_ref[...]

        @pl.when(flag_ref[0] != 1)
        def _():
            a_ref[...] = second_ref[...]
            b_ref[...] = first_ref[...]

    parts, rows, columns = first.shape
    step = pl.BlockSpec((1, rows, columns), lambda i: (i, 0, 0))
    return vmem_call(
        kernel,
        (jax.ShapeDtypeStruct(first.shape, first.dtype),) * 2,
        grid=(parts,),
        in_specs=[smem_spec(), step, step],
        out_specs=(step, step),
    )(flag, first, second)


def assemble(flag, totals, moveds, rows, columns):
    count = len(totals)
    share = totals[0].shape[2]

    def kernel(flag_ref, *refs):
        out_ref = refs[-1]

        def fill(parts):
            at = 0
            for part in parts:
                for k in range(part.shape[0]):
                    out_ref[:, at * share : (at + 1) * share] = part[k].astype(WIDE)
                    at += 1

        @pl.when(flag_ref[0] == 1)
        def _():
            fill(refs[count : 2 * count])

        @pl.when(flag_ref[0] != 1)
        def _():
            fill(refs[:count])

    return vmem_call(
        kernel,
        jax.ShapeDtypeStruct((rows, columns), WIDE),
        in_specs=[smem_spec()] + [whole_spec()] * (2 * count),
        out_specs=whole_spec(),
    )(flag, *totals, *moveds)


def allowed_mask(start_ref, place_ref, key_place_ref):
    key_place = key_place_ref[...]
    return (start_ref[...] <= key_place) & (place_ref[...] >= key_place)


def lay_out(kv_refs, k_held, v_held, size):
    at = 0
    for ref in kv_refs:
        for slot in range(ref.shape[0]):
            tokens = ref.shape[2]
            k_held[at : at + tokens] = ref[slot, 0, :, :size]
            v_held[at : at + tokens] = ref[slot, 0, :, size:]
            at += tokens


def attend_forward(
    row, queries, kv_blocks, start, place, key_place, out_weight, tokens, gain_out, gain_feed, heads
):
    count = start.shape[0]
    width = tokens.shape[2]
    slots = kv_blocks[0].shape[0]
    size = kv_blocks[0].shape[3] // 2
    keys = slots * len(kv_blocks) * count
    lanes_all = heads * size

    def kernel(*refs):
        q_ref, start_ref, place_ref, key_place_ref, w_ref, x_ref, g1_ref, g2_ref = refs[:8]
        kv_refs = refs[8 : 8 + len(kv_blocks)]
        out_ref, log_ref, projected_ref, hidden_ref, inner_ref, k_held, v_held = refs[
            8 + len(kv_blocks) :
        ]
        lay_out(kv_refs, k_held, v_held, size)
        allowed = allowed_mask(start_ref, place_ref, key_place_ref)
        for h in range(heads):
            q = q_ref[:, h * size : (h + 1) * size]
            scores = lax.dot_general(q, k_held[...], NT, preferred_element_type=WIDE) * SCORE_SCALE
            scores = jnp.where(allowed, scores, NEGATIVE)
            peak = jnp.max(scores, axis=-1, keepdims=True)
            raised = jnp.exp(scores - peak)
            weight = jnp.sum(raised, axis=-1, keepdims=True)
            probabilities = (raised * (1.0 / weight)).astype(BF16)
            out = jnp.dot(probabilities, v_held[...], preferred_element_type=WIDE)
            out_ref[:, h * size : (h + 1) * size] = out.astype(BF16)
            log_ref[:, h : h + 1] = peak + jnp.log(weight)
        projected = jnp.dot(out_ref[...], w_ref[...], preferred_element_type=WIDE)
        projected_ref[...] = projected
        hidden = x_ref[0].astype(WIDE) + unit(projected, g1_ref[...].astype(WIDE))[0]
        hidden_ref[...] = hidden
        inner_ref[...] = unit(hidden, g2_ref[...].astype(WIDE))[0].astype(BF16)

    return vmem_call(
        kernel,
        (
            jax.ShapeDtypeStruct((count, lanes_all), BF16),
            jax.ShapeDtypeStruct((count, heads), WIDE),
            jax.ShapeDtypeStruct((count, width), WIDE),
            jax.ShapeDtypeStruct((count, width), WIDE),
            jax.ShapeDtypeStruct((count, width), BF16),
        ),
        grid=(1,),
        in_specs=[
            pl.BlockSpec((count, lanes_all), lambda i: (row, 0)),
            full_spec((count, 1)),
            full_spec((count, 1)),
            full_spec((1, keys)),
            full_spec((lanes_all, width)),
            row_spec((count, width), row),
            full_spec((1, width)),
            full_spec((1, width)),
        ]
        + [
            pl.BlockSpec((slots, 1, count, 2 * size), lambda i: (0, row, 0, 0)) for _ in kv_blocks
        ],
        out_specs=(
            full_spec((count, lanes_all)),
            full_spec((count, heads)),
            full_spec((count, width)),
            full_spec((count, width)),
            full_spec((count, width)),
        ),
        scratch_shapes=[pltpu.VMEM((keys, size), BF16), pltpu.VMEM((keys, size), BF16)],
    )(queries, start, place, key_place, out_weight, tokens, gain_out, gain_feed, *kv_blocks)


def close_row(row, parts, hidden, cotangent, gain):
    count, width = hidden.shape

    def kernel(a_ref, b_ref, c_ref, hidden_ref, e_ref, gain_ref, result_ref, d_ref, dg_ref):
        v = a_ref[0].astype(WIDE) + b_ref[...].astype(WIDE) + c_ref[...].astype(WIDE)
        g = gain_ref[...].astype(WIDE)
        z, r = unit(v, g)
        result_ref[...] = (hidden_ref[...] + z).astype(BF16)
        d_values, dg_ref[...] = unit_back(v, r, g, e_ref[0].astype(WIDE))
        d_ref[...] = d_values.astype(BF16)

    return vmem_call(
        kernel,
        (
            jax.ShapeDtypeStruct((count, width), BF16),
            jax.ShapeDtypeStruct((count, width), BF16),
            jax.ShapeDtypeStruct((1, width), WIDE),
        ),
        grid=(1,),
        in_specs=[
            row_spec((count, width), 0),
            full_spec((count, width)),
            full_spec((count, width)),
            full_spec((count, width)),
            row_spec((count, width), row),
            full_spec((1, width)),
        ],
        out_specs=(full_spec((count, width)), full_spec((count, width)), full_spec((1, width))),
    )(*parts, hidden, cotangent, gain)


def attend_backward(
    row,
    parts,
    kept,
    cotangent,
    out_weight,
    gain_out,
    gain_feed,
    queries,
    kv_blocks,
    place,
    key_place,
    raw,
    cosine,
    sine,
    gain,
    heads,
):
    count, width = kept["hidden"].shape
    slots = kv_blocks[0].shape[0]
    size = kv_blocks[0].shape[3] // 2
    half = size // 2
    keys = slots * len(kv_blocks) * count
    lanes_all = heads * size
    block_count = len(kv_blocks)

    def kernel(*refs):
        (
            a_ref,
            b_ref,
            c_ref,
            hidden_ref,
            projected_ref,
            e_ref,
            w_ref,
            g1_ref,
            g2_ref,
            q_ref,
            start_ref,
            place_ref,
            key_place_ref,
            log_ref,
            raw_ref,
            cos_ref,
            sin_ref,
            gain_ref,
        ) = refs[:18]
        kv_refs = refs[18 : 18 + block_count]
        outs = refs[18 + block_count :]
        d_hidden_ref, d_projected_ref, dg1_ref, dg2_ref, dq_ref, dgain_ref = outs[:6]
        dkv_refs = outs[6 : 6 + block_count]
        k_held, v_held, dk_acc, dv_acc, d_held = outs[6 + block_count :]
        g1 = g1_ref[...].astype(WIDE)
        g2 = g2_ref[...].astype(WIDE)
        e = a_ref[0].astype(WIDE) + b_ref[...].astype(WIDE) + c_ref[...].astype(WIDE)
        hidden = hidden_ref[...]
        d_values, dg2_ref[...] = unit_back(hidden, unit(hidden, g2)[1], g2, e)
        d_hidden = e_ref[0].astype(WIDE) + d_values
        d_hidden_ref[...] = d_hidden
        projected = projected_ref[...]
        d_values, dg1_ref[...] = unit_back(projected, unit(projected, g1)[1], g1, d_hidden)
        d_projected_ref[...] = d_values.astype(BF16)
        d_held[...] = lax.dot_general(
            d_projected_ref[...], w_ref[...], NT, preferred_element_type=WIDE
        ).astype(BF16)
        lay_out(kv_refs, k_held, v_held, size)
        allowed = allowed_mask(start_ref, place_ref, key_place_ref)
        gain_values = gain_ref[...].astype(WIDE)
        cos = cos_ref[...]
        sin = sin_ref[...]
        d_gain = jnp.zeros((1, size), WIDE)
        for h in range(heads):
            lanes = slice(h * size, (h + 1) * size)
            q = q_ref[:, lanes]
            d = d_held[:, lanes]
            k = k_held[...]
            scores = lax.dot_general(q, k, NT, preferred_element_type=WIDE) * SCORE_SCALE
            p = jnp.where(allowed, jnp.exp(scores - log_ref[:, h : h + 1]), 0.0)
            d_p = lax.dot_general(d, v_held[...], NT, preferred_element_type=WIDE)
            inner = jnp.sum(p * d_p, axis=-1, keepdims=True)
            d_s = (p * (d_p - inner)).astype(BF16)
            d_v = lax.dot_general(p.astype(BF16), d, TN, preferred_element_type=WIDE)
            d_k = lax.dot_general(d_s, q, TN, preferred_element_type=WIDE)
            if h == 0:
                dk_acc[...] = d_k
                dv_acc[...] = d_v
            else:
                dk_acc[...] += d_k
                dv_acc[...] += d_v
            d_q = jnp.dot(d_s, k, preferred_element_type=WIDE) * SCORE_SCALE
            d_a, d_b = d_q[:, :half], d_q[:, half:]
            turned = jnp.concatenate([d_a * cos + d_b * sin, d_b * cos - d_a * sin], axis=-1)
            u = raw_ref[:, lanes]
            d_u, d_part = unit_back(u, unit(u, gain_values)[1], gain_values, turned)
            dq_ref[:, lanes] = d_u.astype(BF16)
            d_gain += d_part
        dgain_ref[...] = d_gain
        at = 0
        for ref in dkv_refs:
            for slot in range(slots):
                ref[slot, :, :size] = (dk_acc[at : at + count] * SCORE_SCALE).astype(BF16)
                ref[slot, :, size:] = dv_acc[at : at + count].astype(BF16)
                at += count

    wide_rows = jax.ShapeDtypeStruct((count, width), WIDE)
    mine = pl.BlockSpec((count, lanes_all), lambda i: (row, 0))
    turn = pl.BlockSpec((count, half), lambda i: (row, 0))
    outs = vmem_call(
        kernel,
        (
            wide_rows,
            jax.ShapeDtypeStruct((count, width), BF16),
            jax.ShapeDtypeStruct((1, width), WIDE),
            jax.ShapeDtypeStruct((1, width), WIDE),
            jax.ShapeDtypeStruct((count, lanes_all), BF16),
            jax.ShapeDtypeStruct((1, size), WIDE),
        )
        + (jax.ShapeDtypeStruct((slots, count, 2 * size), BF16),) * block_count,
        grid=(1,),
        in_specs=[
            row_spec((count, width), 0),
            full_spec((count, width)),
            full_spec((count, width)),
            full_spec((count, width)),
            full_spec((count, width)),
            row_spec((count, width), row),
            full_spec((lanes_all, width)),
            full_spec((1, width)),
            full_spec((1, width)),
            mine,
            full_spec((count, 1)),
            full_spec((count, 1)),
            full_spec((1, keys)),
            full_spec((count, heads)),
            mine,
            turn,
            turn,
            full_spec((1, size)),
        ]
        + [
            pl.BlockSpec((slots, 1, count, 2 * size), lambda i: (0, row, 0, 0)) for _ in kv_blocks
        ],
        out_specs=(
            full_spec((count, width)),
            full_spec((count, width)),
            full_spec((1, width)),
            full_spec((1, width)),
            full_spec((count, lanes_all)),
            full_spec((1, size)),
        )
        + (full_spec((slots, count, 2 * size)),) * block_count,
        scratch_shapes=[
            pltpu.VMEM((keys, size), BF16),
            pltpu.VMEM((keys, size), BF16),
            pltpu.VMEM((keys, size), WIDE),
            pltpu.VMEM((keys, size), WIDE),
            pltpu.VMEM((count, lanes_all), BF16),
        ],
    )(
        *parts,
        kept["hidden"],
        kept["projected"],
        cotangent,
        out_weight,
        gain_out,
        gain_feed,
        queries,
        kept["start"],
        place,
        key_place,
        kept["log"],
        raw,
        cosine,
        sine,
        gain,
        *kv_blocks,
    )
    names = ("d_hidden", "d_projected", "grad_out_gain", "grad_feed_gain", "d_query_raw", "d_gain")
    kept.update(zip(names, outs[:6]))
    kept["d_kv"] = outs[6:]


def project_kv(order, normed, blocks, cosine, sine, gain, rows):
    tokens, width = normed.shape
    per_block, part, both = blocks[0].shape
    n = per_block * len(blocks)
    size = both // 2
    half = size // 2

    def kernel(order_ref, x_ref, cos_ref, sin_ref, gain_ref, *refs):
        block_refs = refs[: len(blocks)]
        kv_ref, raw_ref, held = refs[len(blocks) :]
        for d in range(n):
            slot = order_ref[d]
            for k, block in enumerate(block_refs):

                @pl.when((slot >= k * per_block) & (slot < (k + 1) * per_block))
                def _(d=d, k=k, block=block, slot=slot):
                    held[d * part : (d + 1) * part] = block[slot - k * per_block]

        both_raw = jnp.dot(x_ref[...], held[...], preferred_element_type=WIDE)
        u = both_raw[:, :size]
        raw_ref[...] = u
        k = unit(u, gain_ref[...].astype(WIDE))[0]
        cos, sin = cos_ref[...], sin_ref[...]
        a, b = k[:, :half], k[:, half:]
        kv = jnp.concatenate([a * cos - b * sin, b * cos + a * sin, both_raw[:, size:]], axis=-1)
        kv_ref[...] = kv.astype(BF16).reshape(rows, tokens // rows, both)

    return vmem_call(
        kernel,
        (
            jax.ShapeDtypeStruct((rows, tokens // rows, both), BF16),
            jax.ShapeDtypeStruct((tokens, size), WIDE),
            jax.ShapeDtypeStruct((width, both), BF16),
        ),
        in_specs=[smem_spec()] + [whole_spec()] * (4 + len(blocks)),
        out_specs=(whole_spec(), whole_spec(), whole_spec()),
    )(order, normed, cosine, sine, gain, *blocks)


def project_q(normed, weight, cosine, sine, gain, heads):
    tokens, width = normed.shape
    size = weight.shape[1] // heads
    half = size // 2

    def kernel(x_ref, w_ref, cos_ref, sin_ref, gain_ref, q_ref, raw_ref):
        cos, sin = cos_ref[...], sin_ref[...]
        raw_ref[...] = jnp.dot(x_ref[...], w_ref[...], preferred_element_type=WIDE)
        for h in range(heads):
            lanes = slice(h * size, (h + 1) * size)
            q = unit(raw_ref[:, lanes], gain_ref[...].astype(WIDE))[0]
            a, b = q[:, :half], q[:, half:]
            turned = jnp.concatenate([a * cos - b * sin, b * cos + a * sin], axis=-1)
            q_ref[:, lanes] = turned.astype(BF16)

    return vmem_call(
        kernel,
        (
            jax.ShapeDtypeStruct((tokens, heads * size), BF16),
            jax.ShapeDtypeStruct((tokens, heads * size), WIDE),
        ),
        in_specs=[whole_spec()] * 5,
        out_specs=(whole_spec(), whole_spec()),
    )(normed, weight, cosine, sine, gain)


def feed_steps(blocks):
    tokens, width = blocks[0].shape
    step = 256 if tokens % 256 == 0 else tokens
    per_block = tokens // step

    def spec(k):
        return pl.BlockSpec(
            (step, width), lambda i: (jnp.clip(i - k * per_block, 0, per_block - 1), 0)
        )

    return step, per_block, spec


def in_block(k, per_block):
    i = pl.program_id(0)
    return (i >= k * per_block) & (i < (k + 1) * per_block)


def feed_forward(blocks, gate_w, up_w, down_w):
    width = blocks[0].shape[1]
    share = gate_w.shape[1]
    step, per_block, spec = feed_steps(blocks)
    count = len(blocks)
    total = count * per_block * step

    def kernel(gate_ref, up_ref, down_ref, *refs):
        x_ref, slope_ref, value_ref, a_ref = refs[count : count + 4]
        low_refs = refs[count + 4 :]
        for k in range(count):

            @pl.when(in_block(k, per_block))
            def _(k=k):
                x_ref[...] = refs[k][...]

        x = x_ref[...]
        g = jnp.dot(x, gate_ref[...], preferred_element_type=WIDE)
        u = jnp.dot(x, up_ref[...], preferred_element_type=WIDE)
        value, slope = gelu_parts(g)
        active = (value * u).astype(BF16)
        slope_ref[...] = (slope * u).astype(BF16)
        value_ref[...] = value.astype(BF16)
        a_ref[...] = active
        low = jnp.dot(active, down_ref[...], preferred_element_type=WIDE).astype(BF16)
        for k in range(count):

            @pl.when(in_block(k, per_block))
            def _(k=k):
                low_refs[k][...] = low

    each = lambda columns: pl.BlockSpec((step, columns), lambda i: (i, 0))
    whole = lambda shape: pl.BlockSpec(shape, lambda i: (0, 0))
    hidden = jax.ShapeDtypeStruct((total, share), BF16)
    return vmem_call(
        kernel,
        (jax.ShapeDtypeStruct((total, width), BF16), hidden, hidden, hidden)
        + tuple(jax.ShapeDtypeStruct(b.shape, BF16) for b in blocks),
        grid=(total // step,),
        in_specs=[whole((width, share)), whole((width, share)), whole((share, width))]
        + [spec(k) for k in range(count)],
        out_specs=(each(width), each(share), each(share), each(share))
        + tuple(spec(k) for k in range(count)),
    )(gate_w, up_w, down_w, *blocks)


def feed_backward(blocks, slope, value, gate_w, up_w, down_w):
    width = blocks[0].shape[1]
    share = gate_w.shape[1]
    step, per_block, spec = feed_steps(blocks)
    count = len(blocks)
    total = count * per_block * step

    def kernel(gate_ref, up_ref, down_ref, slope_ref, value_ref, *refs):
        d_ref, dg_ref, du_ref = refs[count : count + 3]
        dx_refs = refs[count + 3 :]
        for k in range(count):

            @pl.when(in_block(k, per_block))
            def _(k=k):
                d_ref[...] = refs[k][...]

        d_active = lax.dot_general(d_ref[...], down_ref[...], NT, preferred_element_type=WIDE)
        d_gate = (d_active * slope_ref[...].astype(WIDE)).astype(BF16)
        d_up = (d_active * value_ref[...].astype(WIDE)).astype(BF16)
        dg_ref[...] = d_gate
        du_ref[...] = d_up
        d_x = lax.dot_general(d_gate, gate_ref[...], NT, preferred_element_type=WIDE)
        d_x += lax.dot_general(d_up, up_ref[...], NT, preferred_element_type=WIDE)
        d_x = d_x.astype(BF16)
        for k in range(count):

            @pl.when(in_block(k, per_block))
            def _(k=k):
                dx_refs[k][...] = d_x

    each = lambda columns: pl.BlockSpec((step, columns), lambda i: (i, 0))
    whole = lambda shape: pl.BlockSpec(shape, lambda i: (0, 0))
    hidden = jax.ShapeDtypeStruct((total, share), BF16)
    return vmem_call(
        kernel,
        (jax.ShapeDtypeStruct((total, width), BF16), hidden, hidden)
        + tuple(jax.ShapeDtypeStruct(b.shape, BF16) for b in blocks),
        grid=(total // step,),
        in_specs=[
            whole((width, share)),
            whole((width, share)),
            whole((share, width)),
            each(share),
            each(share),
        ]
        + [spec(k) for k in range(count)],
        out_specs=(each(width), each(share), each(share))
        + tuple(spec(k) for k in range(count)),
    )(gate_w, up_w, down_w, slope, value, *blocks)


def weight_grad(lefts, rights, parts):
    tokens, rows = lefts[0].shape
    columns = rights[0].shape[1]
    step = tokens // 2 if tokens % 32 == 0 else tokens
    per_pair = tokens // step
    count = len(lefts)
    last = count * per_pair - 1

    def kernel(*refs):
        out_ref, acc = refs[2 * count :]
        i = pl.program_id(0)
        for k in range(count):

            @pl.when(in_block(k, per_pair))
            def _(k=k):
                term = lax.dot_general(
                    refs[k][...], refs[count + k][...], TN, preferred_element_type=WIDE
                )
                if k == 0:

                    @pl.when(i == 0)
                    def _():
                        acc[...] = term

                    @pl.when(i != 0)
                    def _():
                        acc[...] += term

                else:
                    acc[...] += term

        @pl.when(i == last)
        def _():
            size = rows // parts
            for p in range(parts):
                out_ref[p] = acc[p * size : (p + 1) * size].astype(BF16)

    def spec(k, width):
        return pl.BlockSpec(
            (step, width), lambda i: (jnp.clip(i - k * per_pair, 0, per_pair - 1), 0)
        )

    return vmem_call(
        kernel,
        jax.ShapeDtypeStruct((parts, rows // parts, columns), BF16),
        grid=(last + 1,),
        in_specs=[spec(k, rows) for k in range(count)] + [spec(k, columns) for k in range(count)],
        out_specs=full_spec((parts, rows // parts, columns)),
        scratch_shapes=[pltpu.VMEM((rows, columns), WIDE)],
    )(*lefts, *rights)


def per_device(
    tokens,
    cotangent,
    segment_ids,
    query_weight,
    key_weight,
    value_weight,
    out_weight,
    gate_weight,
    up_weight,
    down_weight,
    gain_input,
    gain_query,
    gain_key,
    gain_attended,
    gain_feed,
    gain_result,
):
    n = lax.axis_size("ctx")
    n_dp = lax.axis_size("dp")
    me = lax.axis_index("ctx")
    my_dp = lax.axis_index("dp")
    row_count, count_local, width = tokens.shape
    total = row_count * count_local
    head_width = gain_query.shape[0]
    half_width = head_width // 2
    head_count = query_weight.shape[1] // head_width
    qw = head_count * head_width
    share = gate_weight.shape[1] // n
    span = count_local // 2
    codes = xor_layout(n)[3]
    gain_row = {
        "query": gain_query.reshape(1, -1),
        "key": gain_key.reshape(1, -1),
        "out": gain_attended.reshape(1, -1),
        "feed": gain_feed.reshape(1, -1),
        "result": gain_result.reshape(1, -1),
    }
    scale_input = gain_input.astype(WIDE)
    scale_key = gain_key.astype(WIDE)

    kv_weights = Gather(jnp.concatenate([key_weight, value_weight], axis=1), n)
    query_full = lax.all_gather(query_weight, "ctx", axis=0, tiled=True)
    even_flag = ((my_dp % 2) == 0).astype(jnp.int32).reshape(1)
    pieces = spread_pieces(even_flag, gate_weight, up_weight, n)
    spread = lax.all_to_all(pieces, "ctx", 0, 0)

    below = jnp.stack(
        [jnp.sum((segment_ids < s).astype(jnp.int32), axis=1) for s in range(5)], axis=1
    )
    code = 1
    while code < n:
        below = below + xor_permute(below, n, code)
        code *= 2
    starts = sum(jnp.where(segment_ids == s, below[:, s : s + 1], 0) for s in range(5))

    offsets = jnp.arange(span, dtype=jnp.int32)

    def places_of(device):
        return jnp.concatenate([device * span + offsets, (2 * n - 1 - device) * span + offsets])

    local_places = places_of(me)
    key_places = jnp.concatenate([places_of(me ^ code) for code in codes]).reshape(1, -1)
    place_column = local_places.reshape(-1, 1)
    angles = angles_for(local_places.astype(WIDE), head_width)
    cosine = jnp.concatenate([jnp.cos(angles)] * row_count, axis=0)
    sine = jnp.concatenate([jnp.sin(angles)] * row_count, axis=0)

    row_tokens = tokens.reshape(total, width).astype(WIDE)
    normed_wide, normed_pull = jax.vjp(rms_norm, row_tokens, scale_input)
    normed = normed_wide.astype(BF16)
    order_codes = me ^ jnp.arange(n, dtype=jnp.int32)
    order = sum(jnp.where(order_codes == c, k, 0) for k, c in enumerate(codes)).astype(jnp.int32)
    kv_weights.mid(pieces, normed).near()
    kv_local, key_raw, kv_full = project_kv(
        order, normed, kv_weights.blocks, cosine, sine, gain_row["key"], row_count
    )
    kv_gather = Gather(kv_local, n)
    out_full = lax.all_gather(after(out_weight, kv_local), "ctx", axis=0, tiled=True)
    queries, query_raw = project_q(
        after(normed, kv_local), query_full, cosine, sine, gain_row["query"], head_count
    )
    kv_gather.mid(queries)
    swapped = lax.ppermute(
        after(spread, kv_gather.a, kv_gather.b), "dp", [(i, i ^ 1) for i in range(n_dp)]
    )
    kv_gather.near()
    kv_blocks = kv_gather.blocks

    def before_feed(row, *earlier):
        r = {"start": starts[row].reshape(-1, 1)}
        names = ("attended", "log", "projected", "hidden", "inner_local")
        outs = attend_forward(
            row,
            after(queries, *earlier),
            kv_blocks,
            r["start"],
            place_column,
            key_places,
            out_full,
            tokens,
            gain_row["out"],
            gain_row["feed"],
            head_count,
        )
        r.update(zip(names, outs))
        return r

    def feed_piece(r, blocks, *earlier):
        blocks = [after(blocks[0], *earlier)] + blocks[1:]
        outs = feed_forward(blocks, gate_mine, up_mine, down_weight)
        r["inner"], r["slope"], r["value"], r["active"] = outs[:4]
        return [x.reshape(4, count_local, width) for x in outs[4:]]

    def back_piece(r, blocks, *earlier):
        blocks = [after(blocks[0], *earlier)] + blocks[1:]
        outs = feed_backward(blocks, r["slope"], r["value"], gate_mine, up_mine, down_weight)
        r["d_lowered"], r["d_gate"], r["d_up"] = outs[:3]
        return [x.reshape(4, count_local, width) for x in outs[3:]]

    def result_piece(row, r, parts):
        r["result"], d_lowered, r["grad_result_gain"] = close_row(
            row, parts, r["hidden"], cotangent, gain_row["result"]
        )
        return d_lowered

    def attend_back(row, r, parts):
        attend_backward(
            row,
            parts,
            r,
            cotangent,
            out_full,
            gain_row["out"],
            gain_row["feed"],
            queries,
            kv_blocks,
            place_column,
            key_places,
            query_raw,
            cosine,
            sine,
            gain_row["query"],
            head_count,
        )

    r0 = before_feed(0)
    g0 = Gather(r0["inner_local"], n)
    r1 = before_feed(1, r0["inner_local"])
    g0.mid(r1["inner_local"])
    g1 = Gather(after(r1["inner_local"], g0.a, g0.b), n)
    gate_mine, up_mine = in_order(even_flag, spread, swapped)
    gate_mine = gate_mine.reshape(width, share)
    up_mine = up_mine.reshape(width, share)
    g0.near(gate_mine)
    g1.mid(g0.blocks[0])
    low_0 = feed_piece(r0, g0.flat(), g1.a)
    s0 = Scatter(low_0, n)
    g1.near(low_0[0])
    s0.mid(g1.blocks[0])
    low_1 = feed_piece(r1, g1.flat(), s0.sums)
    s1 = Scatter(low_1, n)
    s0.far(low_1[0])
    s1.mid(*s0.sent)
    d_low_0 = result_piece(0, r0, s0.finish(s1.sums))
    h0 = Gather(d_low_0, n)
    s1.far(d_low_0)
    h0.mid(*s1.sent)
    d_low_1 = result_piece(1, r1, s1.finish(h0.a))
    h1 = Gather(d_low_1, n)
    h0.near(d_low_1)
    h1.mid(h0.blocks[0])
    d_in_0 = back_piece(r0, h0.flat(), h1.a)
    s0 = Scatter(d_in_0, n)
    h1.near(d_in_0[0])
    s0.mid(h1.blocks[0])
    d_in_1 = back_piece(r1, h1.flat(), s0.sums)
    s1 = Scatter(d_in_1, n)
    s0.far(d_in_1[0])
    rows = (r0, r1)

    def over_rows(left, right, parts, *earlier):
        return weight_grad(
            [after(r0[left], *earlier), r1[left]], [r0[right], r1[right]], parts
        )

    def exchange(grad):
        return lax.all_to_all(grad, "ctx", 0, 0)

    down_pieces = over_rows("active", "d_lowered", 2, *s0.sent)
    d0, d1 = [Line(x, n_dp) for x in (down_pieces[0], down_pieces[1])]
    s1.mid(d0.total, d1.total)
    grad_gate = over_rows("inner", "d_gate", n, s1.sums)
    s1.far(grad_gate)
    gate_pieces = exchange(after(grad_gate, *s1.sent))
    attend_back(0, r0, s0.finish(*s1.sent))
    d0.step(r0["d_kv"][0])
    grad_up = over_rows("inner", "d_up", n, d0.total)
    d1.step(grad_up)
    attend_back(1, r1, s1.finish(d1.total))
    kv_scatter = Scatter(
        [jnp.stack([a, b], axis=1) for a, b in zip(r0["d_kv"], r1["d_kv"])], n
    )
    d0.step(kv_scatter.blocks[-1])
    up_pieces = exchange(after(grad_up, gate_pieces, d0.total))
    half = n // 2
    g_lines = [Line(after(gate_pieces[:half], d0.total), n_dp)]
    grad_out = (
        t_dot(after(r0["attended"], g_lines[0].total), r0["d_projected"])
        + t_dot(r1["attended"], r1["d_projected"])
    ).astype(BF16)
    part_out = lax.psum_scatter(grad_out, "ctx", scatter_dimension=0, tiled=True)
    kv_scatter.mid(grad_out)
    d1.step(kv_scatter.sums)
    g_lines.append(Line(after(gate_pieces[half:], d1.total), n_dp))
    d_query_raw = jnp.concatenate([r["d_query_raw"] for r in rows], axis=0)
    grad_q = t_dot(after(normed, g_lines[1].total), d_query_raw).astype(BF16)
    kv_scatter.far(grad_q)
    d_normed_q = dot_t(after(d_query_raw, *kv_scatter.sent), query_full)
    g_lines[0].step(d_normed_q)
    d_kv_parts = kv_scatter.finish(g_lines[0].total)
    d_kv = (
        d_kv_parts[0][0].astype(WIDE) + d_kv_parts[1].astype(WIDE) + d_kv_parts[2].astype(WIDE)
    ).reshape(total, 2 * head_width)

    def key_shape(raw_rows, gain_values):
        unturned = rms_norm(raw_rows, gain_values)
        a, b = unturned[:, :half_width], unturned[:, half_width:]
        return jnp.concatenate([a * cosine - b * sine, b * cosine + a * sine], axis=1)

    key_pull = jax.vjp(key_shape, key_raw, scale_key)[1]
    d_key_raw, grad_key_gain = key_pull(d_kv[:, :head_width])
    d_kv_raw = jnp.concatenate([d_key_raw, d_kv[:, head_width:]], axis=1).astype(BF16)
    grad_kv = t_dot(normed, d_kv_raw).astype(BF16)
    grad_qkv = jnp.concatenate([grad_q, grad_kv], axis=1)
    part_qkv = lax.psum_scatter(grad_qkv, "ctx", scatter_dimension=0, tiled=True)
    g_lines[1].step(grad_qkv)
    quarter = max(n // 4, 1)
    cuts = [(0, half), (half, half + quarter), (half + quarter, n)]
    u_lines = [Line(after(up_pieces[:half], g_lines[1].total), n_dp)]
    d_normed = d_normed_q + dot_t(after(d_kv_raw, g_lines[1].total), kv_full)
    d_tokens_part, grad_input_gain = normed_pull(d_normed)
    d_hidden = jnp.concatenate([r["d_hidden"] for r in rows], axis=0)
    tokens_grad = (d_hidden + d_tokens_part).astype(BF16)
    gains = jnp.concatenate(
        [
            grad_input_gain,
            sum(r["d_gain"] for r in rows).reshape(-1),
            grad_key_gain,
            sum(r["grad_out_gain"] for r in rows).reshape(-1),
            sum(r["grad_feed_gain"] for r in rows).reshape(-1),
            sum(r["grad_result_gain"] for r in rows).reshape(-1),
        ]
    ).reshape(-1, 128)
    code = 1
    while code < n:
        gains = gains + xor_permute(gains, n, code)
        code *= 2
    clock = [tokens_grad]

    def step(line):
        if line.at < len(line.steps) - 1:
            line.step(*clock)
            clock[:] = [line.total]

    def begin(part):
        line = Line(after(part, *clock), n_dp)
        clock[:] = [line.total]
        return line

    step(g_lines[0])
    step(u_lines[0])
    u_lines.append(begin(up_pieces[cuts[1][0] : cuts[1][1]]))
    step(g_lines[1])
    u_lines.append(begin(up_pieces[cuts[2][0] : cuts[2][1]]))
    step(u_lines[0])
    step(u_lines[1])
    out_line = begin(part_out)
    step(u_lines[1])
    step(u_lines[2])
    qkv_line = begin(part_qkv)
    gain_line = begin(gains)
    step(u_lines[2])
    tail = [out_line, qkv_line, gain_line]
    for _ in range(n_dp):
        for line in [d0, d1] + g_lines + u_lines + tail:
            step(line)

    def side_by_side(lines):
        ends = lines[0].steps[-1][2]
        mine = (my_dp == ends[0]) | (my_dp == ends[1]) if ends else my_dp < 0
        return assemble(
            mine.astype(jnp.int32).reshape(1),
            [line.total for line in lines],
            [line.moved for line in lines],
            width // n,
            n * share,
        )

    summed_down = jnp.concatenate([d0.finish(), d1.finish()], axis=0).astype(WIDE)
    summed_gate = side_by_side(g_lines)
    summed_up = side_by_side(u_lines)
    summed_out = out_line.finish().astype(WIDE)
    summed_qkv = qkv_line.finish().astype(WIDE)
    gains = gain_line.finish().reshape(-1)
    sizes = [width, head_width, head_width, width, width, width]
    gain_grads = []
    start = 0
    for size in sizes:
        gain_grads.append(gains[start : start + size])
        start += size
    return (
        jnp.stack([r["result"] for r in rows]),
        tokens_grad.reshape(row_count, count_local, width),
        summed_qkv[:, :qw],
        summed_qkv[:, qw : qw + head_width],
        summed_qkv[:, qw + head_width :],
        summed_out,
        summed_gate,
        summed_up,
        summed_down,
        *gain_grads,
    )


def solution(mesh):
    return jax.shard_map(
        per_device,
        mesh=mesh,
        in_specs=(
            P("dp", "ctx", None),
            P("dp", "ctx", None),
            P("dp", "ctx"),
            P("ctx", None),
            P("ctx", None),
            P("ctx", None),
            P("ctx", None),
            P("ctx", None),
            P("ctx", None),
            P("ctx", None),
            P(),
            P(),
            P(),
            P(),
            P(),
            P(),
        ),
        out_specs=(
            P("dp", "ctx", None),
            P("dp", "ctx", None),
            P("ctx", None),
            P("ctx", None),
            P("ctx", None),
            P("ctx", None),
            P("ctx", None),
            P("ctx", None),
            P("ctx", None),
            P(),
            P(),
            P(),
            P(),
            P(),
            P(),
        ),
        check_vma=False,
    )
```

```python
import jax
import jax.numpy as jnp
from jax import lax
from jax.experimental import pallas as pl
from jax.experimental.pallas import tpu as pltpu
from jax.sharding import PartitionSpec as P

EPSILON = 1e-06
ROPE_BASE = 1000000.0
SCORE_SCALE = 0.0625
NEGATIVE = -1e30
GELU_COEFF = 0.044715
ROOT_TWO_PI = 0.7978845608028654
BF16 = jnp.bfloat16
WIDE = jnp.float32


def rms_norm(values, gain_values):
    return (
        values
        * lax.rsqrt(jnp.mean(values * values, axis=-1, keepdims=True) + EPSILON)
        * gain_values
    )


def angles_for(positions, width):
    half_width = width // 2
    frequencies = jnp.power(ROPE_BASE, -jnp.arange(half_width, dtype=jnp.float32) / half_width)
    return positions[:, None] * frequencies[None, :]


def gelu_parts(gate):
    square = gate * gate
    bent = jnp.tanh(ROOT_TWO_PI * (gate + GELU_COEFF * gate * square))
    rise = 0.5 * (1.0 + bent)
    slope = rise + 0.5 * gate * (1.0 - bent * bent) * ROOT_TWO_PI * (
        1.0 + 3.0 * GELU_COEFF * square
    )
    return gate * rise, slope


def dot(left, right):
    return jnp.dot(left, right, preferred_element_type=WIDE)


def dot_t(left, right):
    return lax.dot_general(left, right, (((1,), (1,)), ((), ())), preferred_element_type=WIDE)


def t_dot(left, right):
    return lax.dot_general(left, right, (((0,), (0,)), ((), ())), preferred_element_type=WIDE)


def after(x, *earlier):
    return lax.optimization_barrier((x,) + earlier)[0] if earlier else x


def xor_permute(x, axis_size, code):
    return lax.ppermute(x, "ctx", [(i, i ^ code) for i in range(axis_size)])


def xor_layout(n):
    far_y, far_x = n // 2, n // 4
    near = [1 << b for b in range((n // 4).bit_length() - 1)]
    codes = [0, far_x, far_y, far_x ^ far_y]
    for bit in near:
        codes = codes + [c ^ bit for c in codes]
    return far_x, far_y, near, codes


class Gather:
    def __init__(self, x, n):
        self.n = n
        self.far_x, self.far_y, self.near_bits, _ = xor_layout(n)
        self.x = x
        self.a = xor_permute(x, n, self.far_x)
        self.b = xor_permute(x, n, self.far_y)

    def mid(self, *earlier):
        half = self.x.shape[0] // 2
        a = after(self.a, *earlier)
        self.d1 = xor_permute(a[:half], self.n, self.far_y)
        self.d2 = xor_permute(self.b[half:], self.n, self.far_x)
        return self

    def near(self, *earlier):
        d1 = after(self.d1, *earlier)
        self.blocks = [stack_blocks(self.x, self.a, self.b, d1, self.d2)]
        for bit in self.near_bits:
            self.blocks = self.blocks + [xor_permute(b, self.n, bit) for b in self.blocks]
        return self

    def flat(self):
        return [b.reshape((4 * self.x.shape[0],) + self.x.shape[1:]) for b in self.blocks]


class Scatter:
    def __init__(self, blocks, n):
        self.n = n
        self.far_x, self.far_y, self.near_bits, _ = xor_layout(n)
        self.blocks = list(blocks)
        self.bits = list(reversed(self.near_bits))
        self.send_near()

    def send_near(self):
        if self.bits:
            count = len(self.blocks) // 2
            self.arrived = [xor_permute(b, self.n, self.bits[0]) for b in self.blocks[count:]]

    def mid(self, *earlier):
        while self.bits:
            count = len(self.blocks) // 2
            self.arrived[0] = after(self.arrived[0], *earlier)
            self.blocks = [
                (mine.astype(WIDE) + theirs.astype(WIDE)).astype(BF16)
                for mine, theirs in zip(self.blocks[:count], self.arrived)
            ]
            self.bits = self.bits[1:]
            self.send_near()
        self.sums = self.blocks[0]
        half = self.sums.shape[1] // 2
        self.d_x = xor_permute(self.sums[3, :half], self.n, self.far_x)
        self.d_y = xor_permute(self.sums[3, half:], self.n, self.far_y)
        return self

    def far(self, *earlier):
        half = self.sums.shape[1] // 2
        d_x = after(self.d_x, *earlier).astype(WIDE)
        d_y = self.d_y.astype(WIDE)
        x, y = self.sums[1].astype(WIDE), self.sums[2].astype(WIDE)
        to_x = jnp.concatenate([x[:half], x[half:] + d_y], axis=0).astype(BF16)
        to_y = jnp.concatenate([y[:half] + d_x, y[half:]], axis=0).astype(BF16)
        self.from_x = xor_permute(to_x, self.n, self.far_x)
        self.from_y = xor_permute(to_y, self.n, self.far_y)
        self.sent = (to_x, to_y)
        return self

    def finish(self, *earlier):
        return self.sums, after(self.from_x, *earlier), self.from_y


class Line:
    def __init__(self, part, n):
        self.n = n
        self.total = part
        mid = n // 2
        self.steps = []
        for s in range(mid - 1):
            self.steps.append(("in", [(s, s + 1), (n - 1 - s, n - 2 - s)], None))
        self.steps.append(("in", [(mid - 1, mid), (mid, mid - 1)], None))
        for s in range(mid - 2, -1, -1):
            self.steps.append(("out", [(s + 1, s), (n - 2 - s, n - 1 - s)], (s, n - 1 - s)))
        self.at = 0
        self.send()

    def send(self):
        if self.at < len(self.steps):
            self.moved = lax.ppermute(self.total, "dp", self.steps[self.at][1])

    def step(self, *earlier):
        kind, _, ends = self.steps[self.at]
        moved = after(self.moved, *earlier)
        if kind == "in":
            total = self.total.astype(WIDE) + moved.astype(WIDE)
            self.total = total.astype(self.total.dtype)
        else:
            me = lax.axis_index("dp")
            self.total = jnp.where((me == ends[0]) | (me == ends[1]), moved, self.total)
        self.at += 1
        self.send()
        return self.total

    def finish(self):
        while self.at < len(self.steps):
            self.step()
        return self.total


NT = (((1,), (1,)), ((), ()))
TN = (((0,), (0,)), ((), ()))
MIB = 1024 * 1024


def vmem_call(kernel, out_shape, limit=32, **kwargs):
    return pl.pallas_call(
        kernel,
        out_shape=out_shape,
        compiler_params=pltpu.CompilerParams(vmem_limit_bytes=limit * MIB),
        cost_estimate=pl.CostEstimate(flops=0, bytes_accessed=0, transcendentals=0),
        **kwargs,
    )


def whole_spec():
    return pl.BlockSpec(memory_space=pltpu.VMEM)


def smem_spec():
    return pl.BlockSpec(memory_space=pltpu.SMEM)


def full_spec(shape):
    return pl.BlockSpec(shape, lambda i: (0,) * len(shape))


def row_spec(shape, row):
    return pl.BlockSpec((1,) + shape, lambda i: (row,) + (0,) * len(shape))


def unit(values, gain_values):
    r = lax.rsqrt(jnp.mean(values * values, axis=-1, keepdims=True) + EPSILON)
    return values * r * gain_values, r


def unit_back(values, r, gain_values, e):
    ge = gain_values * e
    d_values = r * ge - values * (r * r * r * jnp.mean(ge * values, axis=-1, keepdims=True))
    return d_values, jnp.sum(e * values * r, axis=0, keepdims=True)


def stack_blocks(x, a, b, d1, d2):
    half = d1.shape[0]

    def kernel(x_ref, a_ref, b_ref, d1_ref, d2_ref, out_ref):
        out_ref[0] = x_ref[...]
        out_ref[1] = a_ref[...]
        out_ref[2] = b_ref[...]
        out_ref[3, :half] = d1_ref[...]
        out_ref[3, half:] = d2_ref[...]

    return vmem_call(
        kernel,
        jax.ShapeDtypeStruct((4,) + x.shape, x.dtype),
        in_specs=[whole_spec()] * 5,
        out_specs=whole_spec(),
    )(x, a, b, d1, d2)


def spread_pieces(flag, first, second, n):
    rows, columns = first.shape
    share = columns // n

    def kernel(flag_ref, first_ref, second_ref, out_ref):
        def fill(source):
            for k in range(n):
                out_ref[k] = source[:, k * share : (k + 1) * share]

        @pl.when(flag_ref[0] == 1)
        def _():
            fill(first_ref)

        @pl.when(flag_ref[0] != 1)
        def _():
            fill(second_ref)

    return vmem_call(
        kernel,
        jax.ShapeDtypeStruct((n, rows, share), first.dtype),
        in_specs=[smem_spec(), whole_spec(), whole_spec()],
        out_specs=whole_spec(),
    )(flag, first, second)


def in_order(flag, first, second):
    def kernel(flag_ref, first_ref, second_ref, a_ref, b_ref):
        @pl.when(flag_ref[0] == 1)
        def _():
            a_ref[...] = first_ref[...]
            b_ref[...] = second_ref[...]

        @pl.when(flag_ref[0] != 1)
        def _():
            a_ref[...] = second_ref[...]
            b_ref[...] = first_ref[...]

    parts, rows, columns = first.shape
    step = pl.BlockSpec((1, rows, columns), lambda i: (i, 0, 0))
    return vmem_call(
        kernel,
        (jax.ShapeDtypeStruct(first.shape, first.dtype),) * 2,
        grid=(parts,),
        in_specs=[smem_spec(), step, step],
        out_specs=(step, step),
    )(flag, first, second)


def assemble(flag, totals, moveds, rows, columns):
    count = len(totals)
    share = totals[0].shape[2]
    moveds = moveds or []

    def kernel(flag_ref, *refs):
        out_ref = refs[-1]

        def fill(parts):
            at = 0
            for part in parts:
                for k in range(part.shape[0]):
                    out_ref[:, at * share : (at + 1) * share] = part[k].astype(WIDE)
                    at += 1

        if not moveds:
            fill(refs[:count])
            return

        @pl.when(flag_ref[0] == 1)
        def _():
            fill(refs[count : 2 * count])

        @pl.when(flag_ref[0] != 1)
        def _():
            fill(refs[:count])

    return vmem_call(
        kernel,
        jax.ShapeDtypeStruct((rows, columns), WIDE),
        in_specs=[smem_spec()] + [whole_spec()] * (count + len(moveds)),
        out_specs=whole_spec(),
    )(flag, *totals, *moveds)


def allowed_mask(start_ref, place_ref, key_place_ref):
    key_place = key_place_ref[...]
    return (start_ref[...] <= key_place) & (place_ref[...] >= key_place)


def lay_out(kv_refs, k_held, v_held, size):
    at = 0
    for ref in kv_refs:
        for slot in range(ref.shape[0]):
            tokens = ref.shape[2]
            k_held[at : at + tokens] = ref[slot, 0, :, :size]
            v_held[at : at + tokens] = ref[slot, 0, :, size:]
            at += tokens


def attend_forward(
    row, queries, kv_blocks, start, place, key_place, out_weight, tokens, gain_out, gain_feed, heads
):
    count = start.shape[0]
    width = tokens.shape[2]
    slots = kv_blocks[0].shape[0]
    size = kv_blocks[0].shape[3] // 2
    keys = slots * len(kv_blocks) * count
    lanes_all = heads * size

    def kernel(*refs):
        q_ref, start_ref, place_ref, key_place_ref, w_ref, x_ref, g1_ref, g2_ref = refs[:8]
        kv_refs = refs[8 : 8 + len(kv_blocks)]
        out_ref, log_ref, projected_ref, hidden_ref, inner_ref, k_held, v_held = refs[
            8 + len(kv_blocks) :
        ]
        lay_out(kv_refs, k_held, v_held, size)
        allowed = allowed_mask(start_ref, place_ref, key_place_ref)
        for h in range(heads):
            q = q_ref[:, h * size : (h + 1) * size]
            scores = lax.dot_general(q, k_held[...], NT, preferred_element_type=WIDE) * SCORE_SCALE
            scores = jnp.where(allowed, scores, NEGATIVE)
            peak = jnp.max(scores, axis=-1, keepdims=True)
            raised = jnp.exp(scores - peak)
            weight = jnp.sum(raised, axis=-1, keepdims=True)
            probabilities = (raised * (1.0 / weight)).astype(BF16)
            out = jnp.dot(probabilities, v_held[...], preferred_element_type=WIDE)
            out_ref[:, h * size : (h + 1) * size] = out.astype(BF16)
            log_ref[:, h : h + 1] = peak + jnp.log(weight)
        projected = jnp.dot(out_ref[...], w_ref[...], preferred_element_type=WIDE)
        projected_ref[...] = projected
        hidden = x_ref[0].astype(WIDE) + unit(projected, g1_ref[...].astype(WIDE))[0]
        hidden_ref[...] = hidden
        inner_ref[...] = unit(hidden, g2_ref[...].astype(WIDE))[0].astype(BF16)

    return vmem_call(
        kernel,
        (
            jax.ShapeDtypeStruct((count, lanes_all), BF16),
            jax.ShapeDtypeStruct((count, heads), WIDE),
            jax.ShapeDtypeStruct((count, width), WIDE),
            jax.ShapeDtypeStruct((count, width), WIDE),
            jax.ShapeDtypeStruct((count, width), BF16),
        ),
        grid=(1,),
        in_specs=[
            pl.BlockSpec((count, lanes_all), lambda i: (row, 0)),
            full_spec((count, 1)),
            full_spec((count, 1)),
            full_spec((1, keys)),
            full_spec((lanes_all, width)),
            row_spec((count, width), row),
            full_spec((1, width)),
            full_spec((1, width)),
        ]
        + [
            pl.BlockSpec((slots, 1, count, 2 * size), lambda i: (0, row, 0, 0)) for _ in kv_blocks
        ],
        out_specs=(
            full_spec((count, lanes_all)),
            full_spec((count, heads)),
            full_spec((count, width)),
            full_spec((count, width)),
            full_spec((count, width)),
        ),
        scratch_shapes=[pltpu.VMEM((keys, size), BF16), pltpu.VMEM((keys, size), BF16)],
    )(queries, start, place, key_place, out_weight, tokens, gain_out, gain_feed, *kv_blocks)


def close_row(row, parts, hidden, cotangent, gain):
    count, width = hidden.shape

    def kernel(a_ref, b_ref, c_ref, hidden_ref, e_ref, gain_ref, result_ref, d_ref, dg_ref):
        v = a_ref[0].astype(WIDE) + b_ref[...].astype(WIDE) + c_ref[...].astype(WIDE)
        g = gain_ref[...].astype(WIDE)
        z, r = unit(v, g)
        result_ref[...] = (hidden_ref[...] + z).astype(BF16)
        d_values, dg_ref[...] = unit_back(v, r, g, e_ref[0].astype(WIDE))
        d_ref[...] = d_values.astype(BF16)

    return vmem_call(
        kernel,
        (
            jax.ShapeDtypeStruct((count, width), BF16),
            jax.ShapeDtypeStruct((count, width), BF16),
            jax.ShapeDtypeStruct((1, width), WIDE),
        ),
        grid=(1,),
        in_specs=[
            row_spec((count, width), 0),
            full_spec((count, width)),
            full_spec((count, width)),
            full_spec((count, width)),
            row_spec((count, width), row),
            full_spec((1, width)),
        ],
        out_specs=(full_spec((count, width)), full_spec((count, width)), full_spec((1, width))),
    )(*parts, hidden, cotangent, gain)


def attend_backward(
    row,
    parts,
    kept,
    cotangent,
    out_weight,
    gain_out,
    gain_feed,
    queries,
    kv_blocks,
    place,
    key_place,
    raw,
    cosine,
    sine,
    gain,
    heads,
):
    count, width = kept["hidden"].shape
    slots = kv_blocks[0].shape[0]
    size = kv_blocks[0].shape[3] // 2
    half = size // 2
    keys = slots * len(kv_blocks) * count
    lanes_all = heads * size
    block_count = len(kv_blocks)

    def kernel(*refs):
        (
            a_ref,
            b_ref,
            c_ref,
            hidden_ref,
            projected_ref,
            e_ref,
            w_ref,
            g1_ref,
            g2_ref,
            q_ref,
            start_ref,
            place_ref,
            key_place_ref,
            log_ref,
            raw_ref,
            cos_ref,
            sin_ref,
            gain_ref,
        ) = refs[:18]
        kv_refs = refs[18 : 18 + block_count]
        outs = refs[18 + block_count :]
        d_hidden_ref, d_projected_ref, dg1_ref, dg2_ref, dq_ref, dgain_ref = outs[:6]
        dkv_refs = outs[6 : 6 + block_count]
        k_held, v_held, dk_acc, dv_acc, d_held = outs[6 + block_count :]
        g1 = g1_ref[...].astype(WIDE)
        g2 = g2_ref[...].astype(WIDE)
        e = a_ref[0].astype(WIDE) + b_ref[...].astype(WIDE) + c_ref[...].astype(WIDE)
        hidden = hidden_ref[...]
        d_values, dg2_ref[...] = unit_back(hidden, unit(hidden, g2)[1], g2, e)
        d_hidden = e_ref[0].astype(WIDE) + d_values
        d_hidden_ref[...] = d_hidden
        projected = projected_ref[...]
        d_values, dg1_ref[...] = unit_back(projected, unit(projected, g1)[1], g1, d_hidden)
        d_projected_ref[...] = d_values.astype(BF16)
        d_held[...] = lax.dot_general(
            d_projected_ref[...], w_ref[...], NT, preferred_element_type=WIDE
        ).astype(BF16)
        lay_out(kv_refs, k_held, v_held, size)
        allowed = allowed_mask(start_ref, place_ref, key_place_ref)
        gain_values = gain_ref[...].astype(WIDE)
        cos = cos_ref[...]
        sin = sin_ref[...]
        d_gain = jnp.zeros((1, size), WIDE)
        for h in range(heads):
            lanes = slice(h * size, (h + 1) * size)
            q = q_ref[:, lanes]
            d = d_held[:, lanes]
            k = k_held[...]
            scores = lax.dot_general(q, k, NT, preferred_element_type=WIDE) * SCORE_SCALE
            p = jnp.where(allowed, jnp.exp(scores - log_ref[:, h : h + 1]), 0.0)
            d_p = lax.dot_general(d, v_held[...], NT, preferred_element_type=WIDE)
            inner = jnp.sum(p * d_p, axis=-1, keepdims=True)
            d_s = (p * (d_p - inner)).astype(BF16)
            d_v = lax.dot_general(p.astype(BF16), d, TN, preferred_element_type=WIDE)
            d_k = lax.dot_general(d_s, q, TN, preferred_element_type=WIDE)
            if h == 0:
                dk_acc[...] = d_k
                dv_acc[...] = d_v
            else:
                dk_acc[...] += d_k
                dv_acc[...] += d_v
            d_q = jnp.dot(d_s, k, preferred_element_type=WIDE) * SCORE_SCALE
            d_a, d_b = d_q[:, :half], d_q[:, half:]
            turned = jnp.concatenate([d_a * cos + d_b * sin, d_b * cos - d_a * sin], axis=-1)
            u = raw_ref[:, lanes]
            d_u, d_part = unit_back(u, unit(u, gain_values)[1], gain_values, turned)
            dq_ref[:, lanes] = d_u.astype(BF16)
            d_gain += d_part
        dgain_ref[...] = d_gain
        at = 0
        for ref in dkv_refs:
            for slot in range(slots):
                ref[slot, :, :size] = (dk_acc[at : at + count] * SCORE_SCALE).astype(BF16)
                ref[slot, :, size:] = dv_acc[at : at + count].astype(BF16)
                at += count

    wide_rows = jax.ShapeDtypeStruct((count, width), WIDE)
    mine = pl.BlockSpec((count, lanes_all), lambda i: (row, 0))
    turn = pl.BlockSpec((count, half), lambda i: (row, 0))
    outs = vmem_call(
        kernel,
        (
            wide_rows,
            jax.ShapeDtypeStruct((count, width), BF16),
            jax.ShapeDtypeStruct((1, width), WIDE),
            jax.ShapeDtypeStruct((1, width), WIDE),
            jax.ShapeDtypeStruct((count, lanes_all), BF16),
            jax.ShapeDtypeStruct((1, size), WIDE),
        )
        + (jax.ShapeDtypeStruct((slots, count, 2 * size), BF16),) * block_count,
        grid=(1,),
        in_specs=[
            row_spec((count, width), 0),
            full_spec((count, width)),
            full_spec((count, width)),
            full_spec((count, width)),
            full_spec((count, width)),
            row_spec((count, width), row),
            full_spec((lanes_all, width)),
            full_spec((1, width)),
            full_spec((1, width)),
            mine,
            full_spec((count, 1)),
            full_spec((count, 1)),
            full_spec((1, keys)),
            full_spec((count, heads)),
            mine,
            turn,
            turn,
            full_spec((1, size)),
        ]
        + [
            pl.BlockSpec((slots, 1, count, 2 * size), lambda i: (0, row, 0, 0)) for _ in kv_blocks
        ],
        out_specs=(
            full_spec((count, width)),
            full_spec((count, width)),
            full_spec((1, width)),
            full_spec((1, width)),
            full_spec((count, lanes_all)),
            full_spec((1, size)),
        )
        + (full_spec((slots, count, 2 * size)),) * block_count,
        scratch_shapes=[
            pltpu.VMEM((keys, size), BF16),
            pltpu.VMEM((keys, size), BF16),
            pltpu.VMEM((keys, size), WIDE),
            pltpu.VMEM((keys, size), WIDE),
            pltpu.VMEM((count, lanes_all), BF16),
        ],
    )(
        *parts,
        kept["hidden"],
        kept["projected"],
        cotangent,
        out_weight,
        gain_out,
        gain_feed,
        queries,
        kept["start"],
        place,
        key_place,
        kept["log"],
        raw,
        cosine,
        sine,
        gain,
        *kv_blocks,
    )
    names = ("d_hidden", "d_projected", "grad_out_gain", "grad_feed_gain", "d_query_raw", "d_gain")
    kept.update(zip(names, outs[:6]))
    kept["d_kv"] = outs[6:]


def project_kv(order, normed, blocks, cosine, sine, gain, rows):
    tokens, width = normed.shape
    per_block, part, both = blocks[0].shape
    n = per_block * len(blocks)
    size = both // 2
    half = size // 2

    def kernel(order_ref, x_ref, cos_ref, sin_ref, gain_ref, *refs):
        block_refs = refs[: len(blocks)]
        kv_ref, raw_ref, held = refs[len(blocks) :]
        for d in range(n):
            slot = order_ref[d]
            for k, block in enumerate(block_refs):

                @pl.when((slot >= k * per_block) & (slot < (k + 1) * per_block))
                def _(d=d, k=k, block=block, slot=slot):
                    held[d * part : (d + 1) * part] = block[slot - k * per_block]

        both_raw = jnp.dot(x_ref[...], held[...], preferred_element_type=WIDE)
        u = both_raw[:, :size]
        raw_ref[...] = u
        k = unit(u, gain_ref[...].astype(WIDE))[0]
        cos, sin = cos_ref[...], sin_ref[...]
        a, b = k[:, :half], k[:, half:]
        kv = jnp.concatenate([a * cos - b * sin, b * cos + a * sin, both_raw[:, size:]], axis=-1)
        kv_ref[...] = kv.astype(BF16).reshape(rows, tokens // rows, both)

    return vmem_call(
        kernel,
        (
            jax.ShapeDtypeStruct((rows, tokens // rows, both), BF16),
            jax.ShapeDtypeStruct((tokens, size), WIDE),
            jax.ShapeDtypeStruct((width, both), BF16),
        ),
        in_specs=[smem_spec()] + [whole_spec()] * (4 + len(blocks)),
        out_specs=(whole_spec(), whole_spec(), whole_spec()),
    )(order, normed, cosine, sine, gain, *blocks)


def project_q(normed, weight, cosine, sine, gain, heads):
    tokens, width = normed.shape
    size = weight.shape[1] // heads
    half = size // 2

    def kernel(x_ref, w_ref, cos_ref, sin_ref, gain_ref, q_ref, raw_ref):
        cos, sin = cos_ref[...], sin_ref[...]
        raw_ref[...] = jnp.dot(x_ref[...], w_ref[...], preferred_element_type=WIDE)
        for h in range(heads):
            lanes = slice(h * size, (h + 1) * size)
            q = unit(raw_ref[:, lanes], gain_ref[...].astype(WIDE))[0]
            a, b = q[:, :half], q[:, half:]
            turned = jnp.concatenate([a * cos - b * sin, b * cos + a * sin], axis=-1)
            q_ref[:, lanes] = turned.astype(BF16)

    return vmem_call(
        kernel,
        (
            jax.ShapeDtypeStruct((tokens, heads * size), BF16),
            jax.ShapeDtypeStruct((tokens, heads * size), WIDE),
        ),
        in_specs=[whole_spec()] * 5,
        out_specs=(whole_spec(), whole_spec()),
    )(normed, weight, cosine, sine, gain)


def feed_step(tokens):
    return 256 if tokens % 256 == 0 else tokens


def feed_forward(inner, gate_w, up_w, down_w):
    tokens, width = inner.shape
    share = gate_w.shape[1]
    step = feed_step(tokens)

    def kernel(x_ref, gate_ref, up_ref, down_ref, slope_ref, value_ref, a_ref, low_ref):
        x = x_ref[...]
        g = jnp.dot(x, gate_ref[...], preferred_element_type=WIDE)
        u = jnp.dot(x, up_ref[...], preferred_element_type=WIDE)
        value, slope = gelu_parts(g)
        active = (value * u).astype(BF16)
        slope_ref[...] = (slope * u).astype(BF16)
        value_ref[...] = value.astype(BF16)
        a_ref[...] = active
        low_ref[...] = jnp.dot(active, down_ref[...], preferred_element_type=WIDE).astype(BF16)

    each = lambda columns: pl.BlockSpec((step, columns), lambda i: (i, 0))
    hidden = jax.ShapeDtypeStruct((tokens, share), BF16)
    return vmem_call(
        kernel,
        (hidden, hidden, hidden, jax.ShapeDtypeStruct((tokens, width), BF16)),
        limit=24,
        grid=(tokens // step,),
        in_specs=[each(width), whole_spec(), whole_spec(), whole_spec()],
        out_specs=(each(share), each(share), each(share), each(width)),
    )(inner, gate_w, up_w, down_w)


def feed_backward(d_lowered, slope, value, gate_w, up_w, down_w):
    tokens, width = d_lowered.shape
    share = gate_w.shape[1]
    step = feed_step(tokens)

    def kernel(d_ref, slope_ref, value_ref, gate_ref, up_ref, down_ref, dg_ref, du_ref, dx_ref):
        d_active = lax.dot_general(d_ref[...], down_ref[...], NT, preferred_element_type=WIDE)
        d_gate = (d_active * slope_ref[...].astype(WIDE)).astype(BF16)
        d_up = (d_active * value_ref[...].astype(WIDE)).astype(BF16)
        dg_ref[...] = d_gate
        du_ref[...] = d_up
        d_x = lax.dot_general(d_gate, gate_ref[...], NT, preferred_element_type=WIDE)
        d_x += lax.dot_general(d_up, up_ref[...], NT, preferred_element_type=WIDE)
        dx_ref[...] = d_x.astype(BF16)

    each = lambda columns: pl.BlockSpec((step, columns), lambda i: (i, 0))
    hidden = jax.ShapeDtypeStruct((tokens, share), BF16)
    return vmem_call(
        kernel,
        (hidden, hidden, jax.ShapeDtypeStruct((tokens, width), BF16)),
        limit=24,
        grid=(tokens // step,),
        in_specs=[each(width), each(share), each(share), whole_spec(), whole_spec(), whole_spec()],
        out_specs=(each(share), each(share), each(width)),
    )(d_lowered, slope, value, gate_w, up_w, down_w)


def weight_grad(lefts, rights):
    rows = lefts[0].shape[1]
    columns = rights[0].shape[1]
    count = len(lefts)
    size = 384

    def kernel(*refs):
        out_ref = refs[2 * count]
        for at in range(0, rows, size):
            lanes = slice(at, min(at + size, rows))
            term = None
            for k in range(count):
                part = lax.dot_general(
                    refs[k][:, lanes], refs[count + k][...], TN, preferred_element_type=WIDE
                )
                term = part if term is None else term + part
            out_ref[lanes, :] = term.astype(BF16)

    return vmem_call(
        kernel,
        jax.ShapeDtypeStruct((rows, columns), BF16),
        limit=24,
        in_specs=[whole_spec()] * (2 * count),
        out_specs=whole_spec(),
    )(*lefts, *rights)


def blocks_grad(order, left_sets, right_sets, n):
    rows = left_sets[0].shape[1]
    part = rows // n
    widths = [r.shape[1] for r in right_sets[0]]
    per_row = len(widths)
    count = len(left_sets)
    blocks = n // 4

    def kernel(order_ref, *refs):
        lefts = refs[:count]
        rights = refs[count : count + count * per_row]
        outs = refs[count + count * per_row : -1]
        held = refs[-1]
        for d in range(n):
            lanes = slice(d * part, (d + 1) * part)
            at = 0
            for j, size in enumerate(widths):
                term = None
                for k in range(count):
                    product = lax.dot_general(
                        lefts[k][:, lanes],
                        rights[k * per_row + j][...],
                        TN,
                        preferred_element_type=WIDE,
                    )
                    term = product if term is None else term + product
                held[order_ref[d], :, at : at + size] = term.astype(BF16)
                at += size
        for b, out in enumerate(outs):
            out[...] = held[4 * b : 4 * b + 4]

    flat = [r for rights in right_sets for r in rights]
    shape = jax.ShapeDtypeStruct((4, part, sum(widths)), BF16)
    return vmem_call(
        kernel,
        (shape,) * blocks,
        limit=24,
        in_specs=[smem_spec()] + [whole_spec()] * (count + len(flat)),
        out_specs=(whole_spec(),) * blocks,
        scratch_shapes=[pltpu.VMEM((n, part, sum(widths)), BF16)],
    )(order, *left_sets, *flat)


def close_keys(parts, raw, cosine, sine, gain):
    slots, rows, count, both = parts[0].shape
    size = both // 2
    half = size // 2

    def kernel(a_ref, b_ref, c_ref, raw_ref, cos_ref, sin_ref, gain_ref, *outs):
        gain_values = gain_ref[...].astype(WIDE)
        d_gain = jnp.zeros((1, size), WIDE)
        for row in range(rows):
            span = slice(row * count, (row + 1) * count)
            e = (
                a_ref[0, row].astype(WIDE) + b_ref[row].astype(WIDE) + c_ref[row].astype(WIDE)
            )
            cos, sin = cos_ref[span], sin_ref[span]
            d_a, d_b = e[:, :half], e[:, half:size]
            turned = jnp.concatenate([d_a * cos + d_b * sin, d_b * cos - d_a * sin], axis=-1)
            u = raw_ref[span]
            d_u, d_part = unit_back(u, unit(u, gain_values)[1], gain_values, turned)
            d_gain += d_part
            outs[row][:, :size] = d_u.astype(BF16)
            outs[row][:, size:] = e[:, size:].astype(BF16)
        outs[rows][...] = d_gain

    return vmem_call(
        kernel,
        (jax.ShapeDtypeStruct((count, both), BF16),) * rows
        + (jax.ShapeDtypeStruct((1, size), WIDE),),
        grid=(1,),
        in_specs=[
            pl.BlockSpec((1, rows, count, both), lambda i: (0, 0, 0, 0)),
            full_spec((rows, count, both)),
            full_spec((rows, count, both)),
            full_spec(raw.shape),
            full_spec(cosine.shape),
            full_spec(sine.shape),
            full_spec((1, size)),
        ],
        out_specs=(full_spec((count, both)),) * rows + (full_spec((1, size)),),
    )(*parts, raw, cosine, sine, gain)


def close_tokens(tokens, d_queries, d_kvs, query_w, kv_w, d_hiddens, gain):
    rows, count, width = tokens.shape

    def kernel(x_ref, q_ref, kv_ref, gain_ref, *refs):
        out_ref, dg_ref = refs[3 * rows :]
        g = gain_ref[...].astype(WIDE)
        d_gain = jnp.zeros((1, width), WIDE)
        for row in range(rows):
            d_q, d_kv, d_hidden = refs[row], refs[rows + row], refs[2 * rows + row]
            e = lax.dot_general(d_q[...], q_ref[...], NT, preferred_element_type=WIDE)
            e += lax.dot_general(d_kv[...], kv_ref[...], NT, preferred_element_type=WIDE)
            x = x_ref[row].astype(WIDE)
            d_x, d_part = unit_back(x, unit(x, g)[1], g, e)
            d_gain += d_part
            out_ref[row] = (d_hidden[...] + d_x).astype(BF16)
        dg_ref[...] = d_gain

    return vmem_call(
        kernel,
        (jax.ShapeDtypeStruct(tokens.shape, BF16), jax.ShapeDtypeStruct((1, width), WIDE)),
        in_specs=[whole_spec()] * (4 + 3 * rows),
        out_specs=(whole_spec(), whole_spec()),
    )(tokens, query_w, kv_w, gain, *d_queries, *d_kvs, *d_hiddens)


def per_device(
    tokens,
    cotangent,
    segment_ids,
    query_weight,
    key_weight,
    value_weight,
    out_weight,
    gate_weight,
    up_weight,
    down_weight,
    gain_input,
    gain_query,
    gain_key,
    gain_attended,
    gain_feed,
    gain_result,
):
    n = lax.axis_size("ctx")
    n_dp = lax.axis_size("dp")
    me = lax.axis_index("ctx")
    my_dp = lax.axis_index("dp")
    row_count, count_local, width = tokens.shape
    total = row_count * count_local
    head_width = gain_query.shape[0]
    head_count = query_weight.shape[1] // head_width
    qw = head_count * head_width
    share = gate_weight.shape[1] // n
    span = count_local // 2
    codes = xor_layout(n)[3]
    kv_weights = Gather(jnp.concatenate([key_weight, value_weight], axis=1), n)
    query_full = lax.all_gather(query_weight, "ctx", axis=0, tiled=True)
    even_flag = ((my_dp % 2) == 0).astype(jnp.int32).reshape(1)
    pieces = spread_pieces(even_flag, gate_weight, up_weight, n)
    spread = lax.all_to_all(pieces, "ctx", 0, 0)
    gain_row = {
        "input": after(gain_input, pieces).reshape(1, -1),
        "query": after(gain_query, pieces).reshape(1, -1),
        "key": after(gain_key, pieces).reshape(1, -1),
        "out": after(gain_attended, pieces).reshape(1, -1),
        "feed": after(gain_feed, pieces).reshape(1, -1),
        "result": after(gain_result, pieces).reshape(1, -1),
    }

    below = jnp.stack(
        [jnp.sum((segment_ids < s).astype(jnp.int32), axis=1) for s in range(5)], axis=1
    )
    code = 1
    while code < n:
        below = below + xor_permute(below, n, code)
        code *= 2
    starts = sum(jnp.where(segment_ids == s, below[:, s : s + 1], 0) for s in range(5))

    offsets = jnp.arange(span, dtype=jnp.int32)

    def places_of(device):
        return jnp.concatenate([device * span + offsets, (2 * n - 1 - device) * span + offsets])

    local_places = places_of(me)
    key_places = jnp.concatenate([places_of(me ^ code) for code in codes]).reshape(1, -1)
    place_column = local_places.reshape(-1, 1)
    angles = angles_for(local_places.astype(WIDE), head_width)
    cosine = jnp.concatenate([jnp.cos(angles)] * row_count, axis=0)
    sine = jnp.concatenate([jnp.sin(angles)] * row_count, axis=0)

    normed_rows = rms_norm(tokens.astype(WIDE), gain_input.astype(WIDE)).astype(BF16)
    normed = normed_rows.reshape(total, width)
    order_codes = me ^ jnp.arange(n, dtype=jnp.int32)
    order = sum(jnp.where(order_codes == c, k, 0) for k, c in enumerate(codes)).astype(jnp.int32)
    start_columns = [starts[row].reshape(-1, 1) for row in range(row_count)]
    kv_weights.mid(pieces).near()
    kv_local, key_raw, kv_full = project_kv(
        order, after(normed, spread), kv_weights.blocks, cosine, sine, gain_row["key"], row_count
    )
    kv_gather = Gather(kv_local, n)
    out_full = lax.all_gather(after(out_weight, kv_local), "ctx", axis=0, tiled=True)
    queries, query_raw = project_q(
        after(normed, kv_local), query_full, cosine, sine, gain_row["query"], head_count
    )
    kv_gather.mid(queries, *start_columns, *gain_row.values(), key_places, place_column)
    swapped = lax.ppermute(
        after(spread, kv_local), "dp", [(i, i ^ 1) for i in range(n_dp)]
    )
    kv_gather.near()
    kv_blocks = kv_gather.blocks

    def before_feed(row, *earlier):
        r = {"start": start_columns[row]}
        names = ("attended", "log", "projected", "hidden", "inner_local")
        outs = attend_forward(
            row,
            after(queries, *earlier),
            kv_blocks,
            r["start"],
            place_column,
            key_places,
            out_full,
            tokens,
            gain_row["out"],
            gain_row["feed"],
            head_count,
        )
        r.update(zip(names, outs))
        return r

    def feed_piece(r, block, *earlier):
        outs = feed_forward(after(block, *earlier), gate_mine, up_mine, down_weight)
        for name, out in zip(("inner", "slope", "value", "active"), (block,) + tuple(outs[:3])):
            r.setdefault(name, []).append(out)
        return outs[3].reshape(4, count_local, width)

    def back_piece(r, block, *earlier):
        k = len(r.setdefault("d_lowered", []))
        outs = feed_backward(
            after(block, *earlier), r["slope"][k], r["value"][k], gate_mine, up_mine, down_weight
        )
        for name, out in zip(("d_lowered", "d_gate", "d_up"), (block,) + tuple(outs[:2])):
            r.setdefault(name, []).append(out)
        return outs[2].reshape(4, count_local, width)

    def pieces_of(piece, r, blocks, *earlier):
        outs = []
        for block in blocks:
            outs.append(piece(r, block, *earlier, *outs[-1:]))
        return outs

    def result_piece(row, r, parts):
        r["result"], d_lowered, r["grad_result_gain"] = close_row(
            row, parts, r["hidden"], cotangent, gain_row["result"]
        )
        return d_lowered

    def attend_back(row, r, parts):
        attend_backward(
            row,
            parts,
            r,
            cotangent,
            out_full,
            gain_row["out"],
            gain_row["feed"],
            queries,
            kv_blocks,
            place_column,
            key_places,
            query_raw,
            cosine,
            sine,
            gain_row["query"],
            head_count,
        )

    r0 = before_feed(0)
    g0 = Gather(r0["inner_local"], n)
    r1 = before_feed(1, r0["inner_local"])
    g0.mid(r1["inner_local"])
    g1 = Gather(after(r1["inner_local"], g0.a, g0.b), n)
    gate_mine, up_mine = in_order(even_flag, spread, swapped)
    gate_mine = gate_mine.reshape(width, share)
    up_mine = up_mine.reshape(width, share)
    g0.near(gate_mine)
    blocks_0 = g0.flat()
    low_0 = [feed_piece(r0, blocks_0[0])]
    g1.mid(low_0[0])
    low_0 += pieces_of(feed_piece, r0, blocks_0[1:], low_0[0], g1.a)
    s0 = Scatter(low_0, n)
    g1.near(low_0[-1])
    blocks_1 = g1.flat()
    low_1 = [feed_piece(r1, blocks_1[0])]
    s0.mid(low_1[0])
    low_1 += pieces_of(feed_piece, r1, blocks_1[1:], low_1[0], s0.sums)
    s1 = Scatter(low_1, n)
    s0.far(low_1[-1])
    s1.mid(*s0.sent)
    d_low_0 = result_piece(0, r0, s0.finish(s1.sums))
    h0 = Gather(d_low_0, n)
    s1.far(d_low_0)
    h0.mid(*s1.sent)
    d_low_1 = result_piece(1, r1, s1.finish(h0.a))
    h1 = Gather(d_low_1, n)
    h0.near(d_low_1)
    blocks_0 = h0.flat()
    d_in_0 = [back_piece(r0, blocks_0[0])]
    h1.mid(d_in_0[0])
    d_in_0 += pieces_of(back_piece, r0, blocks_0[1:], d_in_0[0], h1.a)
    s0 = Scatter(d_in_0, n)
    h1.near(d_in_0[-1])
    blocks_1 = h1.flat()
    d_in_1 = [back_piece(r1, blocks_1[0])]
    s0.mid(d_in_1[0])
    rows = (r0, r1)

    def over_rows(left, right, *earlier):
        lefts, rights = r0[left] + r1[left], r0[right] + r1[right]
        return weight_grad([after(lefts[0], *earlier)] + lefts[1:], rights)

    grad_down = weight_grad(
        [after(r0["active"][0], s0.sums)] + r0["active"][1:] + r1["active"],
        r0["d_lowered"] + blocks_1,
    )
    def begin(part, *earlier):
        line = Line(after(part, *earlier), n_dp)
        clock[:] = [line.total]
        return line

    def land(line):
        line.moved = after(line.moved, *clock)
        clock[:] = [line.moved]

    def step(line, *earlier):
        if line.at < len(line.steps) - 1:
            line.step(*clock, *earlier)
            clock[:] = [line.total]

    def halves(x):
        half = x.shape[0] // 2
        return [x[:half], x[half:]]

    def exchange(grad):
        return lax.all_to_all(grad.reshape(n, width // n, share), "ctx", 0, 0)

    clock = [grad_down]
    summed_down = lax.psum(grad_down, "dp")
    d_in_1 += pieces_of(back_piece, r1, blocks_1[1:], *clock)
    s1 = Scatter(d_in_1, n)
    s0.far(d_in_1[-1])
    grad_gate = over_rows("inner", "d_gate", *s0.sent)
    gate_pieces = exchange(grad_gate)
    grad_up = over_rows("inner", "d_up", grad_gate)
    s1.mid(grad_up)
    clock[:] = [s1.sums]
    attend_back(0, r0, s0.finish(*clock))
    s1.far(r0["d_kv"][0])
    gate_halves = halves(gate_pieces)
    gl0 = begin(gate_halves[0], *s1.sent)
    gl1 = begin(gate_halves[1], *clock)
    up_pieces = exchange(after(grad_up, *clock))
    attend_back(1, r1, s1.finish(summed_down, *clock))
    clock[:] = [r1["d_kv"][0]]
    step(gl0)
    kv_scatter = Scatter(
        [jnp.stack([a, b], axis=1) for a, b in zip(r0["d_kv"], r1["d_kv"])], n
    )
    clock[:] = [gl0.total, *kv_scatter.blocks[-1:]]
    grad_out = (
        t_dot(after(r0["attended"], *clock), r0["d_projected"])
        + t_dot(r1["attended"], r1["d_projected"])
    ).astype(BF16)
    part_out = lax.psum_scatter(grad_out, "ctx", scatter_dimension=0, tiled=True)
    def total_of(parts):
        return (
            parts[0][0].astype(WIDE) + parts[1].astype(WIDE) + parts[2].astype(WIDE)
        ).astype(BF16)

    def last(line):
        line.moved = after(line.moved, *clock)
        total = line.finish().astype(WIDE)
        clock[:] = [total]
        return total

    def side_by_side(lines):
        ends = lines[0].steps[-1][2]
        mine = (my_dp == ends[0]) | (my_dp == ends[1]) if ends else my_dp < 0
        total = assemble(
            mine.astype(jnp.int32).reshape(1),
            [line.total for line in lines],
            [after(line.moved, *clock) for line in lines],
            width // n,
            n * share,
        )
        clock[:] = [total]
        return total

    kv_scatter.mid(grad_out)
    up_halves = halves(up_pieces)
    u0 = begin(up_halves[0], kv_scatter.sums)
    kv_scatter.far(*clock)
    clock[:] = [*kv_scatter.sent]
    step(gl1)
    *d_kvs, grad_key_gain = close_keys(
        kv_scatter.finish(*clock), key_raw, cosine, sine, gain_row["key"]
    )
    clock[:] = [d_kvs[0]]
    step(gl0)
    grad_qkv = blocks_grad(
        order,
        [
            after(normed[row * count_local : (row + 1) * count_local], *clock)
            for row in range(row_count)
        ],
        [[r["d_query_raw"], d_kv] for r, d_kv in zip(rows, d_kvs)],
        n,
    )
    qkv_scatter = Scatter(grad_qkv, n)
    clock[:] = [grad_qkv[0]]
    step(u0)
    u1 = begin(up_halves[1], *clock)
    step(gl1)
    qkv_scatter.mid(*clock)
    clock[:] = [qkv_scatter.sums]
    land(gl0)
    tokens_grad, grad_input_gain = close_tokens(
        tokens,
        [after(r["d_query_raw"], *clock) for r in rows],
        d_kvs,
        query_full,
        kv_full,
        [r["d_hidden"] for r in rows],
        gain_row["input"],
    )
    qkv_scatter.far(tokens_grad)
    gains = jnp.concatenate(
        [
            grad_input_gain,
            sum(r["d_gain"] for r in rows),
            grad_key_gain,
            sum(r["grad_out_gain"] for r in rows),
            sum(r["grad_feed_gain"] for r in rows),
            sum(r["grad_result_gain"] for r in rows),
        ],
        axis=1,
    ).reshape(-1, 128)
    clock[:] = [*qkv_scatter.sent]
    step(u1)
    step(u0)
    part_qkv = total_of(qkv_scatter.finish(*clock))
    clock[:] = [part_qkv]
    qkv_line = begin(part_qkv, *clock)
    land(gl1)
    out_line = begin(part_out, *clock)
    code = 1
    gains = after(gains, *clock)
    while code < n:
        gains = gains + xor_permute(gains, n, code)
        code *= 2
    clock[:] = [gains]
    gain_line = begin(gains, *clock)
    step(u1)
    land(u0)
    step(qkv_line)
    step(out_line)
    step(gain_line)
    for _ in range(n_dp):
        for line in (gl0, gl1, u0, u1, qkv_line, out_line, gain_line):
            step(line)
    summed_gate = side_by_side([gl0, gl1])
    summed_up = side_by_side([u0, u1])
    summed_out = last(out_line)
    summed_qkv = last(qkv_line)
    gains = last(gain_line).reshape(-1)
    sizes = [width, head_width, head_width, width, width, width]
    gain_grads = []
    start = 0
    for size in sizes:
        gain_grads.append(gains[start : start + size])
        start += size
    return (
        jnp.stack([r["result"] for r in rows]),
        tokens_grad,
        summed_qkv[:, :qw],
        summed_qkv[:, qw : qw + head_width],
        summed_qkv[:, qw + head_width :],
        summed_out,
        summed_gate,
        summed_up,
        summed_down.astype(WIDE),
        *gain_grads,
    )


def solution(mesh):
    return jax.shard_map(
        per_device,
        mesh=mesh,
        in_specs=(
            P("dp", "ctx", None),
            P("dp", "ctx", None),
            P("dp", "ctx"),
            P("ctx", None),
            P("ctx", None),
            P("ctx", None),
            P("ctx", None),
            P("ctx", None),
            P("ctx", None),
            P("ctx", None),
            P(),
            P(),
            P(),
            P(),
            P(),
            P(),
        ),
        out_specs=(
            P("dp", "ctx", None),
            P("dp", "ctx", None),
            P("ctx", None),
            P("ctx", None),
            P("ctx", None),
            P("ctx", None),
            P("ctx", None),
            P("ctx", None),
            P("ctx", None),
            P(),
            P(),
            P(),
            P(),
            P(),
            P(),
        ),
        check_vma=False,
    )
```

```python
import jax
import jax.numpy as jnp
from jax import lax
from jax.experimental import pallas as pl
from jax.experimental.pallas import tpu as pltpu
from jax.sharding import PartitionSpec as P

EPSILON = 1e-06
ROPE_BASE = 1000000.0
SCORE_SCALE = 0.0625
NEGATIVE = -1e30
GELU_COEFF = 0.044715
ROOT_TWO_PI = 0.7978845608028654
BF16 = jnp.bfloat16
WIDE = jnp.float32


def rms_norm(values, gain_values):
    return (
        values
        * lax.rsqrt(jnp.mean(values * values, axis=-1, keepdims=True) + EPSILON)
        * gain_values
    )


def angles_for(positions, width):
    half_width = width // 2
    frequencies = jnp.power(ROPE_BASE, -jnp.arange(half_width, dtype=jnp.float32) / half_width)
    return positions[:, None] * frequencies[None, :]


def gelu_parts(gate):
    square = gate * gate
    bent = jnp.tanh(ROOT_TWO_PI * (gate + GELU_COEFF * gate * square))
    rise = 0.5 * (1.0 + bent)
    slope = rise + 0.5 * gate * (1.0 - bent * bent) * ROOT_TWO_PI * (
        1.0 + 3.0 * GELU_COEFF * square
    )
    return gate * rise, slope


def dot(left, right):
    return jnp.dot(left, right, preferred_element_type=WIDE)


def dot_t(left, right):
    return lax.dot_general(left, right, (((1,), (1,)), ((), ())), preferred_element_type=WIDE)


def t_dot(left, right):
    return lax.dot_general(left, right, (((0,), (0,)), ((), ())), preferred_element_type=WIDE)


def after(x, *earlier):
    return lax.optimization_barrier((x,) + earlier)[0] if earlier else x


def together(xs, *earlier):
    return lax.optimization_barrier(tuple(xs) + earlier)[: len(xs)]


def xor_permute(x, axis_size, code):
    return lax.ppermute(x, "ctx", [(i, i ^ code) for i in range(axis_size)])


def xor_layout(n):
    far_y, far_x = n // 2, n // 4
    near = [1 << b for b in range((n // 4).bit_length() - 1)]
    codes = [0, far_x, far_y, far_x ^ far_y]
    for bit in near:
        codes = codes + [c ^ bit for c in codes]
    return far_x, far_y, near, codes


class Gather:
    def __init__(self, x, n):
        self.n = n
        self.far_x, self.far_y, self.near_bits, _ = xor_layout(n)
        self.x = x
        self.a = xor_permute(x, n, self.far_x)
        self.b = xor_permute(x, n, self.far_y)

    def mid(self, *earlier):
        half = self.x.shape[0] // 2
        a, b = together((self.a, self.b), *earlier)
        self.d1 = xor_permute(a[:half], self.n, self.far_y)
        self.d2 = xor_permute(b[half:], self.n, self.far_x)
        return self

    def near(self, *earlier):
        d1, d2 = together((self.d1, self.d2), *earlier)
        self.blocks = [stack_blocks(self.x, self.a, self.b, d1, d2)]
        for bit in self.near_bits:
            self.blocks = self.blocks + [xor_permute(b, self.n, bit) for b in self.blocks]
        return self

    def flat(self):
        return [b.reshape((4 * self.x.shape[0],) + self.x.shape[1:]) for b in self.blocks]


class Scatter:
    def __init__(self, blocks, n):
        self.n = n
        self.far_x, self.far_y, self.near_bits, _ = xor_layout(n)
        self.blocks = list(blocks)
        self.bits = list(reversed(self.near_bits))
        self.send_near()

    def send_near(self):
        if self.bits:
            count = len(self.blocks) // 2
            self.arrived = [xor_permute(b, self.n, self.bits[0]) for b in self.blocks[count:]]

    def mid(self, *earlier):
        while self.bits:
            count = len(self.blocks) // 2
            self.arrived[0] = after(self.arrived[0], *earlier)
            self.blocks = [
                (mine.astype(WIDE) + theirs.astype(WIDE)).astype(BF16)
                for mine, theirs in zip(self.blocks[:count], self.arrived)
            ]
            self.bits = self.bits[1:]
            self.send_near()
        self.sums = self.blocks[0]
        half = self.sums.shape[1] // 2
        self.d_x = xor_permute(self.sums[3, :half], self.n, self.far_x)
        self.d_y = xor_permute(self.sums[3, half:], self.n, self.far_y)
        return self

    def far(self, *earlier):
        half = self.sums.shape[1] // 2
        d_x, d_y = together((self.d_x, self.d_y), *earlier)
        d_x, d_y = d_x.astype(WIDE), d_y.astype(WIDE)
        x, y = self.sums[1].astype(WIDE), self.sums[2].astype(WIDE)
        to_x = jnp.concatenate([x[:half], x[half:] + d_y], axis=0).astype(BF16)
        to_y = jnp.concatenate([y[:half] + d_x, y[half:]], axis=0).astype(BF16)
        self.from_x = xor_permute(to_x, self.n, self.far_x)
        self.from_y = xor_permute(to_y, self.n, self.far_y)
        self.sent = (to_x, to_y)
        return self

    def finish(self, *earlier):
        return self.sums, *together((self.from_x, self.from_y), *earlier)


class Line:
    def __init__(self, part, n):
        self.n = n
        self.total = part
        mid = n // 2
        self.steps = []
        for s in range(mid - 1):
            self.steps.append(("in", [(s, s + 1), (n - 1 - s, n - 2 - s)], None))
        self.steps.append(("in", [(mid - 1, mid), (mid, mid - 1)], None))
        for s in range(mid - 2, -1, -1):
            self.steps.append(("out", [(s + 1, s), (n - 2 - s, n - 1 - s)], (s, n - 1 - s)))
        self.at = 0
        self.send()

    def send(self):
        if self.at < len(self.steps):
            self.moved = lax.ppermute(self.total, "dp", self.steps[self.at][1])

    def step(self, *earlier):
        kind, _, ends = self.steps[self.at]
        moved = after(self.moved, *earlier)
        if kind == "in":
            total = self.total.astype(WIDE) + moved.astype(WIDE)
            self.total = total.astype(self.total.dtype)
        else:
            me = lax.axis_index("dp")
            self.total = jnp.where((me == ends[0]) | (me == ends[1]), moved, self.total)
        self.at += 1
        self.send()
        return self.total

    def finish(self):
        while self.at < len(self.steps):
            self.step()
        return self.total


NT = (((1,), (1,)), ((), ()))
TN = (((0,), (0,)), ((), ()))
MIB = 1024 * 1024


def vmem_call(kernel, out_shape, limit=32, **kwargs):
    return pl.pallas_call(
        kernel,
        out_shape=out_shape,
        compiler_params=pltpu.CompilerParams(vmem_limit_bytes=limit * MIB),
        cost_estimate=pl.CostEstimate(flops=0, bytes_accessed=0, transcendentals=0),
        **kwargs,
    )


def whole_spec():
    return pl.BlockSpec(memory_space=pltpu.VMEM)


def smem_spec():
    return pl.BlockSpec(memory_space=pltpu.SMEM)


def full_spec(shape):
    return pl.BlockSpec(shape, lambda i: (0,) * len(shape))


def row_spec(shape, row):
    return pl.BlockSpec((1,) + shape, lambda i: (row,) + (0,) * len(shape))


def unit(values, gain_values):
    r = lax.rsqrt(jnp.mean(values * values, axis=-1, keepdims=True) + EPSILON)
    return values * r * gain_values, r


def unit_back(values, r, gain_values, e):
    ge = gain_values * e
    d_values = r * ge - values * (r * r * r * jnp.mean(ge * values, axis=-1, keepdims=True))
    return d_values, jnp.sum(e * values * r, axis=0, keepdims=True)


def stack_blocks(x, a, b, d1, d2):
    half = d1.shape[0]

    def kernel(x_ref, a_ref, b_ref, d1_ref, d2_ref, out_ref):
        out_ref[0] = x_ref[...]
        out_ref[1] = a_ref[...]
        out_ref[2] = b_ref[...]
        out_ref[3, :half] = d1_ref[...]
        out_ref[3, half:] = d2_ref[...]

    return vmem_call(
        kernel,
        jax.ShapeDtypeStruct((4,) + x.shape, x.dtype),
        in_specs=[whole_spec()] * 5,
        out_specs=whole_spec(),
    )(x, a, b, d1, d2)


def spread_pieces(flag, first, second, n):
    rows, columns = first.shape
    share = columns // n

    def kernel(flag_ref, first_ref, second_ref, out_ref):
        def fill(source):
            for k in range(n):
                out_ref[k] = source[:, k * share : (k + 1) * share]

        @pl.when(flag_ref[0] == 1)
        def _():
            fill(first_ref)

        @pl.when(flag_ref[0] != 1)
        def _():
            fill(second_ref)

    return vmem_call(
        kernel,
        jax.ShapeDtypeStruct((n, rows, share), first.dtype),
        in_specs=[smem_spec(), whole_spec(), whole_spec()],
        out_specs=whole_spec(),
    )(flag, first, second)


def in_order(flag, first, second):
    def kernel(flag_ref, first_ref, second_ref, a_ref, b_ref):
        @pl.when(flag_ref[0] == 1)
        def _():
            a_ref[...] = first_ref[...]
            b_ref[...] = second_ref[...]

        @pl.when(flag_ref[0] != 1)
        def _():
            a_ref[...] = second_ref[...]
            b_ref[...] = first_ref[...]

    parts, rows, columns = first.shape
    step = pl.BlockSpec((1, rows, columns), lambda i: (i, 0, 0))
    return vmem_call(
        kernel,
        (jax.ShapeDtypeStruct(first.shape, first.dtype),) * 2,
        grid=(parts,),
        in_specs=[smem_spec(), step, step],
        out_specs=(step, step),
    )(flag, first, second)


def assemble(flag, totals, moveds, rows, columns):
    count = len(totals)
    share = totals[0].shape[2]
    moveds = moveds or []

    def kernel(flag_ref, *refs):
        out_ref = refs[-1]

        def fill(parts):
            at = 0
            for part in parts:
                for k in range(part.shape[0]):
                    out_ref[:, at * share : (at + 1) * share] = part[k].astype(WIDE)
                    at += 1

        if not moveds:
            fill(refs[:count])
            return

        @pl.when(flag_ref[0] == 1)
        def _():
            fill(refs[count : 2 * count])

        @pl.when(flag_ref[0] != 1)
        def _():
            fill(refs[:count])

    return vmem_call(
        kernel,
        jax.ShapeDtypeStruct((rows, columns), WIDE),
        in_specs=[smem_spec()] + [whole_spec()] * (count + len(moveds)),
        out_specs=whole_spec(),
    )(flag, *totals, *moveds)


def allowed_mask(start_ref, place_ref, key_place_ref):
    key_place = key_place_ref[...]
    return (start_ref[...] <= key_place) & (place_ref[...] >= key_place)


def lay_out(kv_refs, k_held, v_held, size):
    at = 0
    for ref in kv_refs:
        for slot in range(ref.shape[0]):
            tokens = ref.shape[2]
            k_held[at : at + tokens] = ref[slot, 0, :, :size]
            v_held[at : at + tokens] = ref[slot, 0, :, size:]
            at += tokens


def attend_forward(
    row, queries, kv_blocks, start, place, key_place, out_weight, tokens, gain_out, gain_feed, heads
):
    count = start.shape[0]
    width = tokens.shape[2]
    slots = kv_blocks[0].shape[0]
    size = kv_blocks[0].shape[3] // 2
    keys = slots * len(kv_blocks) * count
    lanes_all = heads * size

    def kernel(*refs):
        q_ref, start_ref, place_ref, key_place_ref, w_ref, x_ref, g1_ref, g2_ref = refs[:8]
        kv_refs = refs[8 : 8 + len(kv_blocks)]
        out_ref, log_ref, projected_ref, hidden_ref, inner_ref, k_held, v_held = refs[
            8 + len(kv_blocks) :
        ]
        lay_out(kv_refs, k_held, v_held, size)
        allowed = allowed_mask(start_ref, place_ref, key_place_ref)
        for h in range(heads):
            q = q_ref[:, h * size : (h + 1) * size]
            scores = lax.dot_general(q, k_held[...], NT, preferred_element_type=WIDE) * SCORE_SCALE
            scores = jnp.where(allowed, scores, NEGATIVE)
            peak = jnp.max(scores, axis=-1, keepdims=True)
            raised = jnp.exp(scores - peak)
            weight = jnp.sum(raised, axis=-1, keepdims=True)
            probabilities = (raised * (1.0 / weight)).astype(BF16)
            out = jnp.dot(probabilities, v_held[...], preferred_element_type=WIDE)
            out_ref[:, h * size : (h + 1) * size] = out.astype(BF16)
            log_ref[:, h : h + 1] = peak + jnp.log(weight)
        projected = jnp.dot(out_ref[...], w_ref[...], preferred_element_type=WIDE)
        projected_ref[...] = projected
        hidden = x_ref[0].astype(WIDE) + unit(projected, g1_ref[...].astype(WIDE))[0]
        hidden_ref[...] = hidden
        inner_ref[...] = unit(hidden, g2_ref[...].astype(WIDE))[0].astype(BF16)

    return vmem_call(
        kernel,
        (
            jax.ShapeDtypeStruct((count, lanes_all), BF16),
            jax.ShapeDtypeStruct((count, heads), WIDE),
            jax.ShapeDtypeStruct((count, width), WIDE),
            jax.ShapeDtypeStruct((count, width), WIDE),
            jax.ShapeDtypeStruct((count, width), BF16),
        ),
        limit=48,
        grid=(1,),
        in_specs=[
            pl.BlockSpec((count, lanes_all), lambda i: (row, 0)),
            full_spec((count, 1)),
            full_spec((count, 1)),
            full_spec((1, keys)),
            full_spec((lanes_all, width)),
            row_spec((count, width), row),
            full_spec((1, width)),
            full_spec((1, width)),
        ]
        + [
            pl.BlockSpec((slots, 1, count, 2 * size), lambda i: (0, row, 0, 0)) for _ in kv_blocks
        ],
        out_specs=(
            full_spec((count, lanes_all)),
            full_spec((count, heads)),
            full_spec((count, width)),
            full_spec((count, width)),
            full_spec((count, width)),
        ),
        scratch_shapes=[pltpu.VMEM((keys, size), BF16), pltpu.VMEM((keys, size), BF16)],
    )(queries, start, place, key_place, out_weight, tokens, gain_out, gain_feed, *kv_blocks)


def close_row(row, parts, hidden, cotangent, gain):
    count, width = hidden.shape

    def kernel(a_ref, b_ref, c_ref, hidden_ref, e_ref, gain_ref, result_ref, d_ref, dg_ref):
        v = a_ref[0].astype(WIDE) + b_ref[...].astype(WIDE) + c_ref[...].astype(WIDE)
        g = gain_ref[...].astype(WIDE)
        z, r = unit(v, g)
        result_ref[...] = (hidden_ref[...] + z).astype(BF16)
        d_values, dg_ref[...] = unit_back(v, r, g, e_ref[0].astype(WIDE))
        d_ref[...] = d_values.astype(BF16)

    return vmem_call(
        kernel,
        (
            jax.ShapeDtypeStruct((count, width), BF16),
            jax.ShapeDtypeStruct((count, width), BF16),
            jax.ShapeDtypeStruct((1, width), WIDE),
        ),
        grid=(1,),
        in_specs=[
            row_spec((count, width), 0),
            full_spec((count, width)),
            full_spec((count, width)),
            full_spec((count, width)),
            row_spec((count, width), row),
            full_spec((1, width)),
        ],
        out_specs=(full_spec((count, width)), full_spec((count, width)), full_spec((1, width))),
    )(*parts, hidden, cotangent, gain)


def attend_backward(
    row,
    parts,
    kept,
    cotangent,
    out_weight,
    gain_out,
    gain_feed,
    queries,
    kv_blocks,
    place,
    key_place,
    raw,
    cosine,
    sine,
    gain,
    heads,
):
    count, width = kept["hidden"].shape
    slots = kv_blocks[0].shape[0]
    size = kv_blocks[0].shape[3] // 2
    half = size // 2
    keys = slots * len(kv_blocks) * count
    lanes_all = heads * size
    block_count = len(kv_blocks)

    def kernel(*refs):
        (
            a_ref,
            b_ref,
            c_ref,
            hidden_ref,
            projected_ref,
            e_ref,
            w_ref,
            g1_ref,
            g2_ref,
            q_ref,
            start_ref,
            place_ref,
            key_place_ref,
            log_ref,
            raw_ref,
            cos_ref,
            sin_ref,
            gain_ref,
        ) = refs[:18]
        kv_refs = refs[18 : 18 + block_count]
        outs = refs[18 + block_count :]
        d_hidden_ref, d_projected_ref, dg1_ref, dg2_ref, dq_ref, dgain_ref = outs[:6]
        dkv_refs = outs[6 : 6 + block_count]
        k_held, v_held, dk_acc, dv_acc, d_held = outs[6 + block_count :]
        g1 = g1_ref[...].astype(WIDE)
        g2 = g2_ref[...].astype(WIDE)
        e = a_ref[0].astype(WIDE) + b_ref[...].astype(WIDE) + c_ref[...].astype(WIDE)
        hidden = hidden_ref[...]
        d_values, dg2_ref[...] = unit_back(hidden, unit(hidden, g2)[1], g2, e)
        d_hidden = e_ref[0].astype(WIDE) + d_values
        d_hidden_ref[...] = d_hidden
        projected = projected_ref[...]
        d_values, dg1_ref[...] = unit_back(projected, unit(projected, g1)[1], g1, d_hidden)
        d_projected_ref[...] = d_values.astype(BF16)
        d_held[...] = lax.dot_general(
            d_projected_ref[...], w_ref[...], NT, preferred_element_type=WIDE
        ).astype(BF16)
        lay_out(kv_refs, k_held, v_held, size)
        allowed = allowed_mask(start_ref, place_ref, key_place_ref)
        gain_values = gain_ref[...].astype(WIDE)
        cos = cos_ref[...]
        sin = sin_ref[...]
        d_gain = jnp.zeros((1, size), WIDE)
        for h in range(heads):
            lanes = slice(h * size, (h + 1) * size)
            q = q_ref[:, lanes]
            d = d_held[:, lanes]
            k = k_held[...]
            scores = lax.dot_general(q, k, NT, preferred_element_type=WIDE) * SCORE_SCALE
            p = jnp.where(allowed, jnp.exp(scores - log_ref[:, h : h + 1]), 0.0)
            d_p = lax.dot_general(d, v_held[...], NT, preferred_element_type=WIDE)
            inner = jnp.sum(p * d_p, axis=-1, keepdims=True)
            d_s = (p * (d_p - inner)).astype(BF16)
            d_v = lax.dot_general(p.astype(BF16), d, TN, preferred_element_type=WIDE)
            d_k = lax.dot_general(d_s, q, TN, preferred_element_type=WIDE)
            if h == 0:
                dk_acc[...] = d_k
                dv_acc[...] = d_v
            else:
                dk_acc[...] += d_k
                dv_acc[...] += d_v
            d_q = jnp.dot(d_s, k, preferred_element_type=WIDE) * SCORE_SCALE
            d_a, d_b = d_q[:, :half], d_q[:, half:]
            turned = jnp.concatenate([d_a * cos + d_b * sin, d_b * cos - d_a * sin], axis=-1)
            u = raw_ref[:, lanes]
            d_u, d_part = unit_back(u, unit(u, gain_values)[1], gain_values, turned)
            dq_ref[:, lanes] = d_u.astype(BF16)
            d_gain += d_part
        dgain_ref[...] = d_gain
        at = 0
        for ref in dkv_refs:
            for slot in range(slots):
                ref[slot, :, :size] = (dk_acc[at : at + count] * SCORE_SCALE).astype(BF16)
                ref[slot, :, size:] = dv_acc[at : at + count].astype(BF16)
                at += count

    wide_rows = jax.ShapeDtypeStruct((count, width), WIDE)
    mine = pl.BlockSpec((count, lanes_all), lambda i: (row, 0))
    turn = pl.BlockSpec((count, half), lambda i: (row, 0))
    outs = vmem_call(
        kernel,
        (
            wide_rows,
            jax.ShapeDtypeStruct((count, width), BF16),
            jax.ShapeDtypeStruct((1, width), WIDE),
            jax.ShapeDtypeStruct((1, width), WIDE),
            jax.ShapeDtypeStruct((count, lanes_all), BF16),
            jax.ShapeDtypeStruct((1, size), WIDE),
        )
        + (jax.ShapeDtypeStruct((slots, count, 2 * size), BF16),) * block_count,
        limit=48,
        grid=(1,),
        in_specs=[
            row_spec((count, width), 0),
            full_spec((count, width)),
            full_spec((count, width)),
            full_spec((count, width)),
            full_spec((count, width)),
            row_spec((count, width), row),
            full_spec((lanes_all, width)),
            full_spec((1, width)),
            full_spec((1, width)),
            mine,
            full_spec((count, 1)),
            full_spec((count, 1)),
            full_spec((1, keys)),
            full_spec((count, heads)),
            mine,
            turn,
            turn,
            full_spec((1, size)),
        ]
        + [
            pl.BlockSpec((slots, 1, count, 2 * size), lambda i: (0, row, 0, 0)) for _ in kv_blocks
        ],
        out_specs=(
            full_spec((count, width)),
            full_spec((count, width)),
            full_spec((1, width)),
            full_spec((1, width)),
            full_spec((count, lanes_all)),
            full_spec((1, size)),
        )
        + (full_spec((slots, count, 2 * size)),) * block_count,
        scratch_shapes=[
            pltpu.VMEM((keys, size), BF16),
            pltpu.VMEM((keys, size), BF16),
            pltpu.VMEM((keys, size), WIDE),
            pltpu.VMEM((keys, size), WIDE),
            pltpu.VMEM((count, lanes_all), BF16),
        ],
    )(
        *parts,
        kept["hidden"],
        kept["projected"],
        cotangent,
        out_weight,
        gain_out,
        gain_feed,
        queries,
        kept["start"],
        place,
        key_place,
        kept["log"],
        raw,
        cosine,
        sine,
        gain,
        *kv_blocks,
    )
    names = ("d_hidden", "d_projected", "grad_out_gain", "grad_feed_gain", "d_query_raw", "d_gain")
    kept.update(zip(names, outs[:6]))
    kept["d_kv"] = outs[6:]


def project_kv(order, normed, blocks, cosine, sine, gain, rows):
    tokens, width = normed.shape
    per_block, part, both = blocks[0].shape
    n = per_block * len(blocks)
    size = both // 2
    half = size // 2

    def kernel(order_ref, x_ref, cos_ref, sin_ref, gain_ref, *refs):
        block_refs = refs[: len(blocks)]
        kv_ref, raw_ref, held = refs[len(blocks) :]
        for d in range(n):
            slot = order_ref[d]
            for k, block in enumerate(block_refs):

                @pl.when((slot >= k * per_block) & (slot < (k + 1) * per_block))
                def _(d=d, k=k, block=block, slot=slot):
                    held[d * part : (d + 1) * part] = block[slot - k * per_block]

        both_raw = jnp.dot(x_ref[...], held[...], preferred_element_type=WIDE)
        u = both_raw[:, :size]
        raw_ref[...] = u
        k = unit(u, gain_ref[...].astype(WIDE))[0]
        cos, sin = cos_ref[...], sin_ref[...]
        a, b = k[:, :half], k[:, half:]
        kv = jnp.concatenate([a * cos - b * sin, b * cos + a * sin, both_raw[:, size:]], axis=-1)
        kv_ref[...] = kv.astype(BF16).reshape(rows, tokens // rows, both)

    return vmem_call(
        kernel,
        (
            jax.ShapeDtypeStruct((rows, tokens // rows, both), BF16),
            jax.ShapeDtypeStruct((tokens, size), WIDE),
            jax.ShapeDtypeStruct((width, both), BF16),
        ),
        in_specs=[smem_spec()] + [whole_spec()] * (4 + len(blocks)),
        out_specs=(whole_spec(), whole_spec(), whole_spec()),
    )(order, normed, cosine, sine, gain, *blocks)


def project_q(normed, weight, cosine, sine, gain, heads):
    tokens, width = normed.shape
    size = weight.shape[1] // heads
    half = size // 2

    def kernel(x_ref, w_ref, cos_ref, sin_ref, gain_ref, q_ref, raw_ref):
        cos, sin = cos_ref[...], sin_ref[...]
        raw_ref[...] = jnp.dot(x_ref[...], w_ref[...], preferred_element_type=WIDE)
        for h in range(heads):
            lanes = slice(h * size, (h + 1) * size)
            q = unit(raw_ref[:, lanes], gain_ref[...].astype(WIDE))[0]
            a, b = q[:, :half], q[:, half:]
            turned = jnp.concatenate([a * cos - b * sin, b * cos + a * sin], axis=-1)
            q_ref[:, lanes] = turned.astype(BF16)

    return vmem_call(
        kernel,
        (
            jax.ShapeDtypeStruct((tokens, heads * size), BF16),
            jax.ShapeDtypeStruct((tokens, heads * size), WIDE),
        ),
        in_specs=[whole_spec()] * 5,
        out_specs=(whole_spec(), whole_spec()),
    )(normed, weight, cosine, sine, gain)


def feed_step(tokens):
    return 256 if tokens % 256 == 0 else tokens


def feed_forward(inner, gate_w, up_w, down_w):
    tokens, width = inner.shape
    share = gate_w.shape[1]
    step = feed_step(tokens)

    def kernel(x_ref, gate_ref, up_ref, down_ref, slope_ref, value_ref, a_ref, low_ref):
        x = x_ref[...]
        g = jnp.dot(x, gate_ref[...], preferred_element_type=WIDE)
        u = jnp.dot(x, up_ref[...], preferred_element_type=WIDE)
        value, slope = gelu_parts(g)
        active = (value * u).astype(BF16)
        slope_ref[...] = (slope * u).astype(BF16)
        value_ref[...] = value.astype(BF16)
        a_ref[...] = active
        low_ref[...] = jnp.dot(active, down_ref[...], preferred_element_type=WIDE).astype(BF16)

    each = lambda columns: pl.BlockSpec((step, columns), lambda i: (i, 0))
    hidden = jax.ShapeDtypeStruct((tokens, share), BF16)
    return vmem_call(
        kernel,
        (hidden, hidden, hidden, jax.ShapeDtypeStruct((tokens, width), BF16)),
        limit=24,
        grid=(tokens // step,),
        in_specs=[each(width), whole_spec(), whole_spec(), whole_spec()],
        out_specs=(each(share), each(share), each(share), each(width)),
    )(inner, gate_w, up_w, down_w)


def feed_backward(d_lowered, slope, value, gate_w, up_w, down_w):
    tokens, width = d_lowered.shape
    share = gate_w.shape[1]
    step = feed_step(tokens)

    def kernel(d_ref, slope_ref, value_ref, gate_ref, up_ref, down_ref, dg_ref, du_ref, dx_ref):
        d_active = lax.dot_general(d_ref[...], down_ref[...], NT, preferred_element_type=WIDE)
        d_gate = (d_active * slope_ref[...].astype(WIDE)).astype(BF16)
        d_up = (d_active * value_ref[...].astype(WIDE)).astype(BF16)
        dg_ref[...] = d_gate
        du_ref[...] = d_up
        d_x = lax.dot_general(d_gate, gate_ref[...], NT, preferred_element_type=WIDE)
        d_x += lax.dot_general(d_up, up_ref[...], NT, preferred_element_type=WIDE)
        dx_ref[...] = d_x.astype(BF16)

    each = lambda columns: pl.BlockSpec((step, columns), lambda i: (i, 0))
    hidden = jax.ShapeDtypeStruct((tokens, share), BF16)
    return vmem_call(
        kernel,
        (hidden, hidden, jax.ShapeDtypeStruct((tokens, width), BF16)),
        limit=24,
        grid=(tokens // step,),
        in_specs=[each(width), each(share), each(share), whole_spec(), whole_spec(), whole_spec()],
        out_specs=(each(share), each(share), each(width)),
    )(d_lowered, slope, value, gate_w, up_w, down_w)


def weight_grad(lefts, rights):
    rows = lefts[0].shape[1]
    columns = rights[0].shape[1]
    count = len(lefts)
    size = 384

    def kernel(*refs):
        out_ref = refs[2 * count]
        for at in range(0, rows, size):
            lanes = slice(at, min(at + size, rows))
            term = None
            for k in range(count):
                part = lax.dot_general(
                    refs[k][:, lanes], refs[count + k][...], TN, preferred_element_type=WIDE
                )
                term = part if term is None else term + part
            out_ref[lanes, :] = term.astype(BF16)

    return vmem_call(
        kernel,
        jax.ShapeDtypeStruct((rows, columns), BF16),
        limit=24,
        in_specs=[whole_spec()] * (2 * count),
        out_specs=whole_spec(),
    )(*lefts, *rights)


def blocks_grad(order, left_sets, right_sets, n):
    rows = left_sets[0].shape[1]
    part = rows // n
    widths = [r.shape[1] for r in right_sets[0]]
    per_row = len(widths)
    count = len(left_sets)
    blocks = n // 4

    def kernel(order_ref, *refs):
        lefts = refs[:count]
        rights = refs[count : count + count * per_row]
        outs = refs[count + count * per_row : -1]
        held = refs[-1]
        for d in range(n):
            lanes = slice(d * part, (d + 1) * part)
            at = 0
            for j, size in enumerate(widths):
                term = None
                for k in range(count):
                    product = lax.dot_general(
                        lefts[k][:, lanes],
                        rights[k * per_row + j][...],
                        TN,
                        preferred_element_type=WIDE,
                    )
                    term = product if term is None else term + product
                held[order_ref[d], :, at : at + size] = term.astype(BF16)
                at += size
        for b, out in enumerate(outs):
            out[...] = held[4 * b : 4 * b + 4]

    flat = [r for rights in right_sets for r in rights]
    shape = jax.ShapeDtypeStruct((4, part, sum(widths)), BF16)
    return vmem_call(
        kernel,
        (shape,) * blocks,
        limit=24,
        in_specs=[smem_spec()] + [whole_spec()] * (count + len(flat)),
        out_specs=(whole_spec(),) * blocks,
        scratch_shapes=[pltpu.VMEM((n, part, sum(widths)), BF16)],
    )(order, *left_sets, *flat)


def close_keys(parts, raw, cosine, sine, gain):
    slots, rows, count, both = parts[0].shape
    size = both // 2
    half = size // 2

    def kernel(a_ref, b_ref, c_ref, raw_ref, cos_ref, sin_ref, gain_ref, *outs):
        gain_values = gain_ref[...].astype(WIDE)
        d_gain = jnp.zeros((1, size), WIDE)
        for row in range(rows):
            span = slice(row * count, (row + 1) * count)
            e = (
                a_ref[0, row].astype(WIDE) + b_ref[row].astype(WIDE) + c_ref[row].astype(WIDE)
            )
            cos, sin = cos_ref[span], sin_ref[span]
            d_a, d_b = e[:, :half], e[:, half:size]
            turned = jnp.concatenate([d_a * cos + d_b * sin, d_b * cos - d_a * sin], axis=-1)
            u = raw_ref[span]
            d_u, d_part = unit_back(u, unit(u, gain_values)[1], gain_values, turned)
            d_gain += d_part
            outs[row][:, :size] = d_u.astype(BF16)
            outs[row][:, size:] = e[:, size:].astype(BF16)
        outs[rows][...] = d_gain

    return vmem_call(
        kernel,
        (jax.ShapeDtypeStruct((count, both), BF16),) * rows
        + (jax.ShapeDtypeStruct((1, size), WIDE),),
        grid=(1,),
        in_specs=[
            pl.BlockSpec((1, rows, count, both), lambda i: (0, 0, 0, 0)),
            full_spec((rows, count, both)),
            full_spec((rows, count, both)),
            full_spec(raw.shape),
            full_spec(cosine.shape),
            full_spec(sine.shape),
            full_spec((1, size)),
        ],
        out_specs=(full_spec((count, both)),) * rows + (full_spec((1, size)),),
    )(*parts, raw, cosine, sine, gain)


def close_tokens(tokens, d_queries, d_kvs, query_w, kv_w, d_hiddens, gain):
    rows, count, width = tokens.shape

    def kernel(x_ref, q_ref, kv_ref, gain_ref, *refs):
        out_ref, dg_ref = refs[3 * rows :]
        g = gain_ref[...].astype(WIDE)
        d_gain = jnp.zeros((1, width), WIDE)
        for row in range(rows):
            d_q, d_kv, d_hidden = refs[row], refs[rows + row], refs[2 * rows + row]
            e = lax.dot_general(d_q[...], q_ref[...], NT, preferred_element_type=WIDE)
            e += lax.dot_general(d_kv[...], kv_ref[...], NT, preferred_element_type=WIDE)
            x = x_ref[row].astype(WIDE)
            d_x, d_part = unit_back(x, unit(x, g)[1], g, e)
            d_gain += d_part
            out_ref[row] = (d_hidden[...] + d_x).astype(BF16)
        dg_ref[...] = d_gain

    return vmem_call(
        kernel,
        (jax.ShapeDtypeStruct(tokens.shape, BF16), jax.ShapeDtypeStruct((1, width), WIDE)),
        in_specs=[whole_spec()] * (4 + 3 * rows),
        out_specs=(whole_spec(), whole_spec()),
    )(tokens, query_w, kv_w, gain, *d_queries, *d_kvs, *d_hiddens)


def per_device(
    tokens,
    cotangent,
    segment_ids,
    query_weight,
    key_weight,
    value_weight,
    out_weight,
    gate_weight,
    up_weight,
    down_weight,
    gain_input,
    gain_query,
    gain_key,
    gain_attended,
    gain_feed,
    gain_result,
):
    n = lax.axis_size("ctx")
    n_dp = lax.axis_size("dp")
    me = lax.axis_index("ctx")
    my_dp = lax.axis_index("dp")
    row_count, count_local, width = tokens.shape
    total = row_count * count_local
    head_width = gain_query.shape[0]
    head_count = query_weight.shape[1] // head_width
    qw = head_count * head_width
    share = gate_weight.shape[1] // n
    span = count_local // 2
    codes = xor_layout(n)[3]
    kv_weights = Gather(jnp.concatenate([key_weight, value_weight], axis=1), n)
    query_full = lax.all_gather(query_weight, "ctx", axis=0, tiled=True)
    even_flag = ((my_dp % 2) == 0).astype(jnp.int32).reshape(1)
    below = jnp.stack(
        [jnp.sum((segment_ids < s).astype(jnp.int32), axis=1) for s in range(5)], axis=1
    )
    code = 1
    while code < n:
        below = below + xor_permute(below, n, code)
        code *= 2
    starts = sum(jnp.where(segment_ids == s, below[:, s : s + 1], 0) for s in range(5))
    start_columns = [starts[row].reshape(-1, 1) for row in range(row_count)]
    kv_weights.mid()
    pieces = spread_pieces(
        even_flag, after(gate_weight, kv_weights.a, kv_weights.b, starts), up_weight, n
    )
    spread = lax.all_to_all(pieces, "ctx", 0, 0)
    kv_weights.near(pieces)
    gain_row = {
        "input": after(gain_input, pieces).reshape(1, -1),
        "query": after(gain_query, pieces).reshape(1, -1),
        "key": after(gain_key, pieces).reshape(1, -1),
        "out": after(gain_attended, pieces).reshape(1, -1),
        "feed": after(gain_feed, pieces).reshape(1, -1),
        "result": after(gain_result, pieces).reshape(1, -1),
    }

    offsets = jnp.arange(span, dtype=jnp.int32)

    def places_of(device):
        return jnp.concatenate([device * span + offsets, (2 * n - 1 - device) * span + offsets])

    local_places = places_of(me)
    key_places = jnp.concatenate([places_of(me ^ code) for code in codes]).reshape(1, -1)
    place_column = local_places.reshape(-1, 1)
    angles = angles_for(local_places.astype(WIDE), head_width)
    cosine = jnp.concatenate([jnp.cos(angles)] * row_count, axis=0)
    sine = jnp.concatenate([jnp.sin(angles)] * row_count, axis=0)

    normed_rows = rms_norm(tokens.astype(WIDE), gain_input.astype(WIDE)).astype(BF16)
    normed = normed_rows.reshape(total, width)
    order_codes = me ^ jnp.arange(n, dtype=jnp.int32)
    order = sum(jnp.where(order_codes == c, k, 0) for k, c in enumerate(codes)).astype(jnp.int32)
    kv_local, key_raw, kv_full = project_kv(
        order, normed, kv_weights.blocks, cosine, sine, gain_row["key"], row_count
    )
    kv_gather = Gather(kv_local, n)
    out_full = lax.all_gather(after(out_weight, kv_local), "ctx", axis=0, tiled=True)
    queries, query_raw = project_q(
        after(normed, kv_local), query_full, cosine, sine, gain_row["query"], head_count
    )
    kv_gather.mid(spread, *start_columns, *gain_row.values(), key_places, place_column)
    swapped = lax.ppermute(
        after(spread, kv_gather.a, kv_gather.b), "dp", [(i, i ^ 1) for i in range(n_dp)]
    )
    kv_gather.near(queries)
    kv_blocks = kv_gather.blocks

    def before_feed(row, *earlier):
        r = {"start": start_columns[row]}
        names = ("attended", "log", "projected", "hidden", "inner_local")
        outs = attend_forward(
            row,
            after(queries, *earlier),
            kv_blocks,
            r["start"],
            place_column,
            key_places,
            out_full,
            tokens,
            gain_row["out"],
            gain_row["feed"],
            head_count,
        )
        r.update(zip(names, outs))
        return r

    def feed_piece(r, block, *earlier):
        outs = feed_forward(after(block, *earlier), gate_mine, up_mine, down_weight)
        for name, out in zip(("inner", "slope", "value", "active"), (block,) + tuple(outs[:3])):
            r.setdefault(name, []).append(out)
        return outs[3].reshape(4, count_local, width)

    def back_piece(r, block, *earlier):
        k = len(r.setdefault("d_lowered", []))
        outs = feed_backward(
            after(block, *earlier), r["slope"][k], r["value"][k], gate_mine, up_mine, down_weight
        )
        for name, out in zip(("d_lowered", "d_gate", "d_up"), (block,) + tuple(outs[:2])):
            r.setdefault(name, []).append(out)
        return outs[2].reshape(4, count_local, width)

    def pieces_of(piece, r, blocks, *earlier):
        outs = []
        for block in blocks:
            outs.append(piece(r, block, *earlier, *outs[-1:]))
        return outs

    def result_piece(row, r, parts):
        r["result"], d_lowered, r["grad_result_gain"] = close_row(
            row, parts, r["hidden"], cotangent, gain_row["result"]
        )
        return d_lowered

    def attend_back(row, r, parts):
        attend_backward(
            row,
            parts,
            r,
            cotangent,
            out_full,
            gain_row["out"],
            gain_row["feed"],
            queries,
            kv_blocks,
            place_column,
            key_places,
            query_raw,
            cosine,
            sine,
            gain_row["query"],
            head_count,
        )

    r0 = before_feed(0)
    g0 = Gather(r0["inner_local"], n)
    r1 = before_feed(1, r0["inner_local"])
    g0.mid(r1["inner_local"])
    g1 = Gather(after(r1["inner_local"], g0.a, g0.b), n)
    gate_mine, up_mine = in_order(even_flag, spread, swapped)
    gate_mine = gate_mine.reshape(width, share)
    up_mine = up_mine.reshape(width, share)
    g0.near(gate_mine, g1.a, g1.b)
    g1.mid(g0.blocks[0])
    blocks_0 = g0.flat()
    low_0 = [feed_piece(r0, blocks_0[0])]
    low_0 += pieces_of(feed_piece, r0, blocks_0[1:], low_0[0])
    s0 = Scatter(low_0, n)
    g1.near(low_0[-1])
    blocks_1 = g1.flat()
    low_1 = [feed_piece(r1, blocks_1[0])]
    s0.mid(low_1[0])
    low_1 += pieces_of(feed_piece, r1, blocks_1[1:], low_1[0], s0.sums)
    s1 = Scatter(low_1, n)
    s0.far(low_1[-1])
    s1.mid(*s0.sent)
    d_low_0 = result_piece(0, r0, s0.finish(s1.sums))
    h0 = Gather(d_low_0, n)
    s1.far(d_low_0)
    h0.mid(*s1.sent)
    d_low_1 = result_piece(1, r1, s1.finish(h0.a))
    h1 = Gather(d_low_1, n)
    h0.near(d_low_1)
    blocks_0 = h0.flat()
    d_in_0 = [back_piece(r0, blocks_0[0])]
    h1.mid(d_in_0[0])
    d_in_0 += pieces_of(back_piece, r0, blocks_0[1:], d_in_0[0], h1.a, h1.b)
    s0 = Scatter(d_in_0, n)
    h1.near(d_in_0[-1])
    blocks_1 = h1.flat()
    d_in_1 = [back_piece(r1, blocks_1[0])]
    s0.mid(d_in_1[0])
    rows = (r0, r1)

    def over_rows(left, right, *earlier):
        lefts, rights = r0[left] + r1[left], r0[right] + r1[right]
        return weight_grad([after(lefts[0], *earlier)] + lefts[1:], rights)

    grad_down = weight_grad(
        [after(r0["active"][0], s0.sums)] + r0["active"][1:] + r1["active"],
        r0["d_lowered"] + blocks_1,
    )
    def begin(part, *earlier):
        line = Line(after(part, *earlier), n_dp)
        clock[:] = [line.total]
        return line

    def land(line):
        line.moved = after(line.moved, *clock)
        clock[:] = [line.moved]

    def step(line, *earlier):
        if line.at < len(line.steps) - 1:
            line.step(*clock, *earlier)
            clock[:] = [line.total]

    def halves(x):
        half = x.shape[0] // 2
        return [x[:half], x[half:]]

    def exchange(grad):
        return lax.all_to_all(grad.reshape(n, width // n, share), "ctx", 0, 0)

    clock = [grad_down]
    summed_down = lax.psum(grad_down, "dp")
    d_in_1 += pieces_of(back_piece, r1, blocks_1[1:], *clock)
    s1 = Scatter(d_in_1, n)
    s0.far(d_in_1[-1])
    grad_gate = over_rows("inner", "d_gate", *s0.sent)
    gate_pieces = exchange(grad_gate)
    s1.mid(grad_gate)
    attend_back(0, r0, s0.finish(s1.sums))
    s1.far(r0["d_kv"][0])
    grad_up = over_rows("inner", "d_up", *s1.sent)
    up_pieces = exchange(grad_up)
    gate_halves = halves(gate_pieces)
    gl0 = begin(gate_halves[0], grad_up)
    attend_back(1, r1, s1.finish(summed_down, *clock))
    gl1 = begin(gate_halves[1], r1["d_kv"][0])
    step(gl0)
    kv_scatter = Scatter(
        [jnp.stack([a, b], axis=1) for a, b in zip(r0["d_kv"], r1["d_kv"])], n
    )
    clock[:] = [gl0.total, *kv_scatter.blocks[-1:]]
    grad_out = (
        t_dot(after(r0["attended"], *clock), r0["d_projected"])
        + t_dot(r1["attended"], r1["d_projected"])
    ).astype(BF16)
    part_out = lax.psum_scatter(grad_out, "ctx", scatter_dimension=0, tiled=True)
    def total_of(parts):
        return (
            parts[0][0].astype(WIDE) + parts[1].astype(WIDE) + parts[2].astype(WIDE)
        ).astype(BF16)

    def last(line):
        line.moved = after(line.moved, *clock)
        total = line.finish().astype(WIDE)
        clock[:] = [total]
        return total

    def side_by_side(lines):
        ends = lines[0].steps[-1][2]
        mine = (my_dp == ends[0]) | (my_dp == ends[1]) if ends else my_dp < 0
        total = assemble(
            mine.astype(jnp.int32).reshape(1),
            [line.total for line in lines],
            [after(line.moved, *clock) for line in lines],
            width // n,
            n * share,
        )
        clock[:] = [total]
        return total

    kv_scatter.mid(grad_out)
    up_halves = halves(up_pieces)
    u0 = begin(up_halves[0], kv_scatter.sums)
    kv_scatter.far(*clock)
    clock[:] = [*kv_scatter.sent]
    step(gl1)
    *d_kvs, grad_key_gain = close_keys(
        kv_scatter.finish(*clock), key_raw, cosine, sine, gain_row["key"]
    )
    clock[:] = [d_kvs[0]]
    step(gl0)
    step(u0)
    step(gl1)
    u1 = begin(up_halves[1], *clock)
    grad_qkv = blocks_grad(
        order,
        [
            after(normed[row * count_local : (row + 1) * count_local], *clock)
            for row in range(row_count)
        ],
        [[r["d_query_raw"], d_kv] for r, d_kv in zip(rows, d_kvs)],
        n,
    )
    qkv_scatter = Scatter(grad_qkv, n)
    qkv_scatter.mid(grad_qkv[0])
    tokens_grad, grad_input_gain = close_tokens(
        tokens,
        [after(r["d_query_raw"], qkv_scatter.sums) for r in rows],
        d_kvs,
        query_full,
        kv_full,
        [r["d_hidden"] for r in rows],
        gain_row["input"],
    )
    qkv_scatter.far(tokens_grad)
    gains = jnp.concatenate(
        [
            grad_input_gain,
            sum(r["d_gain"] for r in rows),
            grad_key_gain,
            sum(r["grad_out_gain"] for r in rows),
            sum(r["grad_feed_gain"] for r in rows),
            sum(r["grad_result_gain"] for r in rows),
        ],
        axis=1,
    ).reshape(-1, 128)
    clock[:] = [*qkv_scatter.sent]
    gains = after(gains, *clock)
    land(gl0)
    step(u1)
    step(u0)
    summed_down = after(summed_down, *clock).astype(WIDE)
    result = after(jnp.stack([r["result"] for r in rows]), *clock)
    clock[:] = [summed_down, result]
    part_qkv = total_of(qkv_scatter.finish(*clock))
    clock[:] = [part_qkv]
    qkv_line = begin(part_qkv, *clock)
    land(gl1)
    out_line = begin(part_out, *clock)
    code = 1
    while code < n:
        gains = gains + xor_permute(gains, n, code)
        code *= 2
    step(qkv_line)
    step(u1)
    land(u0)
    step(out_line)
    gain_line = begin(gains, *clock)
    step(qkv_line)
    step(gain_line)
    step(out_line)
    for _ in range(n_dp):
        for line in (gl0, gl1, u0, u1, qkv_line, out_line, gain_line):
            step(line)
    summed_gate = side_by_side([gl0, gl1])
    summed_up = side_by_side([u0, u1])
    summed_out = last(out_line)
    summed_qkv = last(qkv_line)
    gains = last(gain_line).reshape(-1)
    sizes = [width, head_width, head_width, width, width, width]
    gain_grads = []
    start = 0
    for size in sizes:
        gain_grads.append(gains[start : start + size])
        start += size
    return (
        result,
        tokens_grad,
        summed_qkv[:, :qw],
        summed_qkv[:, qw : qw + head_width],
        summed_qkv[:, qw + head_width :],
        summed_out,
        summed_gate,
        summed_up,
        summed_down,
        *gain_grads,
    )


def solution(mesh):
    return jax.shard_map(
        per_device,
        mesh=mesh,
        in_specs=(
            P("dp", "ctx", None),
            P("dp", "ctx", None),
            P("dp", "ctx"),
            P("ctx", None),
            P("ctx", None),
            P("ctx", None),
            P("ctx", None),
            P("ctx", None),
            P("ctx", None),
            P("ctx", None),
            P(),
            P(),
            P(),
            P(),
            P(),
            P(),
        ),
        out_specs=(
            P("dp", "ctx", None),
            P("dp", "ctx", None),
            P("ctx", None),
            P("ctx", None),
            P("ctx", None),
            P("ctx", None),
            P("ctx", None),
            P("ctx", None),
            P("ctx", None),
            P(),
            P(),
            P(),
            P(),
            P(),
            P(),
        ),
        check_vma=False,
    )
```

```python
import jax
import jax.numpy as jnp
from jax import lax
from jax.experimental import pallas as pl
from jax.experimental.pallas import tpu as pltpu
from jax.sharding import PartitionSpec as P

EPSILON = 1e-06
ROPE_BASE = 1000000.0
SCORE_SCALE = 0.0625
NEGATIVE = -1e30
GELU_COEFF = 0.044715
ROOT_TWO_PI = 0.7978845608028654
BF16 = jnp.bfloat16
WIDE = jnp.float32


def rms_norm(values, gain_values):
    return (
        values
        * lax.rsqrt(jnp.mean(values * values, axis=-1, keepdims=True) + EPSILON)
        * gain_values
    )


def angles_for(positions, width):
    half_width = width // 2
    frequencies = jnp.power(ROPE_BASE, -jnp.arange(half_width, dtype=jnp.float32) / half_width)
    return positions[:, None] * frequencies[None, :]


def gelu_parts(gate):
    square = gate * gate
    bent = jnp.tanh(ROOT_TWO_PI * (gate + GELU_COEFF * gate * square))
    rise = 0.5 * (1.0 + bent)
    slope = rise + 0.5 * gate * (1.0 - bent * bent) * ROOT_TWO_PI * (
        1.0 + 3.0 * GELU_COEFF * square
    )
    return gate * rise, slope


def dot(left, right):
    return jnp.dot(left, right, preferred_element_type=WIDE)


def dot_t(left, right):
    return lax.dot_general(left, right, (((1,), (1,)), ((), ())), preferred_element_type=WIDE)


def t_dot(left, right):
    return lax.dot_general(left, right, (((0,), (0,)), ((), ())), preferred_element_type=WIDE)


def after(x, *earlier):
    return lax.optimization_barrier((x,) + earlier)[0] if earlier else x


def together(xs, *earlier):
    return lax.optimization_barrier(tuple(xs) + earlier)[: len(xs)]


def xor_permute(x, axis_size, code):
    return lax.ppermute(x, "ctx", [(i, i ^ code) for i in range(axis_size)])


def xor_layout(n):
    far_y, far_x = n // 2, n // 4
    near = [1 << b for b in range((n // 4).bit_length() - 1)]
    codes = [0, far_x, far_y, far_x ^ far_y]
    for bit in near:
        codes = codes + [c ^ bit for c in codes]
    return far_x, far_y, near, codes


class Gather:
    def __init__(self, x, n):
        self.n = n
        self.far_x, self.far_y, self.near_bits, _ = xor_layout(n)
        self.x = x
        self.a = xor_permute(x, n, self.far_x)
        self.b = xor_permute(x, n, self.far_y)

    def mid(self, *earlier):
        half = self.x.shape[0] // 2
        a, b = together((self.a, self.b), *earlier)
        self.d1 = xor_permute(a[:half], self.n, self.far_y)
        self.d2 = xor_permute(b[half:], self.n, self.far_x)
        return self

    def near(self, *earlier):
        d1, d2 = together((self.d1, self.d2), *earlier)
        self.blocks = [stack_blocks(self.x, self.a, self.b, d1, d2)]
        for bit in self.near_bits:
            self.blocks = self.blocks + [xor_permute(b, self.n, bit) for b in self.blocks]
        return self

    def flat(self):
        return [b.reshape((4 * self.x.shape[0],) + self.x.shape[1:]) for b in self.blocks]


class Scatter:
    def __init__(self, blocks, n):
        self.n = n
        self.far_x, self.far_y, self.near_bits, _ = xor_layout(n)
        self.blocks = list(blocks)
        self.bits = list(reversed(self.near_bits))
        self.send_near()

    def send_near(self):
        if self.bits:
            count = len(self.blocks) // 2
            self.arrived = [xor_permute(b, self.n, self.bits[0]) for b in self.blocks[count:]]

    def mid(self, *earlier):
        while self.bits:
            count = len(self.blocks) // 2
            self.arrived[0] = after(self.arrived[0], *earlier)
            self.blocks = [
                (mine.astype(WIDE) + theirs.astype(WIDE)).astype(BF16)
                for mine, theirs in zip(self.blocks[:count], self.arrived)
            ]
            self.bits = self.bits[1:]
            self.send_near()
        self.sums = self.blocks[0]
        half = self.sums.shape[1] // 2
        self.d_x = xor_permute(self.sums[3, :half], self.n, self.far_x)
        self.d_y = xor_permute(self.sums[3, half:], self.n, self.far_y)
        return self

    def far(self, *earlier):
        half = self.sums.shape[1] // 2
        d_x, d_y = together((self.d_x, self.d_y), *earlier)
        d_x, d_y = d_x.astype(WIDE), d_y.astype(WIDE)
        x, y = self.sums[1].astype(WIDE), self.sums[2].astype(WIDE)
        to_x = jnp.concatenate([x[:half], x[half:] + d_y], axis=0).astype(BF16)
        to_y = jnp.concatenate([y[:half] + d_x, y[half:]], axis=0).astype(BF16)
        self.from_x = xor_permute(to_x, self.n, self.far_x)
        self.from_y = xor_permute(to_y, self.n, self.far_y)
        self.sent = (to_x, to_y)
        return self

    def finish(self, *earlier):
        return self.sums, *together((self.from_x, self.from_y), *earlier)


class Line:
    def __init__(self, part, n):
        self.n = n
        self.total = part
        mid = n // 2
        self.steps = []
        for s in range(mid - 1):
            self.steps.append(("in", [(s, s + 1), (n - 1 - s, n - 2 - s)], None))
        self.steps.append(("in", [(mid - 1, mid), (mid, mid - 1)], None))
        for s in range(mid - 2, -1, -1):
            self.steps.append(("out", [(s + 1, s), (n - 2 - s, n - 1 - s)], (s, n - 1 - s)))
        self.at = 0
        self.send()

    def send(self):
        if self.at < len(self.steps):
            self.moved = lax.ppermute(self.total, "dp", self.steps[self.at][1])

    def step(self, *earlier):
        kind, _, ends = self.steps[self.at]
        moved = after(self.moved, *earlier)
        if kind == "in":
            total = self.total.astype(WIDE) + moved.astype(WIDE)
            self.total = total.astype(self.total.dtype)
        else:
            me = lax.axis_index("dp")
            self.total = jnp.where((me == ends[0]) | (me == ends[1]), moved, self.total)
        self.at += 1
        self.send()
        return self.total

    def finish(self):
        while self.at < len(self.steps):
            self.step()
        return self.total


NT = (((1,), (1,)), ((), ()))
TN = (((0,), (0,)), ((), ()))
MIB = 1024 * 1024


def vmem_call(kernel, out_shape, limit=32, **kwargs):
    return pl.pallas_call(
        kernel,
        out_shape=out_shape,
        compiler_params=pltpu.CompilerParams(vmem_limit_bytes=limit * MIB),
        cost_estimate=pl.CostEstimate(flops=0, bytes_accessed=0, transcendentals=0),
        **kwargs,
    )


def whole_spec():
    return pl.BlockSpec(memory_space=pltpu.VMEM)


def smem_spec():
    return pl.BlockSpec(memory_space=pltpu.SMEM)


def full_spec(shape):
    return pl.BlockSpec(shape, lambda i: (0,) * len(shape))


def row_spec(shape, row):
    return pl.BlockSpec((1,) + shape, lambda i: (row,) + (0,) * len(shape))


def unit(values, gain_values):
    r = lax.rsqrt(jnp.mean(values * values, axis=-1, keepdims=True) + EPSILON)
    return values * r * gain_values, r


def unit_back(values, r, gain_values, e):
    ge = gain_values * e
    d_values = r * ge - values * (r * r * r * jnp.mean(ge * values, axis=-1, keepdims=True))
    return d_values, jnp.sum(e * values * r, axis=0, keepdims=True)


def stack_blocks(x, a, b, d1, d2):
    half = d1.shape[0]

    def kernel(x_ref, a_ref, b_ref, d1_ref, d2_ref, out_ref):
        out_ref[0] = x_ref[...]
        out_ref[1] = a_ref[...]
        out_ref[2] = b_ref[...]
        out_ref[3, :half] = d1_ref[...]
        out_ref[3, half:] = d2_ref[...]

    return vmem_call(
        kernel,
        jax.ShapeDtypeStruct((4,) + x.shape, x.dtype),
        in_specs=[whole_spec()] * 5,
        out_specs=whole_spec(),
    )(x, a, b, d1, d2)


def spread_pieces(flag, first, second, n):
    rows, columns = first.shape
    share = columns // n

    def kernel(flag_ref, first_ref, second_ref, out_ref):
        def fill(source):
            for k in range(n):
                out_ref[k] = source[:, k * share : (k + 1) * share]

        @pl.when(flag_ref[0] == 1)
        def _():
            fill(first_ref)

        @pl.when(flag_ref[0] != 1)
        def _():
            fill(second_ref)

    return vmem_call(
        kernel,
        jax.ShapeDtypeStruct((n, rows, share), first.dtype),
        in_specs=[smem_spec(), whole_spec(), whole_spec()],
        out_specs=whole_spec(),
    )(flag, first, second)


def in_order(flag, first, second):
    def kernel(flag_ref, first_ref, second_ref, a_ref, b_ref):
        @pl.when(flag_ref[0] == 1)
        def _():
            a_ref[...] = first_ref[...]
            b_ref[...] = second_ref[...]

        @pl.when(flag_ref[0] != 1)
        def _():
            a_ref[...] = second_ref[...]
            b_ref[...] = first_ref[...]

    parts, rows, columns = first.shape
    step = pl.BlockSpec((1, rows, columns), lambda i: (i, 0, 0))
    return vmem_call(
        kernel,
        (jax.ShapeDtypeStruct(first.shape, first.dtype),) * 2,
        grid=(parts,),
        in_specs=[smem_spec(), step, step],
        out_specs=(step, step),
    )(flag, first, second)


def assemble(flag, totals, moveds, rows, columns):
    count = len(totals)
    share = totals[0].shape[2]
    moveds = moveds or []

    def kernel(flag_ref, *refs):
        out_ref = refs[-1]

        def fill(parts):
            at = 0
            for part in parts:
                for k in range(part.shape[0]):
                    out_ref[:, at * share : (at + 1) * share] = part[k].astype(WIDE)
                    at += 1

        if not moveds:
            fill(refs[:count])
            return

        @pl.when(flag_ref[0] == 1)
        def _():
            fill(refs[count : 2 * count])

        @pl.when(flag_ref[0] != 1)
        def _():
            fill(refs[:count])

    return vmem_call(
        kernel,
        jax.ShapeDtypeStruct((rows, columns), WIDE),
        in_specs=[smem_spec()] + [whole_spec()] * (count + len(moveds)),
        out_specs=whole_spec(),
    )(flag, *totals, *moveds)


def allowed_mask(start_ref, place_ref, key_place_ref):
    key_place = key_place_ref[...]
    return (start_ref[...] <= key_place) & (place_ref[...] >= key_place)


def lay_out(kv_refs, k_held, v_held, size):
    at = 0
    for ref in kv_refs:
        for slot in range(ref.shape[0]):
            tokens = ref.shape[2]
            k_held[at : at + tokens] = ref[slot, 0, :, :size]
            v_held[at : at + tokens] = ref[slot, 0, :, size:]
            at += tokens


def attend_forward(
    row, queries, kv_blocks, start, place, key_place, out_weight, tokens, gain_out, gain_feed, heads
):
    count = start.shape[0]
    width = tokens.shape[2]
    slots = kv_blocks[0].shape[0]
    size = kv_blocks[0].shape[3] // 2
    keys = slots * len(kv_blocks) * count
    lanes_all = heads * size

    def kernel(*refs):
        q_ref, start_ref, place_ref, key_place_ref, w_ref, x_ref, g1_ref, g2_ref = refs[:8]
        kv_refs = refs[8 : 8 + len(kv_blocks)]
        out_ref, log_ref, projected_ref, hidden_ref, inner_ref, k_held, v_held = refs[
            8 + len(kv_blocks) :
        ]
        lay_out(kv_refs, k_held, v_held, size)
        allowed = allowed_mask(start_ref, place_ref, key_place_ref)
        for h in range(heads):
            q = q_ref[:, h * size : (h + 1) * size]
            scores = lax.dot_general(q, k_held[...], NT, preferred_element_type=WIDE) * SCORE_SCALE
            scores = jnp.where(allowed, scores, NEGATIVE)
            peak = jnp.max(scores, axis=-1, keepdims=True)
            raised = jnp.exp(scores - peak)
            weight = jnp.sum(raised, axis=-1, keepdims=True)
            probabilities = (raised * (1.0 / weight)).astype(BF16)
            out = jnp.dot(probabilities, v_held[...], preferred_element_type=WIDE)
            out_ref[:, h * size : (h + 1) * size] = out.astype(BF16)
            log_ref[:, h : h + 1] = peak + jnp.log(weight)
        projected = jnp.dot(out_ref[...], w_ref[...], preferred_element_type=WIDE)
        projected_ref[...] = projected
        hidden = x_ref[0].astype(WIDE) + unit(projected, g1_ref[...].astype(WIDE))[0]
        hidden_ref[...] = hidden
        inner_ref[...] = unit(hidden, g2_ref[...].astype(WIDE))[0].astype(BF16)

    return vmem_call(
        kernel,
        (
            jax.ShapeDtypeStruct((count, lanes_all), BF16),
            jax.ShapeDtypeStruct((count, heads), WIDE),
            jax.ShapeDtypeStruct((count, width), WIDE),
            jax.ShapeDtypeStruct((count, width), WIDE),
            jax.ShapeDtypeStruct((count, width), BF16),
        ),
        limit=48,
        grid=(1,),
        in_specs=[
            pl.BlockSpec((count, lanes_all), lambda i: (row, 0)),
            full_spec((count, 1)),
            full_spec((count, 1)),
            full_spec((1, keys)),
            full_spec((lanes_all, width)),
            row_spec((count, width), row),
            full_spec((1, width)),
            full_spec((1, width)),
        ]
        + [
            pl.BlockSpec((slots, 1, count, 2 * size), lambda i: (0, row, 0, 0)) for _ in kv_blocks
        ],
        out_specs=(
            full_spec((count, lanes_all)),
            full_spec((count, heads)),
            full_spec((count, width)),
            full_spec((count, width)),
            full_spec((count, width)),
        ),
        scratch_shapes=[pltpu.VMEM((keys, size), BF16), pltpu.VMEM((keys, size), BF16)],
    )(queries, start, place, key_place, out_weight, tokens, gain_out, gain_feed, *kv_blocks)


def close_row(row, parts, hidden, cotangent, gain):
    count, width = hidden.shape

    def kernel(a_ref, b_ref, c_ref, hidden_ref, e_ref, gain_ref, result_ref, d_ref, dg_ref):
        v = a_ref[0].astype(WIDE) + b_ref[...].astype(WIDE) + c_ref[...].astype(WIDE)
        g = gain_ref[...].astype(WIDE)
        z, r = unit(v, g)
        result_ref[...] = (hidden_ref[...] + z).astype(BF16)
        d_values, dg_ref[...] = unit_back(v, r, g, e_ref[0].astype(WIDE))
        d_ref[...] = d_values.astype(BF16)

    return vmem_call(
        kernel,
        (
            jax.ShapeDtypeStruct((count, width), BF16),
            jax.ShapeDtypeStruct((count, width), BF16),
            jax.ShapeDtypeStruct((1, width), WIDE),
        ),
        grid=(1,),
        in_specs=[
            row_spec((count, width), 0),
            full_spec((count, width)),
            full_spec((count, width)),
            full_spec((count, width)),
            row_spec((count, width), row),
            full_spec((1, width)),
        ],
        out_specs=(full_spec((count, width)), full_spec((count, width)), full_spec((1, width))),
    )(*parts, hidden, cotangent, gain)


def attend_backward(
    row,
    parts,
    kept,
    cotangent,
    out_weight,
    gain_out,
    gain_feed,
    queries,
    kv_blocks,
    place,
    key_place,
    raw,
    cosine,
    sine,
    gain,
    heads,
):
    count, width = kept["hidden"].shape
    slots = kv_blocks[0].shape[0]
    size = kv_blocks[0].shape[3] // 2
    half = size // 2
    keys = slots * len(kv_blocks) * count
    lanes_all = heads * size
    block_count = len(kv_blocks)

    def kernel(*refs):
        (
            a_ref,
            b_ref,
            c_ref,
            hidden_ref,
            projected_ref,
            e_ref,
            w_ref,
            g1_ref,
            g2_ref,
            q_ref,
            start_ref,
            place_ref,
            key_place_ref,
            log_ref,
            raw_ref,
            cos_ref,
            sin_ref,
            gain_ref,
        ) = refs[:18]
        kv_refs = refs[18 : 18 + block_count]
        outs = refs[18 + block_count :]
        d_hidden_ref, d_projected_ref, dg1_ref, dg2_ref, dq_ref, dgain_ref = outs[:6]
        dkv_refs = outs[6 : 6 + block_count]
        k_held, v_held, dk_acc, dv_acc, d_held = outs[6 + block_count :]
        g1 = g1_ref[...].astype(WIDE)
        g2 = g2_ref[...].astype(WIDE)
        e = a_ref[0].astype(WIDE) + b_ref[...].astype(WIDE) + c_ref[...].astype(WIDE)
        hidden = hidden_ref[...]
        d_values, dg2_ref[...] = unit_back(hidden, unit(hidden, g2)[1], g2, e)
        d_hidden = e_ref[0].astype(WIDE) + d_values
        d_hidden_ref[...] = d_hidden
        projected = projected_ref[...]
        d_values, dg1_ref[...] = unit_back(projected, unit(projected, g1)[1], g1, d_hidden)
        d_projected_ref[...] = d_values.astype(BF16)
        d_held[...] = lax.dot_general(
            d_projected_ref[...], w_ref[...], NT, preferred_element_type=WIDE
        ).astype(BF16)
        lay_out(kv_refs, k_held, v_held, size)
        allowed = allowed_mask(start_ref, place_ref, key_place_ref)
        gain_values = gain_ref[...].astype(WIDE)
        cos = cos_ref[...]
        sin = sin_ref[...]
        d_gain = jnp.zeros((1, size), WIDE)
        for h in range(heads):
            lanes = slice(h * size, (h + 1) * size)
            q = q_ref[:, lanes]
            d = d_held[:, lanes]
            k = k_held[...]
            scores = lax.dot_general(q, k, NT, preferred_element_type=WIDE) * SCORE_SCALE
            p = jnp.where(allowed, jnp.exp(scores - log_ref[:, h : h + 1]), 0.0)
            d_p = lax.dot_general(d, v_held[...], NT, preferred_element_type=WIDE)
            inner = jnp.sum(p * d_p, axis=-1, keepdims=True)
            d_s = (p * (d_p - inner)).astype(BF16)
            d_v = lax.dot_general(p.astype(BF16), d, TN, preferred_element_type=WIDE)
            d_k = lax.dot_general(d_s, q, TN, preferred_element_type=WIDE)
            if h == 0:
                dk_acc[...] = d_k
                dv_acc[...] = d_v
            else:
                dk_acc[...] += d_k
                dv_acc[...] += d_v
            d_q = jnp.dot(d_s, k, preferred_element_type=WIDE) * SCORE_SCALE
            d_a, d_b = d_q[:, :half], d_q[:, half:]
            turned = jnp.concatenate([d_a * cos + d_b * sin, d_b * cos - d_a * sin], axis=-1)
            u = raw_ref[:, lanes]
            d_u, d_part = unit_back(u, unit(u, gain_values)[1], gain_values, turned)
            dq_ref[:, lanes] = d_u.astype(BF16)
            d_gain += d_part
        dgain_ref[...] = d_gain
        at = 0
        for ref in dkv_refs:
            for slot in range(slots):
                ref[slot, :, :size] = (dk_acc[at : at + count] * SCORE_SCALE).astype(BF16)
                ref[slot, :, size:] = dv_acc[at : at + count].astype(BF16)
                at += count

    wide_rows = jax.ShapeDtypeStruct((count, width), WIDE)
    mine = pl.BlockSpec((count, lanes_all), lambda i: (row, 0))
    turn = pl.BlockSpec((count, half), lambda i: (row, 0))
    outs = vmem_call(
        kernel,
        (
            wide_rows,
            jax.ShapeDtypeStruct((count, width), BF16),
            jax.ShapeDtypeStruct((1, width), WIDE),
            jax.ShapeDtypeStruct((1, width), WIDE),
            jax.ShapeDtypeStruct((count, lanes_all), BF16),
            jax.ShapeDtypeStruct((1, size), WIDE),
        )
        + (jax.ShapeDtypeStruct((slots, count, 2 * size), BF16),) * block_count,
        limit=48,
        grid=(1,),
        in_specs=[
            row_spec((count, width), 0),
            full_spec((count, width)),
            full_spec((count, width)),
            full_spec((count, width)),
            full_spec((count, width)),
            row_spec((count, width), row),
            full_spec((lanes_all, width)),
            full_spec((1, width)),
            full_spec((1, width)),
            mine,
            full_spec((count, 1)),
            full_spec((count, 1)),
            full_spec((1, keys)),
            full_spec((count, heads)),
            mine,
            turn,
            turn,
            full_spec((1, size)),
        ]
        + [
            pl.BlockSpec((slots, 1, count, 2 * size), lambda i: (0, row, 0, 0)) for _ in kv_blocks
        ],
        out_specs=(
            full_spec((count, width)),
            full_spec((count, width)),
            full_spec((1, width)),
            full_spec((1, width)),
            full_spec((count, lanes_all)),
            full_spec((1, size)),
        )
        + (full_spec((slots, count, 2 * size)),) * block_count,
        scratch_shapes=[
            pltpu.VMEM((keys, size), BF16),
            pltpu.VMEM((keys, size), BF16),
            pltpu.VMEM((keys, size), WIDE),
            pltpu.VMEM((keys, size), WIDE),
            pltpu.VMEM((count, lanes_all), BF16),
        ],
    )(
        *parts,
        kept["hidden"],
        kept["projected"],
        cotangent,
        out_weight,
        gain_out,
        gain_feed,
        queries,
        kept["start"],
        place,
        key_place,
        kept["log"],
        raw,
        cosine,
        sine,
        gain,
        *kv_blocks,
    )
    names = ("d_hidden", "d_projected", "grad_out_gain", "grad_feed_gain", "d_query_raw", "d_gain")
    kept.update(zip(names, outs[:6]))
    kept["d_kv"] = outs[6:]


def project_kv(order, normed, blocks, cosine, sine, gain, rows):
    tokens, width = normed.shape
    per_block, part, both = blocks[0].shape
    n = per_block * len(blocks)
    size = both // 2
    half = size // 2

    def kernel(order_ref, x_ref, cos_ref, sin_ref, gain_ref, *refs):
        block_refs = refs[: len(blocks)]
        kv_ref, raw_ref, held = refs[len(blocks) :]
        for d in range(n):
            slot = order_ref[d]
            for k, block in enumerate(block_refs):

                @pl.when((slot >= k * per_block) & (slot < (k + 1) * per_block))
                def _(d=d, k=k, block=block, slot=slot):
                    held[d * part : (d + 1) * part] = block[slot - k * per_block]

        both_raw = jnp.dot(x_ref[...], held[...], preferred_element_type=WIDE)
        u = both_raw[:, :size]
        raw_ref[...] = u
        k = unit(u, gain_ref[...].astype(WIDE))[0]
        cos, sin = cos_ref[...], sin_ref[...]
        a, b = k[:, :half], k[:, half:]
        kv = jnp.concatenate([a * cos - b * sin, b * cos + a * sin, both_raw[:, size:]], axis=-1)
        kv_ref[...] = kv.astype(BF16).reshape(rows, tokens // rows, both)

    return vmem_call(
        kernel,
        (
            jax.ShapeDtypeStruct((rows, tokens // rows, both), BF16),
            jax.ShapeDtypeStruct((tokens, size), WIDE),
            jax.ShapeDtypeStruct((width, both), BF16),
        ),
        in_specs=[smem_spec()] + [whole_spec()] * (4 + len(blocks)),
        out_specs=(whole_spec(), whole_spec(), whole_spec()),
    )(order, normed, cosine, sine, gain, *blocks)


def project_q(normed, weight, cosine, sine, gain, heads):
    tokens, width = normed.shape
    size = weight.shape[1] // heads
    half = size // 2

    def kernel(x_ref, w_ref, cos_ref, sin_ref, gain_ref, q_ref, raw_ref):
        cos, sin = cos_ref[...], sin_ref[...]
        raw_ref[...] = jnp.dot(x_ref[...], w_ref[...], preferred_element_type=WIDE)
        for h in range(heads):
            lanes = slice(h * size, (h + 1) * size)
            q = unit(raw_ref[:, lanes], gain_ref[...].astype(WIDE))[0]
            a, b = q[:, :half], q[:, half:]
            turned = jnp.concatenate([a * cos - b * sin, b * cos + a * sin], axis=-1)
            q_ref[:, lanes] = turned.astype(BF16)

    return vmem_call(
        kernel,
        (
            jax.ShapeDtypeStruct((tokens, heads * size), BF16),
            jax.ShapeDtypeStruct((tokens, heads * size), WIDE),
        ),
        in_specs=[whole_spec()] * 5,
        out_specs=(whole_spec(), whole_spec()),
    )(normed, weight, cosine, sine, gain)


def feed_step(tokens):
    return 256 if tokens % 256 == 0 else tokens


def feed_forward(inner, gate_w, up_w, down_w):
    tokens, width = inner.shape
    share = gate_w.shape[1]
    step = feed_step(tokens)

    def kernel(x_ref, gate_ref, up_ref, down_ref, slope_ref, value_ref, a_ref, low_ref):
        x = x_ref[...]
        g = jnp.dot(x, gate_ref[...], preferred_element_type=WIDE)
        u = jnp.dot(x, up_ref[...], preferred_element_type=WIDE)
        value, slope = gelu_parts(g)
        active = (value * u).astype(BF16)
        slope_ref[...] = (slope * u).astype(BF16)
        value_ref[...] = value.astype(BF16)
        a_ref[...] = active
        low_ref[...] = jnp.dot(active, down_ref[...], preferred_element_type=WIDE).astype(BF16)

    each = lambda columns: pl.BlockSpec((step, columns), lambda i: (i, 0))
    hidden = jax.ShapeDtypeStruct((tokens, share), BF16)
    return vmem_call(
        kernel,
        (hidden, hidden, hidden, jax.ShapeDtypeStruct((tokens, width), BF16)),
        limit=24,
        grid=(tokens // step,),
        in_specs=[each(width), whole_spec(), whole_spec(), whole_spec()],
        out_specs=(each(share), each(share), each(share), each(width)),
    )(inner, gate_w, up_w, down_w)


def feed_backward(d_lowered, slope, value, gate_w, up_w, down_w):
    tokens, width = d_lowered.shape
    share = gate_w.shape[1]
    step = feed_step(tokens)

    def kernel(d_ref, slope_ref, value_ref, gate_ref, up_ref, down_ref, dg_ref, du_ref, dx_ref):
        d_active = lax.dot_general(d_ref[...], down_ref[...], NT, preferred_element_type=WIDE)
        d_gate = (d_active * slope_ref[...].astype(WIDE)).astype(BF16)
        d_up = (d_active * value_ref[...].astype(WIDE)).astype(BF16)
        dg_ref[...] = d_gate
        du_ref[...] = d_up
        d_x = lax.dot_general(d_gate, gate_ref[...], NT, preferred_element_type=WIDE)
        d_x += lax.dot_general(d_up, up_ref[...], NT, preferred_element_type=WIDE)
        dx_ref[...] = d_x.astype(BF16)

    each = lambda columns: pl.BlockSpec((step, columns), lambda i: (i, 0))
    hidden = jax.ShapeDtypeStruct((tokens, share), BF16)
    return vmem_call(
        kernel,
        (hidden, hidden, jax.ShapeDtypeStruct((tokens, width), BF16)),
        limit=24,
        grid=(tokens // step,),
        in_specs=[each(width), each(share), each(share), whole_spec(), whole_spec(), whole_spec()],
        out_specs=(each(share), each(share), each(width)),
    )(d_lowered, slope, value, gate_w, up_w, down_w)


def weight_grad(lefts, rights):
    rows = lefts[0].shape[1]
    columns = rights[0].shape[1]
    count = len(lefts)
    size = 384

    def kernel(*refs):
        out_ref = refs[2 * count]
        for at in range(0, rows, size):
            lanes = slice(at, min(at + size, rows))
            term = None
            for k in range(count):
                part = lax.dot_general(
                    refs[k][:, lanes], refs[count + k][...], TN, preferred_element_type=WIDE
                )
                term = part if term is None else term + part
            out_ref[lanes, :] = term.astype(BF16)

    return vmem_call(
        kernel,
        jax.ShapeDtypeStruct((rows, columns), BF16),
        limit=24,
        in_specs=[whole_spec()] * (2 * count),
        out_specs=whole_spec(),
    )(*lefts, *rights)


def blocks_grad(order, left_sets, right_sets, n):
    rows = left_sets[0].shape[1]
    part = rows // n
    widths = [r.shape[1] for r in right_sets[0]]
    per_row = len(widths)
    count = len(left_sets)
    blocks = n // 4

    def kernel(order_ref, *refs):
        lefts = refs[:count]
        rights = refs[count : count + count * per_row]
        outs = refs[count + count * per_row : -1]
        held = refs[-1]
        for d in range(n):
            lanes = slice(d * part, (d + 1) * part)
            at = 0
            for j, size in enumerate(widths):
                term = None
                for k in range(count):
                    product = lax.dot_general(
                        lefts[k][:, lanes],
                        rights[k * per_row + j][...],
                        TN,
                        preferred_element_type=WIDE,
                    )
                    term = product if term is None else term + product
                held[order_ref[d], :, at : at + size] = term.astype(BF16)
                at += size
        for b, out in enumerate(outs):
            out[...] = held[4 * b : 4 * b + 4]

    flat = [r for rights in right_sets for r in rights]
    shape = jax.ShapeDtypeStruct((4, part, sum(widths)), BF16)
    return vmem_call(
        kernel,
        (shape,) * blocks,
        limit=24,
        in_specs=[smem_spec()] + [whole_spec()] * (count + len(flat)),
        out_specs=(whole_spec(),) * blocks,
        scratch_shapes=[pltpu.VMEM((n, part, sum(widths)), BF16)],
    )(order, *left_sets, *flat)


def close_keys(parts, raw, cosine, sine, gain):
    slots, rows, count, both = parts[0].shape
    size = both // 2
    half = size // 2

    def kernel(a_ref, b_ref, c_ref, raw_ref, cos_ref, sin_ref, gain_ref, *outs):
        gain_values = gain_ref[...].astype(WIDE)
        d_gain = jnp.zeros((1, size), WIDE)
        for row in range(rows):
            span = slice(row * count, (row + 1) * count)
            e = (
                a_ref[0, row].astype(WIDE) + b_ref[row].astype(WIDE) + c_ref[row].astype(WIDE)
            )
            cos, sin = cos_ref[span], sin_ref[span]
            d_a, d_b = e[:, :half], e[:, half:size]
            turned = jnp.concatenate([d_a * cos + d_b * sin, d_b * cos - d_a * sin], axis=-1)
            u = raw_ref[span]
            d_u, d_part = unit_back(u, unit(u, gain_values)[1], gain_values, turned)
            d_gain += d_part
            outs[row][:, :size] = d_u.astype(BF16)
            outs[row][:, size:] = e[:, size:].astype(BF16)
        outs[rows][...] = d_gain

    return vmem_call(
        kernel,
        (jax.ShapeDtypeStruct((count, both), BF16),) * rows
        + (jax.ShapeDtypeStruct((1, size), WIDE),),
        grid=(1,),
        in_specs=[
            pl.BlockSpec((1, rows, count, both), lambda i: (0, 0, 0, 0)),
            full_spec((rows, count, both)),
            full_spec((rows, count, both)),
            full_spec(raw.shape),
            full_spec(cosine.shape),
            full_spec(sine.shape),
            full_spec((1, size)),
        ],
        out_specs=(full_spec((count, both)),) * rows + (full_spec((1, size)),),
    )(*parts, raw, cosine, sine, gain)


def close_tokens(tokens, d_queries, d_kvs, query_w, kv_w, d_hiddens, gain):
    rows, count, width = tokens.shape

    def kernel(x_ref, q_ref, kv_ref, gain_ref, *refs):
        out_ref, dg_ref = refs[3 * rows :]
        g = gain_ref[...].astype(WIDE)
        d_gain = jnp.zeros((1, width), WIDE)
        for row in range(rows):
            d_q, d_kv, d_hidden = refs[row], refs[rows + row], refs[2 * rows + row]
            e = lax.dot_general(d_q[...], q_ref[...], NT, preferred_element_type=WIDE)
            e += lax.dot_general(d_kv[...], kv_ref[...], NT, preferred_element_type=WIDE)
            x = x_ref[row].astype(WIDE)
            d_x, d_part = unit_back(x, unit(x, g)[1], g, e)
            d_gain += d_part
            out_ref[row] = (d_hidden[...] + d_x).astype(BF16)
        dg_ref[...] = d_gain

    return vmem_call(
        kernel,
        (jax.ShapeDtypeStruct(tokens.shape, BF16), jax.ShapeDtypeStruct((1, width), WIDE)),
        in_specs=[whole_spec()] * (4 + 3 * rows),
        out_specs=(whole_spec(), whole_spec()),
    )(tokens, query_w, kv_w, gain, *d_queries, *d_kvs, *d_hiddens)


def per_device(
    tokens,
    cotangent,
    segment_ids,
    query_weight,
    key_weight,
    value_weight,
    out_weight,
    gate_weight,
    up_weight,
    down_weight,
    gain_input,
    gain_query,
    gain_key,
    gain_attended,
    gain_feed,
    gain_result,
):
    n = lax.axis_size("ctx")
    n_dp = lax.axis_size("dp")
    me = lax.axis_index("ctx")
    my_dp = lax.axis_index("dp")
    row_count, count_local, width = tokens.shape
    total = row_count * count_local
    head_width = gain_query.shape[0]
    head_count = query_weight.shape[1] // head_width
    qw = head_count * head_width
    share = gate_weight.shape[1] // n
    span = count_local // 2
    codes = xor_layout(n)[3]
    kv_weights = Gather(jnp.concatenate([key_weight, value_weight], axis=1), n)
    query_full = lax.all_gather(query_weight, "ctx", axis=0, tiled=True)
    even_flag = ((my_dp % 2) == 0).astype(jnp.int32).reshape(1)
    below = jnp.stack(
        [jnp.sum((segment_ids < s).astype(jnp.int32), axis=1) for s in range(5)], axis=1
    )
    code = 1
    while code < n:
        below = below + xor_permute(below, n, code)
        code *= 2
    starts = sum(jnp.where(segment_ids == s, below[:, s : s + 1], 0) for s in range(5))
    start_columns = [starts[row].reshape(-1, 1) for row in range(row_count)]
    kv_weights.mid()
    pieces = spread_pieces(
        even_flag, after(gate_weight, kv_weights.a, kv_weights.b, starts), up_weight, n
    )
    spread = lax.all_to_all(pieces, "ctx", 0, 0)
    kv_weights.near(pieces)
    gain_row = {
        "input": after(gain_input, pieces).reshape(1, -1),
        "query": after(gain_query, pieces).reshape(1, -1),
        "key": after(gain_key, pieces).reshape(1, -1),
        "out": after(gain_attended, pieces).reshape(1, -1),
        "feed": after(gain_feed, pieces).reshape(1, -1),
        "result": after(gain_result, pieces).reshape(1, -1),
    }

    offsets = jnp.arange(span, dtype=jnp.int32)

    def places_of(device):
        return jnp.concatenate([device * span + offsets, (2 * n - 1 - device) * span + offsets])

    local_places = places_of(me)
    key_places = jnp.concatenate([places_of(me ^ code) for code in codes]).reshape(1, -1)
    place_column = local_places.reshape(-1, 1)
    angles = angles_for(local_places.astype(WIDE), head_width)
    cosine = jnp.concatenate([jnp.cos(angles)] * row_count, axis=0)
    sine = jnp.concatenate([jnp.sin(angles)] * row_count, axis=0)

    normed_rows = rms_norm(tokens.astype(WIDE), gain_input.astype(WIDE)).astype(BF16)
    normed = normed_rows.reshape(total, width)
    order_codes = me ^ jnp.arange(n, dtype=jnp.int32)
    order = sum(jnp.where(order_codes == c, k, 0) for k, c in enumerate(codes)).astype(jnp.int32)
    kv_local, key_raw, kv_full = project_kv(
        order, normed, kv_weights.blocks, cosine, sine, gain_row["key"], row_count
    )
    kv_gather = Gather(kv_local, n)
    out_full = lax.all_gather(after(out_weight, kv_local), "ctx", axis=0, tiled=True)
    queries, query_raw = project_q(
        after(normed, kv_local), query_full, cosine, sine, gain_row["query"], head_count
    )
    kv_gather.mid(spread, *start_columns, *gain_row.values(), key_places, place_column)
    swapped = lax.ppermute(
        after(spread, kv_gather.a, kv_gather.b), "dp", [(i, i ^ 1) for i in range(n_dp)]
    )
    kv_gather.near(queries)
    kv_blocks = kv_gather.blocks

    def before_feed(row, *earlier):
        r = {"start": start_columns[row]}
        names = ("attended", "log", "projected", "hidden", "inner_local")
        outs = attend_forward(
            row,
            after(queries, *earlier),
            kv_blocks,
            r["start"],
            place_column,
            key_places,
            out_full,
            tokens,
            gain_row["out"],
            gain_row["feed"],
            head_count,
        )
        r.update(zip(names, outs))
        return r

    def feed_piece(r, block, *earlier):
        outs = feed_forward(after(block, *earlier), gate_mine, up_mine, down_weight)
        for name, out in zip(("inner", "slope", "value", "active"), (block,) + tuple(outs[:3])):
            r.setdefault(name, []).append(out)
        return outs[3].reshape(4, count_local, width)

    def back_piece(r, block, *earlier):
        k = len(r.setdefault("d_lowered", []))
        outs = feed_backward(
            after(block, *earlier), r["slope"][k], r["value"][k], gate_mine, up_mine, down_weight
        )
        for name, out in zip(("d_lowered", "d_gate", "d_up"), (block,) + tuple(outs[:2])):
            r.setdefault(name, []).append(out)
        return outs[2].reshape(4, count_local, width)

    def pieces_of(piece, r, blocks, *earlier):
        outs = []
        for block in blocks:
            outs.append(piece(r, block, *earlier, *outs[-1:]))
        return outs

    def result_piece(row, r, parts):
        r["result"], d_lowered, r["grad_result_gain"] = close_row(
            row, parts, r["hidden"], cotangent, gain_row["result"]
        )
        return d_lowered

    def attend_back(row, r, parts):
        attend_backward(
            row,
            parts,
            r,
            cotangent,
            out_full,
            gain_row["out"],
            gain_row["feed"],
            queries,
            kv_blocks,
            place_column,
            key_places,
            query_raw,
            cosine,
            sine,
            gain_row["query"],
            head_count,
        )

    r0 = before_feed(0)
    g0 = Gather(r0["inner_local"], n)
    r1 = before_feed(1, r0["inner_local"])
    g0.mid(r1["inner_local"])
    g1 = Gather(after(r1["inner_local"], g0.a, g0.b), n)
    gate_mine, up_mine = in_order(even_flag, spread, swapped)
    gate_mine = gate_mine.reshape(width, share)
    up_mine = up_mine.reshape(width, share)
    g0.near(gate_mine, g1.a, g1.b)
    g1.mid(g0.blocks[0])
    blocks_0 = g0.flat()
    low_0 = [feed_piece(r0, blocks_0[0])]
    low_0 += pieces_of(feed_piece, r0, blocks_0[1:], low_0[0])
    s0 = Scatter(low_0, n)
    g1.near(low_0[-1])
    blocks_1 = g1.flat()
    low_1 = [feed_piece(r1, blocks_1[0])]
    s0.mid(low_1[0])
    low_1 += pieces_of(feed_piece, r1, blocks_1[1:], low_1[0], s0.sums)
    s1 = Scatter(low_1, n)
    s0.far(low_1[-1])
    s1.mid(*s0.sent)
    d_low_0 = result_piece(0, r0, s0.finish(s1.sums))
    h0 = Gather(d_low_0, n)
    s1.far(d_low_0)
    h0.mid(*s1.sent)
    d_low_1 = result_piece(1, r1, s1.finish(h0.a))
    h1 = Gather(d_low_1, n)
    h0.near(d_low_1)
    blocks_0 = h0.flat()
    d_in_0 = [back_piece(r0, blocks_0[0])]
    h1.mid(d_in_0[0])
    d_in_0 += pieces_of(back_piece, r0, blocks_0[1:], d_in_0[0], h1.a, h1.b)
    s0 = Scatter(d_in_0, n)
    h1.near(d_in_0[-1])
    blocks_1 = h1.flat()
    d_in_1 = [back_piece(r1, blocks_1[0])]
    s0.mid(d_in_1[0])
    rows = (r0, r1)

    def over_rows(left, right, *earlier):
        lefts, rights = r0[left] + r1[left], r0[right] + r1[right]
        return weight_grad([after(lefts[0], *earlier)] + lefts[1:], rights)

    def begin(part, *earlier):
        line = Line(after(part, *earlier), n_dp)
        clock[:] = [line.total]
        return line

    def land(line):
        line.moved = after(line.moved, *clock)
        clock[:] = [line.moved]

    def step(line, *earlier):
        if line.at < len(line.steps) - 1:
            line.step(*clock, *earlier)
            clock[:] = [line.total]

    def halves(x):
        half = x.shape[0] // 2
        return [x[:half], x[half:]]

    def exchange(grad):
        return lax.all_to_all(grad.reshape(n, width // n, share), "ctx", 0, 0)

    clock = []
    grad_down = weight_grad(
        [after(r0["active"][0], s0.sums)] + r0["active"][1:] + r1["active"],
        r0["d_lowered"] + blocks_1,
    )
    down_line = begin(grad_down)
    d_in_1 += pieces_of(back_piece, r1, blocks_1[1:], d_in_1[0], grad_down)
    s1 = Scatter(d_in_1, n)
    s0.far(d_in_1[-1])
    grad_gate = over_rows("inner", "d_gate", *s0.sent)
    gate_pieces = exchange(grad_gate)
    s1.mid(grad_gate)
    attend_back(0, r0, s0.finish(s1.sums))
    clock[:] = [r0["d_kv"][0]]
    step(down_line)
    s1.far(*clock)
    grad_up = over_rows("inner", "d_up", *s1.sent)
    up_pieces = exchange(grad_up)
    gate_halves = halves(gate_pieces)
    gl0 = begin(gate_halves[0], grad_up)
    attend_back(1, r1, s1.finish(*clock))
    clock[:] = [r1["d_kv"][0]]
    step(down_line)
    gl1 = begin(gate_halves[1], *clock)
    step(gl0)
    kv_scatter = Scatter(
        [jnp.stack([a, b], axis=1) for a, b in zip(r0["d_kv"], r1["d_kv"])], n
    )
    clock[:] = [gl0.total, *kv_scatter.blocks[-1:]]
    grad_out = (
        t_dot(after(r0["attended"], *clock), r0["d_projected"])
        + t_dot(r1["attended"], r1["d_projected"])
    ).astype(BF16)
    part_out = lax.psum_scatter(grad_out, "ctx", scatter_dimension=0, tiled=True)
    def total_of(parts):
        return (
            parts[0][0].astype(WIDE) + parts[1].astype(WIDE) + parts[2].astype(WIDE)
        ).astype(BF16)

    def last(line):
        line.moved = after(line.moved, *clock)
        total = line.finish().astype(WIDE)
        clock[:] = [total]
        return total

    def side_by_side(lines):
        ends = lines[0].steps[-1][2]
        mine = (my_dp == ends[0]) | (my_dp == ends[1]) if ends else my_dp < 0
        total = assemble(
            mine.astype(jnp.int32).reshape(1),
            [line.total for line in lines],
            [after(line.moved, *clock) for line in lines],
            width // n,
            n * share,
        )
        clock[:] = [total]
        return total

    kv_scatter.mid(grad_out)
    up_halves = halves(up_pieces)
    u0 = begin(up_halves[0], kv_scatter.sums)
    kv_scatter.far(*clock)
    clock[:] = [*kv_scatter.sent]
    step(gl1)
    *d_kvs, grad_key_gain = close_keys(
        kv_scatter.finish(*clock), key_raw, cosine, sine, gain_row["key"]
    )
    clock[:] = [d_kvs[0]]
    step(gl0)
    land(down_line)
    step(u0)
    step(gl1)
    u1 = begin(up_halves[1], *clock)
    grad_qkv = blocks_grad(
        order,
        [
            after(normed[row * count_local : (row + 1) * count_local], *clock)
            for row in range(row_count)
        ],
        [[r["d_query_raw"], d_kv] for r, d_kv in zip(rows, d_kvs)],
        n,
    )
    qkv_scatter = Scatter(grad_qkv, n)
    qkv_scatter.mid(grad_qkv[0])
    tokens_grad, grad_input_gain = close_tokens(
        tokens,
        [after(r["d_query_raw"], qkv_scatter.sums) for r in rows],
        d_kvs,
        query_full,
        kv_full,
        [r["d_hidden"] for r in rows],
        gain_row["input"],
    )
    qkv_scatter.far(tokens_grad)
    gains = jnp.concatenate(
        [
            grad_input_gain,
            sum(r["d_gain"] for r in rows),
            grad_key_gain,
            sum(r["grad_out_gain"] for r in rows),
            sum(r["grad_feed_gain"] for r in rows),
            sum(r["grad_result_gain"] for r in rows),
        ],
        axis=1,
    ).reshape(-1, 128)
    clock[:] = [*qkv_scatter.sent]
    gains = after(gains, *clock)
    land(gl0)
    step(u1)
    step(u0)
    summed_down = last(down_line)
    result = after(jnp.stack([r["result"] for r in rows]), *clock)
    clock[:] = [summed_down, result]
    part_qkv = total_of(qkv_scatter.finish(*clock))
    clock[:] = [part_qkv]
    qkv_line = begin(part_qkv, *clock)
    land(gl1)
    out_line = begin(part_out, *clock)
    code = 1
    while code < n:
        gains = gains + xor_permute(gains, n, code)
        code *= 2
    step(qkv_line)
    step(u1)
    land(u0)
    step(out_line)
    gain_line = begin(gains, *clock)
    step(qkv_line)
    step(gain_line)
    step(out_line)
    for _ in range(n_dp):
        for line in (gl0, gl1, u0, u1, qkv_line, out_line, gain_line):
            step(line)
    summed_gate = side_by_side([gl0, gl1])
    summed_up = side_by_side([u0, u1])
    summed_out = last(out_line)
    summed_qkv = last(qkv_line)
    gains = last(gain_line).reshape(-1)
    sizes = [width, head_width, head_width, width, width, width]
    gain_grads = []
    start = 0
    for size in sizes:
        gain_grads.append(gains[start : start + size])
        start += size
    return (
        result,
        tokens_grad,
        summed_qkv[:, :qw],
        summed_qkv[:, qw : qw + head_width],
        summed_qkv[:, qw + head_width :],
        summed_out,
        summed_gate,
        summed_up,
        summed_down,
        *gain_grads,
    )


def solution(mesh):
    return jax.shard_map(
        per_device,
        mesh=mesh,
        in_specs=(
            P("dp", "ctx", None),
            P("dp", "ctx", None),
            P("dp", "ctx"),
            P("ctx", None),
            P("ctx", None),
            P("ctx", None),
            P("ctx", None),
            P("ctx", None),
            P("ctx", None),
            P("ctx", None),
            P(),
            P(),
            P(),
            P(),
            P(),
            P(),
        ),
        out_specs=(
            P("dp", "ctx", None),
            P("dp", "ctx", None),
            P("ctx", None),
            P("ctx", None),
            P("ctx", None),
            P("ctx", None),
            P("ctx", None),
            P("ctx", None),
            P("ctx", None),
            P(),
            P(),
            P(),
            P(),
            P(),
            P(),
        ),
        check_vma=False,
    )
```

```python
import jax
import jax.numpy as jnp
from jax import lax
from jax.experimental import pallas as pl
from jax.experimental.pallas import tpu as pltpu
from jax.sharding import PartitionSpec as P

EPSILON = 1e-06
ROPE_BASE = 1000000.0
SCORE_SCALE = 0.0625
NEGATIVE = -1e30
GELU_COEFF = 0.044715
ROOT_TWO_PI = 0.7978845608028654
BF16 = jnp.bfloat16
WIDE = jnp.float32


def rms_norm(values, gain_values):
    return (
        values
        * lax.rsqrt(jnp.mean(values * values, axis=-1, keepdims=True) + EPSILON)
        * gain_values
    )


def angles_for(positions, width):
    half_width = width // 2
    frequencies = jnp.power(ROPE_BASE, -jnp.arange(half_width, dtype=jnp.float32) / half_width)
    return positions[:, None] * frequencies[None, :]


def gelu_parts(gate):
    square = gate * gate
    bent = jnp.tanh(ROOT_TWO_PI * (gate + GELU_COEFF * gate * square))
    rise = 0.5 * (1.0 + bent)
    slope = rise + 0.5 * gate * (1.0 - bent * bent) * ROOT_TWO_PI * (
        1.0 + 3.0 * GELU_COEFF * square
    )
    return gate * rise, slope


def dot(left, right):
    return jnp.dot(left, right, preferred_element_type=WIDE)


def dot_t(left, right):
    return lax.dot_general(left, right, (((1,), (1,)), ((), ())), preferred_element_type=WIDE)


def t_dot(left, right):
    return lax.dot_general(left, right, (((0,), (0,)), ((), ())), preferred_element_type=WIDE)


def after(x, *earlier):
    return lax.optimization_barrier((x,) + earlier)[0] if earlier else x


def together(xs, *earlier):
    return lax.optimization_barrier(tuple(xs) + earlier)[: len(xs)]


def xor_permute(x, axis_size, code):
    return lax.ppermute(x, "ctx", [(i, i ^ code) for i in range(axis_size)])


def xor_layout(n):
    far_y, far_x = n // 2, n // 4
    near = [1 << b for b in range((n // 4).bit_length() - 1)]
    codes = [0, far_x, far_y, far_x ^ far_y]
    for bit in near:
        codes = codes + [c ^ bit for c in codes]
    return far_x, far_y, near, codes


class Gather:
    def __init__(self, x, n):
        self.n = n
        self.far_x, self.far_y, self.near_bits, _ = xor_layout(n)
        self.x = x
        self.a = xor_permute(x, n, self.far_x)
        self.b = xor_permute(x, n, self.far_y)

    def mid(self, *earlier):
        half = self.x.shape[0] // 2
        a, b = together((self.a, self.b), *earlier)
        self.d1 = xor_permute(a[:half], self.n, self.far_y)
        self.d2 = xor_permute(b[half:], self.n, self.far_x)
        return self

    def near(self, *earlier):
        d1, d2 = together((self.d1, self.d2), *earlier)
        self.blocks = [stack_blocks(self.x, self.a, self.b, d1, d2)]
        for bit in self.near_bits:
            self.blocks = self.blocks + [xor_permute(b, self.n, bit) for b in self.blocks]
        return self

    def flat(self):
        return [b.reshape((4 * self.x.shape[0],) + self.x.shape[1:]) for b in self.blocks]


class Scatter:
    def __init__(self, blocks, n):
        self.n = n
        self.far_x, self.far_y, self.near_bits, _ = xor_layout(n)
        self.blocks = list(blocks)
        self.bits = list(reversed(self.near_bits))
        self.send_near()

    def send_near(self):
        if self.bits:
            count = len(self.blocks) // 2
            self.arrived = [xor_permute(b, self.n, self.bits[0]) for b in self.blocks[count:]]

    def mid(self, *earlier):
        while self.bits:
            count = len(self.blocks) // 2
            self.arrived[0] = after(self.arrived[0], *earlier)
            self.blocks = [
                (mine.astype(WIDE) + theirs.astype(WIDE)).astype(BF16)
                for mine, theirs in zip(self.blocks[:count], self.arrived)
            ]
            self.bits = self.bits[1:]
            self.send_near()
        self.sums = self.blocks[0]
        half = self.sums.shape[1] // 2
        self.d_x = xor_permute(self.sums[3, :half], self.n, self.far_x)
        self.d_y = xor_permute(self.sums[3, half:], self.n, self.far_y)
        return self

    def far(self, *earlier):
        half = self.sums.shape[1] // 2
        d_x, d_y = together((self.d_x, self.d_y), *earlier)
        d_x, d_y = d_x.astype(WIDE), d_y.astype(WIDE)
        x, y = self.sums[1].astype(WIDE), self.sums[2].astype(WIDE)
        to_x = jnp.concatenate([x[:half], x[half:] + d_y], axis=0).astype(BF16)
        to_y = jnp.concatenate([y[:half] + d_x, y[half:]], axis=0).astype(BF16)
        self.from_x = xor_permute(to_x, self.n, self.far_x)
        self.from_y = xor_permute(to_y, self.n, self.far_y)
        self.sent = (to_x, to_y)
        return self

    def finish(self, *earlier):
        return self.sums, *together((self.from_x, self.from_y), *earlier)


class Line:
    def __init__(self, part, n):
        self.n = n
        self.total = part
        mid = n // 2
        self.steps = []
        for s in range(mid - 1):
            self.steps.append(("in", [(s, s + 1), (n - 1 - s, n - 2 - s)], None))
        self.steps.append(("in", [(mid - 1, mid), (mid, mid - 1)], None))
        for s in range(mid - 2, -1, -1):
            self.steps.append(("out", [(s + 1, s), (n - 2 - s, n - 1 - s)], (s, n - 1 - s)))
        self.at = 0
        self.send()

    def send(self):
        if self.at < len(self.steps):
            self.moved = lax.ppermute(self.total, "dp", self.steps[self.at][1])

    def step(self, *earlier):
        kind, _, ends = self.steps[self.at]
        moved = after(self.moved, *earlier)
        if kind == "in":
            total = self.total.astype(WIDE) + moved.astype(WIDE)
            self.total = total.astype(self.total.dtype)
        else:
            me = lax.axis_index("dp")
            self.total = jnp.where((me == ends[0]) | (me == ends[1]), moved, self.total)
        self.at += 1
        self.send()
        return self.total

    def finish(self):
        while self.at < len(self.steps):
            self.step()
        return self.total


NT = (((1,), (1,)), ((), ()))
TN = (((0,), (0,)), ((), ()))
MIB = 1024 * 1024


def vmem_call(kernel, out_shape, limit=32, **kwargs):
    return pl.pallas_call(
        kernel,
        out_shape=out_shape,
        compiler_params=pltpu.CompilerParams(vmem_limit_bytes=limit * MIB),
        cost_estimate=pl.CostEstimate(flops=0, bytes_accessed=0, transcendentals=0),
        **kwargs,
    )


def whole_spec():
    return pl.BlockSpec(memory_space=pltpu.VMEM)


def smem_spec():
    return pl.BlockSpec(memory_space=pltpu.SMEM)


def full_spec(shape):
    return pl.BlockSpec(shape, lambda i: (0,) * len(shape))


def row_spec(shape, row):
    return pl.BlockSpec((1,) + shape, lambda i: (row,) + (0,) * len(shape))


def unit(values, gain_values):
    r = lax.rsqrt(jnp.mean(values * values, axis=-1, keepdims=True) + EPSILON)
    return values * r * gain_values, r


def unit_back(values, r, gain_values, e):
    ge = gain_values * e
    d_values = r * ge - values * (r * r * r * jnp.mean(ge * values, axis=-1, keepdims=True))
    return d_values, jnp.sum(e * values * r, axis=0, keepdims=True)


def stack_blocks(x, a, b, d1, d2):
    half = d1.shape[0]

    def kernel(x_ref, a_ref, b_ref, d1_ref, d2_ref, out_ref):
        out_ref[0] = x_ref[...]
        out_ref[1] = a_ref[...]
        out_ref[2] = b_ref[...]
        out_ref[3, :half] = d1_ref[...]
        out_ref[3, half:] = d2_ref[...]

    return vmem_call(
        kernel,
        jax.ShapeDtypeStruct((4,) + x.shape, x.dtype),
        in_specs=[whole_spec()] * 5,
        out_specs=whole_spec(),
    )(x, a, b, d1, d2)


def spread_pieces(flag, first, second, n):
    rows, columns = first.shape
    share = columns // n

    def kernel(flag_ref, first_ref, second_ref, out_ref):
        def fill(source):
            for k in range(n):
                out_ref[k] = source[:, k * share : (k + 1) * share]

        @pl.when(flag_ref[0] == 1)
        def _():
            fill(first_ref)

        @pl.when(flag_ref[0] != 1)
        def _():
            fill(second_ref)

    return vmem_call(
        kernel,
        jax.ShapeDtypeStruct((n, rows, share), first.dtype),
        in_specs=[smem_spec(), whole_spec(), whole_spec()],
        out_specs=whole_spec(),
    )(flag, first, second)


def in_order(flag, first, second):
    def kernel(flag_ref, first_ref, second_ref, a_ref, b_ref):
        @pl.when(flag_ref[0] == 1)
        def _():
            a_ref[...] = first_ref[...]
            b_ref[...] = second_ref[...]

        @pl.when(flag_ref[0] != 1)
        def _():
            a_ref[...] = second_ref[...]
            b_ref[...] = first_ref[...]

    parts, rows, columns = first.shape
    step = pl.BlockSpec((1, rows, columns), lambda i: (i, 0, 0))
    return vmem_call(
        kernel,
        (jax.ShapeDtypeStruct(first.shape, first.dtype),) * 2,
        grid=(parts,),
        in_specs=[smem_spec(), step, step],
        out_specs=(step, step),
    )(flag, first, second)


def assemble(flag, totals, moveds, rows, columns):
    count = len(totals)
    share = totals[0].shape[2]
    moveds = moveds or []

    def kernel(flag_ref, *refs):
        out_ref = refs[-1]

        def fill(parts):
            at = 0
            for part in parts:
                for k in range(part.shape[0]):
                    out_ref[:, at * share : (at + 1) * share] = part[k].astype(WIDE)
                    at += 1

        if not moveds:
            fill(refs[:count])
            return

        @pl.when(flag_ref[0] == 1)
        def _():
            fill(refs[count : 2 * count])

        @pl.when(flag_ref[0] != 1)
        def _():
            fill(refs[:count])

    return vmem_call(
        kernel,
        jax.ShapeDtypeStruct((rows, columns), WIDE),
        in_specs=[smem_spec()] + [whole_spec()] * (count + len(moveds)),
        out_specs=whole_spec(),
    )(flag, *totals, *moveds)


def allowed_mask(start_ref, place_ref, key_place_ref):
    key_place = key_place_ref[...]
    return (start_ref[...] <= key_place) & (place_ref[...] >= key_place)


def lay_out(kv_refs, k_held, v_held, size):
    at = 0
    for ref in kv_refs:
        for slot in range(ref.shape[0]):
            tokens = ref.shape[2]
            k_held[at : at + tokens] = ref[slot, 0, :, :size]
            v_held[at : at + tokens] = ref[slot, 0, :, size:]
            at += tokens


def attend_forward(
    row, queries, kv_blocks, start, place, key_place, out_weight, tokens, gain_out, gain_feed, heads
):
    count = start.shape[0]
    width = tokens.shape[2]
    slots = kv_blocks[0].shape[0]
    size = kv_blocks[0].shape[3] // 2
    keys = slots * len(kv_blocks) * count
    lanes_all = heads * size

    def kernel(*refs):
        q_ref, start_ref, place_ref, key_place_ref, w_ref, x_ref, g1_ref, g2_ref = refs[:8]
        kv_refs = refs[8 : 8 + len(kv_blocks)]
        out_ref, log_ref, projected_ref, hidden_ref, inner_ref, k_held, v_held = refs[
            8 + len(kv_blocks) :
        ]
        lay_out(kv_refs, k_held, v_held, size)
        allowed = allowed_mask(start_ref, place_ref, key_place_ref)
        for h in range(heads):
            q = q_ref[:, h * size : (h + 1) * size]
            scores = lax.dot_general(q, k_held[...], NT, preferred_element_type=WIDE) * SCORE_SCALE
            scores = jnp.where(allowed, scores, NEGATIVE)
            peak = jnp.max(scores, axis=-1, keepdims=True)
            raised = jnp.exp(scores - peak)
            weight = jnp.sum(raised, axis=-1, keepdims=True)
            probabilities = (raised * (1.0 / weight)).astype(BF16)
            out = jnp.dot(probabilities, v_held[...], preferred_element_type=WIDE)
            out_ref[:, h * size : (h + 1) * size] = out.astype(BF16)
            log_ref[:, h : h + 1] = peak + jnp.log(weight)
        projected = jnp.dot(out_ref[...], w_ref[...], preferred_element_type=WIDE)
        projected_ref[...] = projected
        hidden = x_ref[0].astype(WIDE) + unit(projected, g1_ref[...].astype(WIDE))[0]
        hidden_ref[...] = hidden
        inner_ref[...] = unit(hidden, g2_ref[...].astype(WIDE))[0].astype(BF16)

    return vmem_call(
        kernel,
        (
            jax.ShapeDtypeStruct((count, lanes_all), BF16),
            jax.ShapeDtypeStruct((count, heads), WIDE),
            jax.ShapeDtypeStruct((count, width), WIDE),
            jax.ShapeDtypeStruct((count, width), WIDE),
            jax.ShapeDtypeStruct((count, width), BF16),
        ),
        limit=48,
        grid=(1,),
        in_specs=[
            pl.BlockSpec((count, lanes_all), lambda i: (row, 0)),
            full_spec((count, 1)),
            full_spec((count, 1)),
            full_spec((1, keys)),
            full_spec((lanes_all, width)),
            row_spec((count, width), row),
            full_spec((1, width)),
            full_spec((1, width)),
        ]
        + [
            pl.BlockSpec((slots, 1, count, 2 * size), lambda i: (0, row, 0, 0)) for _ in kv_blocks
        ],
        out_specs=(
            full_spec((count, lanes_all)),
            full_spec((count, heads)),
            full_spec((count, width)),
            full_spec((count, width)),
            full_spec((count, width)),
        ),
        scratch_shapes=[pltpu.VMEM((keys, size), BF16), pltpu.VMEM((keys, size), BF16)],
    )(queries, start, place, key_place, out_weight, tokens, gain_out, gain_feed, *kv_blocks)


def close_row(row, parts, hidden, cotangent, gain):
    count, width = hidden.shape

    def kernel(a_ref, b_ref, c_ref, hidden_ref, e_ref, gain_ref, result_ref, d_ref, dg_ref):
        v = a_ref[0].astype(WIDE) + b_ref[...].astype(WIDE) + c_ref[...].astype(WIDE)
        g = gain_ref[...].astype(WIDE)
        z, r = unit(v, g)
        result_ref[...] = (hidden_ref[...] + z).astype(BF16)
        d_values, dg_ref[...] = unit_back(v, r, g, e_ref[0].astype(WIDE))
        d_ref[...] = d_values.astype(BF16)

    return vmem_call(
        kernel,
        (
            jax.ShapeDtypeStruct((count, width), BF16),
            jax.ShapeDtypeStruct((count, width), BF16),
            jax.ShapeDtypeStruct((1, width), WIDE),
        ),
        grid=(1,),
        in_specs=[
            row_spec((count, width), 0),
            full_spec((count, width)),
            full_spec((count, width)),
            full_spec((count, width)),
            row_spec((count, width), row),
            full_spec((1, width)),
        ],
        out_specs=(full_spec((count, width)), full_spec((count, width)), full_spec((1, width))),
    )(*parts, hidden, cotangent, gain)


def attend_backward(
    row,
    parts,
    kept,
    cotangent,
    out_weight,
    gain_out,
    gain_feed,
    queries,
    kv_blocks,
    place,
    key_place,
    raw,
    cosine,
    sine,
    gain,
    heads,
):
    count, width = kept["hidden"].shape
    slots = kv_blocks[0].shape[0]
    size = kv_blocks[0].shape[3] // 2
    half = size // 2
    keys = slots * len(kv_blocks) * count
    lanes_all = heads * size
    block_count = len(kv_blocks)

    def kernel(*refs):
        (
            a_ref,
            b_ref,
            c_ref,
            hidden_ref,
            projected_ref,
            e_ref,
            w_ref,
            g1_ref,
            g2_ref,
            q_ref,
            start_ref,
            place_ref,
            key_place_ref,
            log_ref,
            raw_ref,
            cos_ref,
            sin_ref,
            gain_ref,
        ) = refs[:18]
        kv_refs = refs[18 : 18 + block_count]
        outs = refs[18 + block_count :]
        d_hidden_ref, d_projected_ref, dg1_ref, dg2_ref, dq_ref, dgain_ref = outs[:6]
        dkv_refs = outs[6 : 6 + block_count]
        k_held, v_held, dk_acc, dv_acc, d_held = outs[6 + block_count :]
        g1 = g1_ref[...].astype(WIDE)
        g2 = g2_ref[...].astype(WIDE)
        e = a_ref[0].astype(WIDE) + b_ref[...].astype(WIDE) + c_ref[...].astype(WIDE)
        hidden = hidden_ref[...]
        d_values, dg2_ref[...] = unit_back(hidden, unit(hidden, g2)[1], g2, e)
        d_hidden = e_ref[0].astype(WIDE) + d_values
        d_hidden_ref[...] = d_hidden
        projected = projected_ref[...]
        d_values, dg1_ref[...] = unit_back(projected, unit(projected, g1)[1], g1, d_hidden)
        d_projected_ref[...] = d_values.astype(BF16)
        d_held[...] = lax.dot_general(
            d_projected_ref[...], w_ref[...], NT, preferred_element_type=WIDE
        ).astype(BF16)
        lay_out(kv_refs, k_held, v_held, size)
        allowed = allowed_mask(start_ref, place_ref, key_place_ref)
        gain_values = gain_ref[...].astype(WIDE)
        cos = cos_ref[...]
        sin = sin_ref[...]
        d_gain = jnp.zeros((1, size), WIDE)
        for h in range(heads):
            lanes = slice(h * size, (h + 1) * size)
            q = q_ref[:, lanes]
            d = d_held[:, lanes]
            k = k_held[...]
            scores = lax.dot_general(q, k, NT, preferred_element_type=WIDE) * SCORE_SCALE
            p = jnp.where(allowed, jnp.exp(scores - log_ref[:, h : h + 1]), 0.0)
            d_p = lax.dot_general(d, v_held[...], NT, preferred_element_type=WIDE)
            inner = jnp.sum(p * d_p, axis=-1, keepdims=True)
            d_s = (p * (d_p - inner)).astype(BF16)
            d_v = lax.dot_general(p.astype(BF16), d, TN, preferred_element_type=WIDE)
            d_k = lax.dot_general(d_s, q, TN, preferred_element_type=WIDE)
            if h == 0:
                dk_acc[...] = d_k
                dv_acc[...] = d_v
            else:
                dk_acc[...] += d_k
                dv_acc[...] += d_v
            d_q = jnp.dot(d_s, k, preferred_element_type=WIDE) * SCORE_SCALE
            d_a, d_b = d_q[:, :half], d_q[:, half:]
            turned = jnp.concatenate([d_a * cos + d_b * sin, d_b * cos - d_a * sin], axis=-1)
            u = raw_ref[:, lanes]
            d_u, d_part = unit_back(u, unit(u, gain_values)[1], gain_values, turned)
            dq_ref[:, lanes] = d_u.astype(BF16)
            d_gain += d_part
        dgain_ref[...] = d_gain
        at = 0
        for ref in dkv_refs:
            for slot in range(slots):
                ref[slot, :, :size] = (dk_acc[at : at + count] * SCORE_SCALE).astype(BF16)
                ref[slot, :, size:] = dv_acc[at : at + count].astype(BF16)
                at += count

    wide_rows = jax.ShapeDtypeStruct((count, width), WIDE)
    mine = pl.BlockSpec((count, lanes_all), lambda i: (row, 0))
    turn = pl.BlockSpec((count, half), lambda i: (row, 0))
    outs = vmem_call(
        kernel,
        (
            wide_rows,
            jax.ShapeDtypeStruct((count, width), BF16),
            jax.ShapeDtypeStruct((1, width), WIDE),
            jax.ShapeDtypeStruct((1, width), WIDE),
            jax.ShapeDtypeStruct((count, lanes_all), BF16),
            jax.ShapeDtypeStruct((1, size), WIDE),
        )
        + (jax.ShapeDtypeStruct((slots, count, 2 * size), BF16),) * block_count,
        limit=48,
        grid=(1,),
        in_specs=[
            row_spec((count, width), 0),
            full_spec((count, width)),
            full_spec((count, width)),
            full_spec((count, width)),
            full_spec((count, width)),
            row_spec((count, width), row),
            full_spec((lanes_all, width)),
            full_spec((1, width)),
            full_spec((1, width)),
            mine,
            full_spec((count, 1)),
            full_spec((count, 1)),
            full_spec((1, keys)),
            full_spec((count, heads)),
            mine,
            turn,
            turn,
            full_spec((1, size)),
        ]
        + [
            pl.BlockSpec((slots, 1, count, 2 * size), lambda i: (0, row, 0, 0)) for _ in kv_blocks
        ],
        out_specs=(
            full_spec((count, width)),
            full_spec((count, width)),
            full_spec((1, width)),
            full_spec((1, width)),
            full_spec((count, lanes_all)),
            full_spec((1, size)),
        )
        + (full_spec((slots, count, 2 * size)),) * block_count,
        scratch_shapes=[
            pltpu.VMEM((keys, size), BF16),
            pltpu.VMEM((keys, size), BF16),
            pltpu.VMEM((keys, size), WIDE),
            pltpu.VMEM((keys, size), WIDE),
            pltpu.VMEM((count, lanes_all), BF16),
        ],
    )(
        *parts,
        kept["hidden"],
        kept["projected"],
        cotangent,
        out_weight,
        gain_out,
        gain_feed,
        queries,
        kept["start"],
        place,
        key_place,
        kept["log"],
        raw,
        cosine,
        sine,
        gain,
        *kv_blocks,
    )
    names = ("d_hidden", "d_projected", "grad_out_gain", "grad_feed_gain", "d_query_raw", "d_gain")
    kept.update(zip(names, outs[:6]))
    kept["d_kv"] = outs[6:]


def project_kv(order, normed, blocks, cosine, sine, gain, rows):
    tokens, width = normed.shape
    per_block, part, both = blocks[0].shape
    n = per_block * len(blocks)
    size = both // 2
    half = size // 2

    def kernel(order_ref, x_ref, cos_ref, sin_ref, gain_ref, *refs):
        block_refs = refs[: len(blocks)]
        kv_ref, raw_ref, held = refs[len(blocks) :]
        for d in range(n):
            slot = order_ref[d]
            for k, block in enumerate(block_refs):

                @pl.when((slot >= k * per_block) & (slot < (k + 1) * per_block))
                def _(d=d, k=k, block=block, slot=slot):
                    held[d * part : (d + 1) * part] = block[slot - k * per_block]

        both_raw = jnp.dot(x_ref[...], held[...], preferred_element_type=WIDE)
        u = both_raw[:, :size]
        raw_ref[...] = u
        k = unit(u, gain_ref[...].astype(WIDE))[0]
        cos, sin = cos_ref[...], sin_ref[...]
        a, b = k[:, :half], k[:, half:]
        kv = jnp.concatenate([a * cos - b * sin, b * cos + a * sin, both_raw[:, size:]], axis=-1)
        kv_ref[...] = kv.astype(BF16).reshape(rows, tokens // rows, both)

    return vmem_call(
        kernel,
        (
            jax.ShapeDtypeStruct((rows, tokens // rows, both), BF16),
            jax.ShapeDtypeStruct((tokens, size), WIDE),
            jax.ShapeDtypeStruct((width, both), BF16),
        ),
        in_specs=[smem_spec()] + [whole_spec()] * (4 + len(blocks)),
        out_specs=(whole_spec(), whole_spec(), whole_spec()),
    )(order, normed, cosine, sine, gain, *blocks)


def project_q(normed, weight, cosine, sine, gain, heads):
    tokens, width = normed.shape
    size = weight.shape[1] // heads
    half = size // 2

    def kernel(x_ref, w_ref, cos_ref, sin_ref, gain_ref, q_ref, raw_ref):
        cos, sin = cos_ref[...], sin_ref[...]
        raw_ref[...] = jnp.dot(x_ref[...], w_ref[...], preferred_element_type=WIDE)
        for h in range(heads):
            lanes = slice(h * size, (h + 1) * size)
            q = unit(raw_ref[:, lanes], gain_ref[...].astype(WIDE))[0]
            a, b = q[:, :half], q[:, half:]
            turned = jnp.concatenate([a * cos - b * sin, b * cos + a * sin], axis=-1)
            q_ref[:, lanes] = turned.astype(BF16)

    return vmem_call(
        kernel,
        (
            jax.ShapeDtypeStruct((tokens, heads * size), BF16),
            jax.ShapeDtypeStruct((tokens, heads * size), WIDE),
        ),
        in_specs=[whole_spec()] * 5,
        out_specs=(whole_spec(), whole_spec()),
    )(normed, weight, cosine, sine, gain)


def feed_step(tokens):
    return 256 if tokens % 256 == 0 else tokens


def feed_forward(inner, gate_w, up_w, down_w):
    tokens, width = inner.shape
    share = gate_w.shape[1]
    step = feed_step(tokens)

    def kernel(x_ref, gate_ref, up_ref, down_ref, slope_ref, value_ref, a_ref, low_ref):
        x = x_ref[...]
        g = jnp.dot(x, gate_ref[...], preferred_element_type=WIDE)
        u = jnp.dot(x, up_ref[...], preferred_element_type=WIDE)
        value, slope = gelu_parts(g)
        active = (value * u).astype(BF16)
        slope_ref[...] = (slope * u).astype(BF16)
        value_ref[...] = value.astype(BF16)
        a_ref[...] = active
        low_ref[...] = jnp.dot(active, down_ref[...], preferred_element_type=WIDE).astype(BF16)

    each = lambda columns: pl.BlockSpec((step, columns), lambda i: (i, 0))
    hidden = jax.ShapeDtypeStruct((tokens, share), BF16)
    return vmem_call(
        kernel,
        (hidden, hidden, hidden, jax.ShapeDtypeStruct((tokens, width), BF16)),
        limit=24,
        grid=(tokens // step,),
        in_specs=[each(width), whole_spec(), whole_spec(), whole_spec()],
        out_specs=(each(share), each(share), each(share), each(width)),
    )(inner, gate_w, up_w, down_w)


def feed_backward(d_lowered, slope, value, gate_w, up_w, down_w):
    tokens, width = d_lowered.shape
    share = gate_w.shape[1]
    step = feed_step(tokens)

    def kernel(d_ref, slope_ref, value_ref, gate_ref, up_ref, down_ref, dg_ref, du_ref, dx_ref):
        d_active = lax.dot_general(d_ref[...], down_ref[...], NT, preferred_element_type=WIDE)
        d_gate = (d_active * slope_ref[...].astype(WIDE)).astype(BF16)
        d_up = (d_active * value_ref[...].astype(WIDE)).astype(BF16)
        dg_ref[...] = d_gate
        du_ref[...] = d_up
        d_x = lax.dot_general(d_gate, gate_ref[...], NT, preferred_element_type=WIDE)
        d_x += lax.dot_general(d_up, up_ref[...], NT, preferred_element_type=WIDE)
        dx_ref[...] = d_x.astype(BF16)

    each = lambda columns: pl.BlockSpec((step, columns), lambda i: (i, 0))
    hidden = jax.ShapeDtypeStruct((tokens, share), BF16)
    return vmem_call(
        kernel,
        (hidden, hidden, jax.ShapeDtypeStruct((tokens, width), BF16)),
        limit=24,
        grid=(tokens // step,),
        in_specs=[each(width), each(share), each(share), whole_spec(), whole_spec(), whole_spec()],
        out_specs=(each(share), each(share), each(width)),
    )(d_lowered, slope, value, gate_w, up_w, down_w)


def weight_grad(lefts, rights):
    rows = lefts[0].shape[1]
    columns = rights[0].shape[1]
    count = len(lefts)
    size = 384

    def kernel(*refs):
        out_ref = refs[2 * count]
        for at in range(0, rows, size):
            lanes = slice(at, min(at + size, rows))
            term = None
            for k in range(count):
                part = lax.dot_general(
                    refs[k][:, lanes], refs[count + k][...], TN, preferred_element_type=WIDE
                )
                term = part if term is None else term + part
            out_ref[lanes, :] = term.astype(BF16)

    return vmem_call(
        kernel,
        jax.ShapeDtypeStruct((rows, columns), BF16),
        limit=24,
        in_specs=[whole_spec()] * (2 * count),
        out_specs=whole_spec(),
    )(*lefts, *rights)


def blocks_grad(order, left_sets, right_sets, n):
    rows = left_sets[0].shape[1]
    part = rows // n
    widths = [r.shape[1] for r in right_sets[0]]
    per_row = len(widths)
    count = len(left_sets)
    blocks = n // 4

    def kernel(order_ref, *refs):
        lefts = refs[:count]
        rights = refs[count : count + count * per_row]
        outs = refs[count + count * per_row : -1]
        held = refs[-1]
        for d in range(n):
            lanes = slice(d * part, (d + 1) * part)
            at = 0
            for j, size in enumerate(widths):
                term = None
                for k in range(count):
                    product = lax.dot_general(
                        lefts[k][:, lanes],
                        rights[k * per_row + j][...],
                        TN,
                        preferred_element_type=WIDE,
                    )
                    term = product if term is None else term + product
                held[order_ref[d], :, at : at + size] = term.astype(BF16)
                at += size
        for b, out in enumerate(outs):
            out[...] = held[4 * b : 4 * b + 4]

    flat = [r for rights in right_sets for r in rights]
    shape = jax.ShapeDtypeStruct((4, part, sum(widths)), BF16)
    return vmem_call(
        kernel,
        (shape,) * blocks,
        limit=24,
        in_specs=[smem_spec()] + [whole_spec()] * (count + len(flat)),
        out_specs=(whole_spec(),) * blocks,
        scratch_shapes=[pltpu.VMEM((n, part, sum(widths)), BF16)],
    )(order, *left_sets, *flat)


def close_keys(parts, raw, cosine, sine, gain):
    slots, rows, count, both = parts[0].shape
    size = both // 2
    half = size // 2

    def kernel(a_ref, b_ref, c_ref, raw_ref, cos_ref, sin_ref, gain_ref, *outs):
        gain_values = gain_ref[...].astype(WIDE)
        d_gain = jnp.zeros((1, size), WIDE)
        for row in range(rows):
            span = slice(row * count, (row + 1) * count)
            e = (
                a_ref[0, row].astype(WIDE) + b_ref[row].astype(WIDE) + c_ref[row].astype(WIDE)
            )
            cos, sin = cos_ref[span], sin_ref[span]
            d_a, d_b = e[:, :half], e[:, half:size]
            turned = jnp.concatenate([d_a * cos + d_b * sin, d_b * cos - d_a * sin], axis=-1)
            u = raw_ref[span]
            d_u, d_part = unit_back(u, unit(u, gain_values)[1], gain_values, turned)
            d_gain += d_part
            outs[row][:, :size] = d_u.astype(BF16)
            outs[row][:, size:] = e[:, size:].astype(BF16)
        outs[rows][...] = d_gain

    return vmem_call(
        kernel,
        (jax.ShapeDtypeStruct((count, both), BF16),) * rows
        + (jax.ShapeDtypeStruct((1, size), WIDE),),
        grid=(1,),
        in_specs=[
            pl.BlockSpec((1, rows, count, both), lambda i: (0, 0, 0, 0)),
            full_spec((rows, count, both)),
            full_spec((rows, count, both)),
            full_spec(raw.shape),
            full_spec(cosine.shape),
            full_spec(sine.shape),
            full_spec((1, size)),
        ],
        out_specs=(full_spec((count, both)),) * rows + (full_spec((1, size)),),
    )(*parts, raw, cosine, sine, gain)


def close_tokens(tokens, d_queries, d_kvs, query_w, kv_w, d_hiddens, gain):
    rows, count, width = tokens.shape

    def kernel(x_ref, q_ref, kv_ref, gain_ref, *refs):
        out_ref, dg_ref = refs[3 * rows :]
        g = gain_ref[...].astype(WIDE)
        d_gain = jnp.zeros((1, width), WIDE)
        for row in range(rows):
            d_q, d_kv, d_hidden = refs[row], refs[rows + row], refs[2 * rows + row]
            e = lax.dot_general(d_q[...], q_ref[...], NT, preferred_element_type=WIDE)
            e += lax.dot_general(d_kv[...], kv_ref[...], NT, preferred_element_type=WIDE)
            x = x_ref[row].astype(WIDE)
            d_x, d_part = unit_back(x, unit(x, g)[1], g, e)
            d_gain += d_part
            out_ref[row] = (d_hidden[...] + d_x).astype(BF16)
        dg_ref[...] = d_gain

    return vmem_call(
        kernel,
        (jax.ShapeDtypeStruct(tokens.shape, BF16), jax.ShapeDtypeStruct((1, width), WIDE)),
        in_specs=[whole_spec()] * (4 + 3 * rows),
        out_specs=(whole_spec(), whole_spec()),
    )(tokens, query_w, kv_w, gain, *d_queries, *d_kvs, *d_hiddens)


def per_device(
    tokens,
    cotangent,
    segment_ids,
    query_weight,
    key_weight,
    value_weight,
    out_weight,
    gate_weight,
    up_weight,
    down_weight,
    gain_input,
    gain_query,
    gain_key,
    gain_attended,
    gain_feed,
    gain_result,
):
    n = lax.axis_size("ctx")
    n_dp = lax.axis_size("dp")
    me = lax.axis_index("ctx")
    my_dp = lax.axis_index("dp")
    row_count, count_local, width = tokens.shape
    total = row_count * count_local
    head_width = gain_query.shape[0]
    head_count = query_weight.shape[1] // head_width
    qw = head_count * head_width
    share = gate_weight.shape[1] // n
    span = count_local // 2
    codes = xor_layout(n)[3]
    kv_weights = Gather(jnp.concatenate([key_weight, value_weight], axis=1), n)
    query_full = lax.all_gather(query_weight, "ctx", axis=0, tiled=True)
    even_flag = ((my_dp % 2) == 0).astype(jnp.int32).reshape(1)
    below = jnp.stack(
        [jnp.sum((segment_ids < s).astype(jnp.int32), axis=1) for s in range(5)], axis=1
    )
    code = 1
    while code < n:
        below = below + xor_permute(below, n, code)
        code *= 2
    starts = sum(jnp.where(segment_ids == s, below[:, s : s + 1], 0) for s in range(5))
    start_columns = [starts[row].reshape(-1, 1) for row in range(row_count)]
    kv_weights.mid()
    pieces = spread_pieces(
        even_flag, after(gate_weight, kv_weights.a, kv_weights.b, starts), up_weight, n
    )
    spread = lax.all_to_all(pieces, "ctx", 0, 0)
    kv_weights.near(pieces)
    gain_row = {
        "input": after(gain_input, pieces).reshape(1, -1),
        "query": after(gain_query, pieces).reshape(1, -1),
        "key": after(gain_key, pieces).reshape(1, -1),
        "out": after(gain_attended, pieces).reshape(1, -1),
        "feed": after(gain_feed, pieces).reshape(1, -1),
        "result": after(gain_result, pieces).reshape(1, -1),
    }

    offsets = jnp.arange(span, dtype=jnp.int32)

    def places_of(device):
        return jnp.concatenate([device * span + offsets, (2 * n - 1 - device) * span + offsets])

    local_places = places_of(me)
    key_places = jnp.concatenate([places_of(me ^ code) for code in codes]).reshape(1, -1)
    place_column = local_places.reshape(-1, 1)
    angles = angles_for(local_places.astype(WIDE), head_width)
    cosine = jnp.concatenate([jnp.cos(angles)] * row_count, axis=0)
    sine = jnp.concatenate([jnp.sin(angles)] * row_count, axis=0)

    normed_rows = rms_norm(tokens.astype(WIDE), gain_input.astype(WIDE)).astype(BF16)
    normed = normed_rows.reshape(total, width)
    order_codes = me ^ jnp.arange(n, dtype=jnp.int32)
    order = sum(jnp.where(order_codes == c, k, 0) for k, c in enumerate(codes)).astype(jnp.int32)
    kv_local, key_raw, kv_full = project_kv(
        order, normed, kv_weights.blocks, cosine, sine, gain_row["key"], row_count
    )
    kv_gather = Gather(kv_local, n)
    out_full = lax.all_gather(after(out_weight, kv_local), "ctx", axis=0, tiled=True)
    queries, query_raw = project_q(
        after(normed, kv_local), query_full, cosine, sine, gain_row["query"], head_count
    )
    kv_gather.mid(spread, *start_columns, *gain_row.values(), key_places, place_column)
    swapped = lax.ppermute(
        after(spread, kv_gather.a, kv_gather.b), "dp", [(i, i ^ 1) for i in range(n_dp)]
    )
    kv_gather.near(queries)
    kv_blocks = kv_gather.blocks

    def before_feed(row, *earlier):
        r = {"start": start_columns[row]}
        names = ("attended", "log", "projected", "hidden", "inner_local")
        outs = attend_forward(
            row,
            after(queries, *earlier),
            kv_blocks,
            r["start"],
            place_column,
            key_places,
            out_full,
            tokens,
            gain_row["out"],
            gain_row["feed"],
            head_count,
        )
        r.update(zip(names, outs))
        return r

    def feed_piece(r, block, *earlier):
        outs = feed_forward(after(block, *earlier), gate_mine, up_mine, down_weight)
        for name, out in zip(("inner", "slope", "value", "active"), (block,) + tuple(outs[:3])):
            r.setdefault(name, []).append(out)
        return outs[3].reshape(4, count_local, width)

    def back_piece(r, block, *earlier):
        k = len(r.setdefault("d_lowered", []))
        outs = feed_backward(
            after(block, *earlier), r["slope"][k], r["value"][k], gate_mine, up_mine, down_weight
        )
        for name, out in zip(("d_lowered", "d_gate", "d_up"), (block,) + tuple(outs[:2])):
            r.setdefault(name, []).append(out)
        return outs[2].reshape(4, count_local, width)

    def pieces_of(piece, r, blocks, *earlier):
        outs = []
        for block in blocks:
            outs.append(piece(r, block, *earlier, *outs[-1:]))
        return outs

    def result_piece(row, r, parts):
        r["result"], d_lowered, r["grad_result_gain"] = close_row(
            row, parts, r["hidden"], cotangent, gain_row["result"]
        )
        return d_lowered

    def attend_back(row, r, parts):
        attend_backward(
            row,
            parts,
            r,
            cotangent,
            out_full,
            gain_row["out"],
            gain_row["feed"],
            queries,
            kv_blocks,
            place_column,
            key_places,
            query_raw,
            cosine,
            sine,
            gain_row["query"],
            head_count,
        )

    r0 = before_feed(0)
    g0 = Gather(r0["inner_local"], n)
    r1 = before_feed(1, r0["inner_local"])
    g0.mid(r1["inner_local"])
    g1 = Gather(after(r1["inner_local"], g0.a, g0.b), n)
    gate_mine, up_mine = in_order(even_flag, spread, swapped)
    gate_mine = gate_mine.reshape(width, share)
    up_mine = up_mine.reshape(width, share)
    g0.near(gate_mine, g1.a, g1.b)
    g1.mid(g0.blocks[0])
    blocks_0 = g0.flat()
    low_0 = [feed_piece(r0, blocks_0[0])]
    low_0 += pieces_of(feed_piece, r0, blocks_0[1:], low_0[0])
    s0 = Scatter(low_0, n)
    g1.near(low_0[-1])
    blocks_1 = g1.flat()
    low_1 = [feed_piece(r1, blocks_1[0])]
    s0.mid(low_1[0])
    low_1 += pieces_of(feed_piece, r1, blocks_1[1:], low_1[0], s0.sums)
    s1 = Scatter(low_1, n)
    s0.far(low_1[-1])
    s1.mid(*s0.sent)
    d_low_0 = result_piece(0, r0, s0.finish(s1.sums))
    h0 = Gather(d_low_0, n)
    s1.far(d_low_0)
    h0.mid(*s1.sent)
    d_low_1 = result_piece(1, r1, s1.finish(h0.a))
    h1 = Gather(d_low_1, n)
    h0.near(d_low_1)
    blocks_0 = h0.flat()
    d_in_0 = [back_piece(r0, blocks_0[0])]
    h1.mid(d_in_0[0])
    d_in_0 += pieces_of(back_piece, r0, blocks_0[1:], d_in_0[0], h1.a, h1.b)
    s0 = Scatter(d_in_0, n)
    h1.near(d_in_0[-1])
    blocks_1 = h1.flat()
    d_in_1 = [back_piece(r1, blocks_1[0])]
    s0.mid(d_in_1[0])
    rows = (r0, r1)

    def over_rows(left, right, *earlier):
        lefts, rights = r0[left] + r1[left], r0[right] + r1[right]
        return weight_grad([after(lefts[0], *earlier)] + lefts[1:], rights)

    def begin(part, *earlier):
        line = Line(after(part, *earlier), n_dp)
        clock[:] = [line.total]
        return line

    def land(line):
        line.moved = after(line.moved, *clock)
        clock[:] = [line.moved]

    def step(line, *earlier):
        if line.at < len(line.steps) - 1:
            line.step(*clock, *earlier)
            clock[:] = [line.total]

    def halves(x):
        half = x.shape[0] // 2
        return [x[:half], x[half:]]

    def exchange(grad):
        return lax.all_to_all(grad.reshape(n, width // n, share), "ctx", 0, 0)

    clock = []
    grad_down = weight_grad(
        [after(r0["active"][0], s0.sums)] + r0["active"][1:] + r1["active"],
        r0["d_lowered"] + blocks_1,
    )
    down_line = begin(grad_down)
    d_in_1 += pieces_of(back_piece, r1, blocks_1[1:], d_in_1[0], grad_down)
    s1 = Scatter(d_in_1, n)
    s0.far(d_in_1[-1])
    grad_gate = over_rows("inner", "d_gate", *s0.sent)
    gate_pieces = exchange(grad_gate)
    s1.mid(grad_gate)
    attend_back(0, r0, s0.finish(s1.sums))
    clock[:] = [r0["d_kv"][0]]
    step(down_line)
    s1.far(*clock)
    grad_up = over_rows("inner", "d_up", *s1.sent)
    up_pieces = exchange(grad_up)
    gate_halves = halves(gate_pieces)
    gl0 = begin(gate_halves[0], grad_up)
    attend_back(1, r1, s1.finish(*clock))
    clock[:] = [r1["d_kv"][0]]
    step(down_line)
    gl1 = begin(gate_halves[1], *clock)
    step(gl0)
    kv_scatter = Scatter(
        [jnp.stack([a, b], axis=1) for a, b in zip(r0["d_kv"], r1["d_kv"])], n
    )
    clock[:] = [gl0.total, *kv_scatter.blocks[-1:]]
    grad_out = (
        t_dot(after(r0["attended"], *clock), r0["d_projected"])
        + t_dot(r1["attended"], r1["d_projected"])
    ).astype(BF16)
    part_out = lax.psum_scatter(grad_out, "ctx", scatter_dimension=0, tiled=True)
    def total_of(parts):
        return (
            parts[0][0].astype(WIDE) + parts[1].astype(WIDE) + parts[2].astype(WIDE)
        ).astype(BF16)

    def last(line):
        line.moved = after(line.moved, *clock)
        total = line.finish().astype(WIDE)
        clock[:] = [total]
        return total

    def side_by_side(lines):
        ends = lines[0].steps[-1][2]
        mine = (my_dp == ends[0]) | (my_dp == ends[1]) if ends else my_dp < 0
        total = assemble(
            mine.astype(jnp.int32).reshape(1),
            [line.total for line in lines],
            [after(line.moved, *clock) for line in lines],
            width // n,
            n * share,
        )
        clock[:] = [total]
        return total

    kv_scatter.mid(grad_out)
    up_halves = halves(up_pieces)
    u0 = begin(up_halves[0], kv_scatter.sums)
    kv_scatter.far(*clock)
    clock[:] = [*kv_scatter.sent]
    step(gl1)
    *d_kvs, grad_key_gain = close_keys(
        kv_scatter.finish(*clock), key_raw, cosine, sine, gain_row["key"]
    )
    clock[:] = [d_kvs[0]]
    step(gl0)
    land(down_line)
    step(u0)
    step(gl1)
    out_line = begin(part_out, *clock)
    u1 = begin(up_halves[1], *clock)
    grad_qkv = blocks_grad(
        order,
        [
            after(normed[row * count_local : (row + 1) * count_local], *clock)
            for row in range(row_count)
        ],
        [[r["d_query_raw"], d_kv] for r, d_kv in zip(rows, d_kvs)],
        n,
    )
    qkv_scatter = Scatter(grad_qkv, n)
    qkv_scatter.mid(grad_qkv[0])
    tokens_grad, grad_input_gain = close_tokens(
        tokens,
        [after(r["d_query_raw"], qkv_scatter.sums) for r in rows],
        d_kvs,
        query_full,
        kv_full,
        [r["d_hidden"] for r in rows],
        gain_row["input"],
    )
    qkv_scatter.far(tokens_grad)
    gains = jnp.concatenate(
        [
            grad_input_gain,
            sum(r["d_gain"] for r in rows),
            grad_key_gain,
            sum(r["grad_out_gain"] for r in rows),
            sum(r["grad_feed_gain"] for r in rows),
            sum(r["grad_result_gain"] for r in rows),
        ],
        axis=1,
    ).reshape(-1, 128)
    clock[:] = [*qkv_scatter.sent]
    gains = after(gains, *clock)
    land(gl0)
    step(u1)
    step(u0)
    summed_down = last(down_line)
    result = after(jnp.stack([r["result"] for r in rows]), *clock)
    clock[:] = [summed_down, result]
    part_qkv = total_of(qkv_scatter.finish(*clock))
    clock[:] = [part_qkv]
    qkv_line = begin(part_qkv, *clock)
    land(gl1)
    step(out_line)
    code = 1
    while code < n:
        gains = gains + xor_permute(gains, n, code)
        code *= 2
    step(qkv_line)
    step(u1)
    land(u0)
    step(out_line)
    gain_line = begin(gains, *clock)
    step(qkv_line)
    step(gain_line)
    step(out_line)
    for _ in range(n_dp):
        for line in (gl0, gl1, u0, u1, qkv_line, out_line, gain_line):
            step(line)
    summed_gate = side_by_side([gl0, gl1])
    summed_up = side_by_side([u0, u1])
    summed_out = last(out_line)
    summed_qkv = last(qkv_line)
    gains = last(gain_line).reshape(-1)
    sizes = [width, head_width, head_width, width, width, width]
    gain_grads = []
    start = 0
    for size in sizes:
        gain_grads.append(gains[start : start + size])
        start += size
    return (
        result,
        tokens_grad,
        summed_qkv[:, :qw],
        summed_qkv[:, qw : qw + head_width],
        summed_qkv[:, qw + head_width :],
        summed_out,
        summed_gate,
        summed_up,
        summed_down,
        *gain_grads,
    )


def solution(mesh):
    return jax.shard_map(
        per_device,
        mesh=mesh,
        in_specs=(
            P("dp", "ctx", None),
            P("dp", "ctx", None),
            P("dp", "ctx"),
            P("ctx", None),
            P("ctx", None),
            P("ctx", None),
            P("ctx", None),
            P("ctx", None),
            P("ctx", None),
            P("ctx", None),
            P(),
            P(),
            P(),
            P(),
            P(),
            P(),
        ),
        out_specs=(
            P("dp", "ctx", None),
            P("dp", "ctx", None),
            P("ctx", None),
            P("ctx", None),
            P("ctx", None),
            P("ctx", None),
            P("ctx", None),
            P("ctx", None),
            P("ctx", None),
            P(),
            P(),
            P(),
            P(),
            P(),
            P(),
        ),
        check_vma=False,
    )
```
